32 devices in a mesh: dp: 4 (over y, x), seq: 8 (over z, core).
Axes of the slice: x: 2, y: 2, z: 4, core: 2. Of those that a mesh axis runs over, the one named last changes fastest.
Arguments:
- target: bfloat16 [1024, 16, 1024], P('seq', 'dp'), may hold values from -6 to 6
- source: bfloat16 [1024, 16, 1024], P('seq', 'dp'), may hold values from -6 to 6
- target_len: int32 [16], P('dp'), may hold values from 256 to 1024, as said below
- source_len: int32 [16], P('dp'), may hold values from 256 to 1024, as said below
- self_query: bfloat16 [1024, 1024], P('dp'), may hold values from -0.1875 to 0.1875
- self_key: bfloat16 [1024, 1024], P('dp'), may hold values from -0.1875 to 0.1875
- self_value: bfloat16 [1024, 1024], P('dp'), may hold values from -0.1875 to 0.1875
- self_output: bfloat16 [1024, 1024], P('dp'), may hold values from -3 to 3
- cross_query: bfloat16 [1024, 1024], P('dp'), may hold values from -0.1875 to 0.1875
- cross_key: bfloat16 [1024, 1024], P('dp'), may hold values from -0.1875 to 0.1875
- cross_value: bfloat16 [1024, 1024], P('dp'), may hold values from -0.1875 to 0.1875
- cross_output: bfloat16 [1024, 1024], P('dp'), may hold values from -3 to 3
- feed_in: bfloat16 [1024, 4096], P('dp'), may hold values from -0.1875 to 0.1875
- feed_out: bfloat16 [4096, 1024], P('dp'), may hold values from -0.09375 to 0.09375
- adapter_down: bfloat16 [1024, 512], P('dp'), may hold values from -0.1875 to 0.1875
- adapter_up: bfloat16 [512, 1024], P('dp'), may hold values from -0.0625 to 0.0625
- self_gain: bfloat16 [1024], P('dp'), may hold values from 0.5 to 1.5
- self_shift: bfloat16 [1024], P('dp'), may hold values from -1 to 1
- cross_gain: bfloat16 [1024], P('dp'), may hold values from 0.5 to 1.5
- cross_shift: bfloat16 [1024], P('dp'), may hold values from -1 to 1
- final_gain: bfloat16 [1024], P('dp'), may hold values from 0.5 to 1.5
- final_shift: bfloat16 [1024], P('dp'), may hold values from -1 to 1
- cotangent: bfloat16 [1024, 16, 1024], P('seq', 'dp'), may hold values from -6 to 6
Outputs:
- output: bfloat16 [1024, 16, 1024], P('seq', 'dp')
- grad_target: bfloat16 [1024, 16, 1024], P('seq', 'dp')
- grad_source: bfloat16 [1024, 16, 1024], P('seq', 'dp')
- self_query_grad: float32 [1024, 1024], P(('dp', 'seq'))
- self_key_grad: float32 [1024, 1024], P(('dp', 'seq'))
- self_value_grad: float32 [1024, 1024], P(('dp', 'seq'))
- self_output_grad: float32 [1024, 1024], P(('dp', 'seq'))
- cross_query_grad: float32 [1024, 1024], P(('dp', 'seq'))
- cross_key_grad: float32 [1024, 1024], P(('dp', 'seq'))
- cross_value_grad: float32 [1024, 1024], P(('dp', 'seq'))
- cross_output_grad: float32 [1024, 1024], P(('dp', 'seq'))
- adapter_down_grad: float32 [1024, 512], P(('dp', 'seq'))
- adapter_up_grad: float32 [512, 1024], P(('dp', 'seq'))
- self_gain_grad: float32 [1024], P(('dp', 'seq'))
- self_shift_grad: float32 [1024], P(('dp', 'seq'))
- cross_gain_grad: float32 [1024], P(('dp', 'seq'))
- cross_shift_grad: float32 [1024], P(('dp', 'seq'))
- final_gain_grad: float32 [1024], P(('dp', 'seq'))
- final_shift_grad: float32 [1024], P(('dp', 'seq'))
The draws below stay inside these ranges and needn't reach their ends.
Inputs may be any that keep to these rules, and one draw needn't show every extreme that they name: `target_len`: of the 4 sequences on each index of dp, one has all 1024 positions. `source_len`: of the 4 sequences on each index of dp, one has all 1024 positions.
All inputs are finite; a program needn't handle non-finite values.
Results may differ from the reference program's by a relative error of at most 0.028.
Values may be sent and summed in bfloat16 or wider, within the bound.
No kernel may reach another device: no remote copies, remote signals or barrier semaphores. Data moves between devices by JAX's collectives and lax.ppermute only.
A program may use at most 576 MiB of HBM per device.

```python
import jax
import jax.numpy as jnp
from jax import lax

D = 1024
H = 16
HEAD = 64
FF = 4096
AD = 512
LENGTH = 1024
SEQ_DEV = 4
NSEQ = 16


def group_lengths(key):
    drawn_key, chosen_key = jax.random.split(key)
    groups = NSEQ // SEQ_DEV
    drawn = jax.random.randint(drawn_key, (groups, SEQ_DEV), LENGTH // 4, LENGTH + 1)
    chosen = jax.random.randint(chosen_key, (groups, 1), 0, SEQ_DEV)
    columns = jnp.arange(SEQ_DEV, dtype=jnp.int32)[None, :]
    return jnp.where(columns == chosen, LENGTH, drawn).reshape(NSEQ).astype(jnp.int32)


def draw_target_len(key, part):
    key = jax.random.fold_in(key, 11)
    return group_lengths(key)


def draw_source_len(key, part):
    key = jax.random.fold_in(key, 23)
    return group_lengths(key)


def block_scale(key, dims, pieces, least, high):
    def one(axis_at, shards_of):
        steps = jax.random.uniform(jax.random.fold_in(jax.random.fold_in(key, 6), axis_at), (shards_of,), jnp.float32, least / len(pieces), high / len(pieces))
        return jnp.repeat(jnp.exp(steps), dims[axis_at] // shards_of).reshape((-1,) + (1,) * (len(dims) - axis_at - 1))

    loudness = one(*pieces[0])
    for cut in pieces[1:]:
        loudness = loudness * one(*cut)
    return loudness


def scatter_about(stream_key, extent, width, limit, cuts=(), held_as=jnp.bfloat16):
    values = width * jax.random.normal(stream_key, extent, jnp.float32)
    if cuts:
        values = values * block_scale(stream_key, extent, cuts, -0.22, 0.18)
    return jnp.clip(values, -limit, limit).astype(held_as)


def setup_inputs(seed: int = 0) -> dict:
    seeds = jax.random.split(jax.random.key(seed), 24)
    target = scatter_about(seeds[0], (LENGTH, NSEQ, D), 1.0, 6.0, ((0, 8), (1, 4)))
    source = scatter_about(seeds[1], (LENGTH, NSEQ, D), 1.0, 6.0, ((0, 8), (1, 4)))
    target_len = draw_target_len(jax.random.fold_in(seeds[23], 71), 0)
    source_len = draw_source_len(jax.random.fold_in(seeds[23], 71), 0)
    self_query = scatter_about(seeds[4], (D, D), D ** -0.5, 0.1875, ((0, 4),))
    self_key = scatter_about(seeds[5], (D, D), D ** -0.5, 0.1875, ((0, 4),))
    self_value = scatter_about(seeds[6], (D, D), D ** -0.5, 0.1875, ((0, 4),))
    self_output = scatter_about(seeds[7], (D, D), (max(D // 256, 1)) ** -0.5, 3.0, ((0, 4),))
    cross_query = scatter_about(seeds[8], (D, D), D ** -0.5, 0.1875, ((0, 4),))
    cross_key = scatter_about(seeds[9], (D, D), D ** -0.5, 0.1875, ((0, 4),))
    cross_value = scatter_about(seeds[10], (D, D), D ** -0.5, 0.1875, ((0, 4),))
    cross_output = scatter_about(seeds[11], (D, D), (max(D // 256, 1)) ** -0.5, 3.0, ((0, 4),))
    feed_in = scatter_about(seeds[12], (D, FF), D ** -0.5, 0.1875, ((0, 4),))
    feed_out = scatter_about(seeds[13], (FF, D), FF ** -0.5, 0.09375, ((0, 4),))
    adapter_down = scatter_about(seeds[14], (D, AD), D ** -0.5, 0.1875, ((0, 4),))
    adapter_up = scatter_about(seeds[15], (AD, D), (16 * AD) ** -0.5, 0.0625, ((0, 4),))
    self_gain = jnp.clip(1.0 + 0.1 * jax.random.normal(seeds[16], (D,), jnp.float32), 0.5, 1.5).astype(jnp.bfloat16)
    self_shift = scatter_about(seeds[17], (D,), 0.2, 1.0, ((0, 4),))
    cross_gain = jnp.clip(1.0 + 0.1 * jax.random.normal(seeds[18], (D,), jnp.float32), 0.5, 1.5).astype(jnp.bfloat16)
    cross_shift = scatter_about(seeds[19], (D,), 0.2, 1.0, ((0, 4),))
    final_gain = jnp.clip(1.0 + 0.1 * jax.random.normal(seeds[20], (D,), jnp.float32), 0.5, 1.5).astype(jnp.bfloat16)
    final_shift = scatter_about(seeds[21], (D,), 0.2, 1.0, ((0, 4),))
    cotangent = scatter_about(seeds[22], (LENGTH, NSEQ, D), 1.0, 6.0, ((0, 8), (1, 4)))
    return {"target": target, "source": source, "target_len": target_len, "source_len": source_len, "self_query": self_query, "self_key": self_key, "self_value": self_value, "self_output": self_output, "cross_query": cross_query, "cross_key": cross_key, "cross_value": cross_value, "cross_output": cross_output, "feed_in": feed_in, "feed_out": feed_out, "adapter_down": adapter_down, "adapter_up": adapter_up, "self_gain": self_gain, "self_shift": self_shift, "cross_gain": cross_gain, "cross_shift": cross_shift, "final_gain": final_gain, "final_shift": final_shift, "cotangent": cotangent}


@jax.custom_vjp
def low(v):
    return lax.optimization_barrier(v.astype(jnp.bfloat16)).astype(jnp.float32)

@jax.custom_vjp
def low_back(v):
    return v

def low_keep(v):
    return (low(v), None)

def low_pass(kept, grad):
    return (grad,)

def back_keep(v):
    return (v, None)

def back_low(kept, grad):
    return (low(grad),)
low.defvjp(low_keep, low_pass)
low_back.defvjp(back_keep, back_low)
MASKED_SCORE = -1e+30

def rounded(inputs):
    return low_back(low(inputs))

def matmul(left, right):
    return jnp.dot(left, right, precision=lax.Precision.HIGHEST)

def layer_norm(inputs, gain, shift):
    centre = lax.optimization_barrier(jnp.mean(inputs, axis=-1, keepdims=True))
    centred = inputs - centre
    spread = lax.optimization_barrier(jnp.mean(centred * centred, axis=-1, keepdims=True))
    return centred * lax.rsqrt(spread + 1e-05) * gain + shift

def gelu_exact(inputs):
    return jax.nn.gelu(inputs, approximate=False)

def attend(queries, keys_all, values_all, key_limit, causal):
    length = queries.shape[0]
    block = min(512, length)
    key_count = keys_all.shape[0]
    key_pos = jnp.arange(key_count, dtype=jnp.int32)
    key_heads = keys_all.reshape(key_count, H, HEAD)
    value_heads = values_all.reshape(key_count, H, HEAD)

    def one_block(item):
        query_rows, first_row = item
        query_heads = query_rows.reshape(block, H, HEAD)
        scores = jnp.einsum('qhe,khe->hqk', query_heads, key_heads, precision=lax.Precision.HIGHEST)
        scores = low_back(scores * HEAD ** (-0.5))
        allowed = (key_pos < key_limit)[None, :]
        if causal:
            query_pos = first_row + jnp.arange(block, dtype=jnp.int32)
            allowed = allowed & (key_pos[None, :] <= query_pos[:, None])
        scores = jnp.where(allowed[None], scores, MASKED_SCORE)
        highest = lax.optimization_barrier(jnp.max(scores, axis=-1, keepdims=True))
        raised = jnp.exp(scores - highest)
        weights_soft = low(raised / lax.optimization_barrier(jnp.sum(raised, axis=-1, keepdims=True)))
        mixed_rows = jnp.einsum('hqk,khe->qhe', weights_soft, value_heads, precision=lax.Precision.HIGHEST)
        return mixed_rows.reshape(block, H * HEAD)
    starts = jnp.arange(length // block, dtype=jnp.int32) * block
    blocks_in = queries.reshape(length // block, block, queries.shape[1])
    mixed_all = lax.map(jax.checkpoint(one_block), (blocks_in, starts))
    return mixed_all.reshape(length, H * HEAD)

def decode_layer(trainable, frozen, target_seq, source_seq, target_limit, source_limit):
    self_query, self_key, self_value, self_output, cross_query, cross_key, cross_value, cross_output, adapter_down, adapter_up, self_gain, self_shift, cross_gain, cross_shift, final_gain, final_shift = trainable
    feed_in, feed_out = frozen
    queries = rounded(matmul(target_seq, self_query))
    keys_now = rounded(matmul(target_seq, self_key))
    values_now = rounded(matmul(target_seq, self_value))
    self_mixed = rounded(attend(queries, keys_now, values_now, target_limit, True))
    first_norm = layer_norm(target_seq + low_back(matmul(self_mixed, self_output)), self_gain, self_shift)
    first_low = low(first_norm)
    cross_queries = rounded(matmul(first_low, cross_query))
    cross_keys = rounded(matmul(source_seq, cross_key))
    cross_values = rounded(matmul(source_seq, cross_value))
    cross_mixed = rounded(attend(cross_queries, cross_keys, cross_values, source_limit, False))
    second_norm = layer_norm(first_norm + low_back(matmul(cross_mixed, cross_output)), cross_gain, cross_shift)
    second_low = low(second_norm)
    hidden_ffn = low(gelu_exact(low_back(matmul(second_low, feed_in))))
    hidden_adapter = low(gelu_exact(low_back(matmul(second_low, adapter_down))))
    branch = low_back(matmul(hidden_ffn, feed_out) + 4.0 * matmul(hidden_adapter, adapter_up))
    return layer_norm(second_norm + branch, final_gain, final_shift)

def reference(target, source, target_len, source_len, self_query, self_key, self_value, self_output, cross_query, cross_key, cross_value, cross_output, feed_in, feed_out, adapter_down, adapter_up, self_gain, self_shift, cross_gain, cross_shift, final_gain, final_shift, cotangent):
    trainable = tuple((weight_arg.astype(jnp.float32) for weight_arg in (self_query, self_key, self_value, self_output, cross_query, cross_key, cross_value, cross_output, adapter_down, adapter_up, self_gain, self_shift, cross_gain, cross_shift, final_gain, final_shift)))
    frozen = (feed_in.astype(jnp.float32), feed_out.astype(jnp.float32))

    def one_sequence(totals, item):
        target_seq, source_seq, target_limit, source_limit, cot_seq = item

        def layer_of(params, target_in, source_in):
            return decode_layer(params, frozen, target_in, source_in, target_limit, source_limit)
        result, backward = jax.vjp(layer_of, trainable, target_seq, source_seq)
        param_grads, target_grad, source_grad = backward(cot_seq)
        totals = jax.tree.map(jnp.add, totals, param_grads)
        return (totals, (result.astype(jnp.bfloat16), target_grad.astype(jnp.bfloat16), source_grad.astype(jnp.bfloat16)))
    zeros_init = tuple((jnp.zeros(weight_arg.shape, jnp.float32) for weight_arg in trainable))
    items = (jnp.swapaxes(target, 0, 1).astype(jnp.float32), jnp.swapaxes(source, 0, 1).astype(jnp.float32), target_len, source_len, jnp.swapaxes(cotangent, 0, 1).astype(jnp.float32))
    totals, (results, target_grads, source_grads) = lax.scan(one_sequence, zeros_init, items)
    return (jnp.swapaxes(results, 0, 1), jnp.swapaxes(target_grads, 0, 1), jnp.swapaxes(source_grads, 0, 1), totals[0], totals[1], totals[2], totals[3], totals[4], totals[5], totals[6], totals[7], totals[8], totals[9], totals[10], totals[11], totals[12], totals[13], totals[14], totals[15])
```

```python
import functools

import jax
import jax.numpy as jnp
from jax import lax
from jax.experimental import pallas as pl
from jax.experimental.pallas import tpu as pltpu
from jax.sharding import PartitionSpec as P

HEAD = 64
PAIR = 2 * HEAD
SCALE = HEAD ** (-0.5)
MASKED_SCORE = -1e30
NEVER = 2**30
ALWAYS = 2**29
F32 = jnp.float32
BF16 = jnp.bfloat16
VMEM_LIMIT = 56 * 1024 * 1024


def dot(left, right):
    return jnp.dot(left, right, preferred_element_type=F32)


def dot_tn(left, right):
    return lax.dot_general(left, right, (((0,), (0,)), ((), ())), preferred_element_type=F32)


def dot_nt(left, right):
    return lax.dot_general(left, right, (((1,), (1,)), ((), ())), preferred_element_type=F32)


def gelu_exact(inputs):
    return jax.nn.gelu(inputs, approximate=False)


def norm_forward(inputs, gain, shift):
    centre = jnp.mean(inputs, axis=-1, keepdims=True)
    centred = inputs - centre
    spread = jnp.mean(centred * centred, axis=-1, keepdims=True)
    rstd = lax.rsqrt(spread + 1e-05)
    return centred * rstd * gain + shift, centre, rstd


def norm_backward(inputs, centre, rstd, gain, grad):
    normed = (inputs - centre) * rstd
    grad_gain = jnp.sum(grad * normed, axis=0)
    grad_shift = jnp.sum(grad, axis=0)
    inner = grad * gain
    mean_one = jnp.mean(inner, axis=-1, keepdims=True)
    mean_two = jnp.mean(inner * normed, axis=-1, keepdims=True)
    return rstd * (inner - mean_one - normed * mean_two), grad_gain, grad_shift


def tile_of(rows):
    return 128 if rows % 128 == 0 else rows


def key_rows(tile_end, rows, block, causal):
    if not causal:
        return rows
    return min(rows, ((tile_end - 1) // block + 1) * block)


def beside(top):
    row = lax.broadcasted_iota(jnp.int32, top.shape, 0)
    zero = jnp.zeros_like(top)
    return jnp.concatenate(
        [jnp.where(row < HEAD, top, zero), jnp.where(row < HEAD, zero, top)], axis=1
    )


def below(side):
    lane = lax.broadcasted_iota(jnp.int32, side.shape, 1)
    zero = jnp.zeros_like(side)
    return jnp.concatenate(
        [jnp.where(lane < HEAD, side, zero), jnp.where(lane < HEAD, zero, side)], axis=0
    )


def heads_back(wide, tile):
    return jnp.concatenate([wide[:HEAD, :tile], wide[HEAD:, tile:]], axis=0).T


def forward_kernel(pieces, block, causal, *refs):
    query_ref, key_pos_ref, query_pos_ref = refs[:3]
    key_refs = refs[3 : 3 + pieces]
    value_refs = refs[3 + pieces : 3 + 2 * pieces]
    out_ref, total_ref = refs[3 + 2 * pieces :]
    rows = query_ref.shape[0]
    tile = tile_of(rows)
    scaled = query_ref[...].astype(F32) * SCALE
    query_up = scaled.T.astype(BF16)
    values_up = [ref[...].astype(F32).T.astype(BF16) for ref in value_refs]
    for start in range(0, rows, tile):
        keys = key_rows(start + tile, rows, block, causal)
        wide = beside(query_up[:, start : start + tile])
        query_pos = query_pos_ref[:, start : start + tile]
        limit = jnp.concatenate([query_pos, query_pos], axis=1)
        scores = []
        for piece in range(pieces):
            score = dot(key_refs[piece][:keys, :], wide)
            allowed = key_pos_ref[piece, :keys, :] <= limit
            scores.append(jnp.where(allowed, score, MASKED_SCORE))
        highest = functools.reduce(
            jnp.maximum, [jnp.max(score, axis=0, keepdims=True) for score in scores]
        )
        summed = jnp.zeros_like(highest)
        mixed = jnp.zeros((PAIR, 2 * tile), F32)
        for piece in range(pieces):
            raised = jnp.exp(scores[piece] - highest)
            summed = summed + jnp.sum(raised, axis=0, keepdims=True)
            mixed = mixed + dot(values_up[piece][:, :keys], raised.astype(BF16))
        mixed = mixed / summed
        out_ref[start : start + tile, :] = heads_back(mixed, tile).astype(BF16)
        total = highest + jnp.log(summed)
        total_ref[0, 0:1, start : start + tile] = total[:, :tile]
        total_ref[0, 1:2, start : start + tile] = total[:, tile:]


def attend_forward(queries, keys_values, key_pos, query_pos, block, causal):
    rows, width = queries.shape
    pieces = len(keys_values)
    pairs = width // PAIR
    column = pl.BlockSpec((rows, PAIR), lambda p: (0, p))
    second = pl.BlockSpec((rows, PAIR), lambda p: (0, p + pairs))
    whole_pos = pl.BlockSpec((pieces, rows, 1), lambda p: (0, 0, 0))
    row_pos = pl.BlockSpec((1, rows), lambda p: (0, 0))
    return pl.pallas_call(
        functools.partial(forward_kernel, pieces, block, causal),
        grid=(pairs,),
        in_specs=[column, whole_pos, row_pos] + [column] * pieces + [second] * pieces,
        out_specs=[column, pl.BlockSpec((1, 2, rows), lambda p: (p, 0, 0))],
        out_shape=[
            jax.ShapeDtypeStruct((rows, width), BF16),
            jax.ShapeDtypeStruct((pairs, 2, rows), F32),
        ],
        compiler_params=pltpu.CompilerParams(vmem_limit_bytes=VMEM_LIMIT),
        cost_estimate=pl.CostEstimate(
            flops=8 * rows * rows * pieces * width,
            bytes_accessed=2 * rows * width * (2 + 2 * pieces),
            transcendentals=rows * rows * pieces * width // HEAD,
        ),
    )(queries, key_pos, query_pos, *keys_values, *keys_values)


def backward_kernel(pieces, block, causal, *refs):
    query_ref, out_ref, grad_ref, total_ref, key_pos_ref, query_pos_ref = refs[:6]
    key_refs = refs[6 : 6 + pieces]
    value_refs = refs[6 + pieces : 6 + 2 * pieces]
    dquery_ref, down_ref = refs[6 + 2 * pieces : 8 + 2 * pieces]
    dother_refs = refs[8 + 2 * pieces : 7 + 3 * pieces]
    dkey_ref, dvalue_ref = refs[7 + 3 * pieces :]
    rows = query_ref.shape[0]
    tile = tile_of(rows)
    scaled = query_ref[...].astype(F32) * SCALE
    query_up = scaled.T
    scaled = scaled.astype(BF16)
    grad_up = grad_ref[...].astype(F32).T
    out_up = out_ref[...].astype(F32).T
    keys_up = [ref[...].astype(F32).T.astype(BF16) for ref in key_refs]
    product_up = grad_up * out_up
    query_up = query_up.astype(BF16)
    grad_up = grad_up.astype(BF16)
    dkey_ref[...] = jnp.zeros_like(dkey_ref)
    dvalue_ref[...] = jnp.zeros_like(dvalue_ref)
    for start in range(0, rows, tile):
        stop = start + tile
        keys = key_rows(stop, rows, block, causal)
        query_wide = beside(query_up[:, start:stop])
        grad_wide = beside(grad_up[:, start:stop])
        query_tall = below(scaled[start:stop, :])
        grad_tall = below(grad_ref[start:stop, :])
        product = product_up[:, start:stop]
        centre = jnp.concatenate(
            [
                jnp.sum(product[:HEAD], axis=0, keepdims=True),
                jnp.sum(product[HEAD:], axis=0, keepdims=True),
            ],
            axis=1,
        )
        total = jnp.concatenate(
            [total_ref[0, 0:1, start:stop], total_ref[0, 1:2, start:stop]], axis=1
        )
        query_pos = query_pos_ref[:, start:stop]
        limit = jnp.concatenate([query_pos, query_pos], axis=1)
        dquery = jnp.zeros((PAIR, 2 * tile), F32)
        for piece in range(pieces):
            score = dot(key_refs[piece][:keys, :], query_wide)
            allowed = key_pos_ref[piece, :keys, :] <= limit
            probs = jnp.exp(jnp.where(allowed, score, MASKED_SCORE) - total)
            dprob = dot(value_refs[piece][:keys, :], grad_wide)
            dscore = (probs * (dprob - centre)).astype(BF16)
            dvalue_ref[piece, :keys, :] += dot(probs.astype(BF16), grad_tall)
            dkey_ref[piece, :keys, :] += dot(dscore, query_tall)
            dquery = dquery + dot(keys_up[piece][:, :keys], dscore)
        dquery_ref[start:stop, :] = (heads_back(dquery, tile) * SCALE).astype(BF16)
    down_ref[0] = dkey_ref[0]
    down_ref[1] = dvalue_ref[0]
    for piece in range(1, pieces):
        dother_refs[piece - 1][0] = dkey_ref[piece].astype(BF16)
        dother_refs[piece - 1][1] = dvalue_ref[piece].astype(BF16)


def attend_backward(
    queries, keys_values, outputs, grads, totals, key_pos, query_pos, block, causal
):
    rows, width = queries.shape
    pieces = len(keys_values)
    pairs = width // PAIR
    column = pl.BlockSpec((rows, PAIR), lambda p: (0, p))
    second = pl.BlockSpec((rows, PAIR), lambda p: (0, p + pairs))
    whole_pos = pl.BlockSpec((pieces, rows, 1), lambda p: (0, 0, 0))
    row_pos = pl.BlockSpec((1, rows), lambda p: (0, 0))
    both = pl.BlockSpec((2, rows, PAIR), lambda p: (0, 0, p))
    return pl.pallas_call(
        functools.partial(backward_kernel, pieces, block, causal),
        grid=(pairs,),
        in_specs=[
            column,
            column,
            column,
            pl.BlockSpec((1, 2, rows), lambda p: (p, 0, 0)),
            whole_pos,
            row_pos,
        ]
        + [column] * pieces
        + [second] * pieces,
        out_specs=[column, both] + [both] * (pieces - 1),
        out_shape=[
            jax.ShapeDtypeStruct((rows, width), BF16),
            jax.ShapeDtypeStruct((2, rows, width), F32),
        ]
        + [jax.ShapeDtypeStruct((2, rows, width), BF16)] * (pieces - 1),
        scratch_shapes=[pltpu.VMEM((pieces, rows, PAIR), F32)] * 2,
        compiler_params=pltpu.CompilerParams(vmem_limit_bytes=VMEM_LIMIT),
        cost_estimate=pl.CostEstimate(
            flops=20 * rows * rows * pieces * width,
            bytes_accessed=2 * rows * width * (6 + 4 * pieces),
            transcendentals=rows * rows * pieces * width // HEAD,
        ),
    )(queries, outputs, grads, totals, key_pos, query_pos, *keys_values, *keys_values)


def place_kernel(place_ref, *refs):
    out_ref = refs[8]
    here, core = place_ref[0], place_ref[1]
    half = refs[0].shape[1]
    for which in range(2):
        side = core if which == 0 else 1 - core
        columns = pl.ds(pl.multiple_of(side * half, 128), half)
        for step in range(4):
            out_ref[here ^ step, :, columns] = refs[which * 4 + step][...]


def placed(place, parts, first, count):
    rows = parts[0].shape[0]
    half = 512
    steps = 2
    chunk = rows // steps
    out = pl.pallas_call(
        place_kernel,
        grid_spec=pltpu.PrefetchScalarGridSpec(
            num_scalar_prefetch=1,
            grid=(count, steps),
            in_specs=[pl.BlockSpec((chunk, half), lambda w, r, s: (r, first + w))] * 8,
            out_specs=pl.BlockSpec((4, chunk, 2 * half), lambda w, r, s: (0, r, w)),
        ),
        out_shape=jax.ShapeDtypeStruct((4, rows, count * 2 * half), BF16),
        compiler_params=pltpu.CompilerParams(vmem_limit_bytes=VMEM_LIMIT),
        cost_estimate=pl.CostEstimate(
            flops=0, bytes_accessed=4 * 4 * rows * count * 2 * half, transcendentals=0
        ),
    )(place, *parts)
    return out.reshape(4 * rows, count * 2 * half)


def swap_pairs(size, bit):
    return [(index, index ^ bit) for index in range(size)]


def gather_group(weights, core):
    seq = lax.axis_size("seq")
    half = weights[0].shape[1] // 2
    mine = jnp.concatenate(
        [lax.dynamic_slice_in_dim(item, core * half, half, 1) for item in weights], axis=1
    )
    other = jnp.concatenate(
        [lax.dynamic_slice_in_dim(item, (1 - core) * half, half, 1) for item in weights], axis=1
    )
    along_x, along_y, cores = swap_pairs(4, 1), swap_pairs(4, 2), swap_pairs(seq, 1)
    from_x = lax.ppermute(mine, "dp", along_x)
    from_y = lax.ppermute(mine, "dp", along_y)
    rows = mine.shape[0] // 2
    diagonal = jnp.concatenate(
        [
            lax.ppermute(from_y[:rows], "dp", along_x),
            lax.ppermute(from_x[rows:], "dp", along_y),
        ],
        axis=0,
    )
    return [mine, from_x, from_y, diagonal, other] + [
        lax.ppermute(item, "seq", cores) for item in (from_x, from_y, diagonal)
    ]


def gather_dp(item):
    return lax.all_gather(item, "dp", axis=0, tiled=True)


def gather_all(item):
    count = lax.axis_size("seq")
    rows = item.shape[0] // count
    mine = lax.dynamic_slice_in_dim(item, lax.axis_index("seq") * rows, rows, 0)
    return lax.all_gather(mine, ("dp", "seq"), axis=0, tiled=True)


def take(item, index, axis):
    return lax.dynamic_index_in_dim(item, index, axis, keepdims=False)


def halve(item, axis, bit, name, mask, kind):
    size = lax.axis_size(name)
    received = lax.ppermute(take(item, 1 - bit, axis), name, swap_pairs(size, mask))
    return (take(item, bit, axis).astype(F32) + received.astype(F32)).astype(kind)


def scatter_sum(partial):
    rows, columns = partial.shape
    dp, seq = lax.axis_size("dp"), lax.axis_size("seq")
    if dp != 4 or seq != 8:
        return lax.psum_scatter(
            partial.astype(BF16), ("dp", "seq"), scatter_dimension=0, tiled=True
        ).astype(F32)
    here, there = lax.axis_index("dp"), lax.axis_index("seq")
    along_x, along_y = here % 2, here // 2
    core, z_low, z_high = there % 2, (there // 2) % 2, there // 4
    own = rows // 32
    kind = partial.dtype
    item = partial.reshape(2, 2, 4, 2, own, columns)
    item = halve(item, 3, core, "seq", 1, kind)
    one = halve(item[..., : columns // 2], 1, along_x, "dp", 1, kind)
    two = halve(item[..., columns // 2 :], 0, along_y, "dp", 2, kind)
    one = halve(one, 0, along_y, "dp", 2, kind)
    two = halve(two, 0, along_x, "dp", 1, kind)
    item = jnp.concatenate([one, two], axis=-1).reshape(2, 2, own, columns)
    item = halve(item, 1, z_low, "seq", 2, kind)
    return halve(item, 0, z_high, "seq", 4, F32)


def scatter_norms(norms):
    dp, seq = lax.axis_size("dp"), lax.axis_size("seq")
    width = norms[0].shape[0]
    own = width // (dp * seq)
    stacked = jnp.stack(norms, axis=0)
    if dp != 4 or seq != 8:
        return lax.psum_scatter(stacked, ("dp", "seq"), scatter_dimension=1, tiled=True)
    here, there = lax.axis_index("dp"), lax.axis_index("seq")
    item = stacked.reshape(6, 32, own).swapaxes(0, 1).reshape(2, 2, 2, 2, 2, 6, own)
    item = halve(item, 4, there % 2, "seq", 1, F32)
    item = halve(item, 1, here % 2, "dp", 1, F32)
    item = halve(item, 0, here // 2, "dp", 2, F32)
    item = halve(item, 1, (there // 2) % 2, "seq", 2, F32)
    return halve(item, 0, there // 4, "seq", 4, F32)


def body(
    target,
    source,
    target_len,
    source_len,
    self_query,
    self_key,
    self_value,
    self_output,
    cross_query,
    cross_key,
    cross_value,
    cross_output,
    feed_in,
    feed_out,
    adapter_down,
    adapter_up,
    self_gain,
    self_shift,
    cross_gain,
    cross_shift,
    final_gain,
    final_shift,
    cotangent,
):
    block, seqs, width = target.shape
    dp, seq = lax.axis_size("dp"), lax.axis_size("seq")
    group = seq // seqs
    rows = seqs * block
    there = lax.axis_index("seq")
    inner, which = there % group, there // group
    apart = [[start + group * step for step in range(seqs)] for start in range(group)]

    def to_sequence(item):
        return lax.all_to_all(
            item.swapaxes(0, 1), "seq", 0, 0, axis_index_groups=apart, tiled=True
        ).reshape(rows, width)

    def from_sequence(item):
        return lax.all_to_all(
            item.reshape(seqs, block, width), "seq", 0, 0, axis_index_groups=apart, tiled=True
        ).swapaxes(0, 1)

    def near(shift):
        return [
            (k * group + c, k * group + (c + shift) % group)
            for k in range(seqs)
            for c in range(group)
        ]

    def spread(item):
        return [item] + [lax.ppermute(item, "seq", near(-s)) for s in range(1, group)]

    def collect(own, others):
        for shift, other in enumerate(others, 1):
            own = own + lax.ppermute(other, "seq", near(shift)).astype(F32)
        return own.astype(BF16)

    inputs = to_sequence(target)
    memory = to_sequence(source)
    grad_out = to_sequence(cotangent).astype(F32)

    place = jnp.stack([lax.axis_index("dp"), there % 2]).astype(jnp.int32)
    if dp == 4 and seq == 8:
        core = there % 2
        parts = gather_group([self_query, self_key, self_value], core)
        w_kv = placed(place, parts, 1, 2)
        w_q = placed(place, parts, 0, 1)
        parts = gather_group(
            [self_output, cross_query, cross_key, cross_value, cross_output], core
        )
        w_o = placed(place, parts, 0, 1)
        w_cq = placed(place, parts, 1, 1)
        w_ckv = placed(place, parts, 2, 2)
        w_co = placed(place, parts, 4, 1)
    else:
        w_q = gather_dp(self_query)
        w_kv = gather_dp(jnp.concatenate([self_key, self_value], axis=1))
        w_o = gather_dp(self_output)
        w_cq = gather_dp(cross_query)
        w_ckv = gather_dp(jnp.concatenate([cross_key, cross_value], axis=1))
        w_co = gather_dp(cross_output)
    w_in = gather_all(feed_in)
    w_out = gather_all(feed_out)
    w_down = gather_all(adapter_down)
    w_up = gather_all(adapter_up)
    norms = jnp.stack([self_gain, self_shift, cross_gain, cross_shift, final_gain, final_shift])
    norms = lax.all_gather(norms, "dp", axis=1, tiled=True).astype(F32)
    gain_one, shift_one, gain_two, shift_two, gain_three, shift_three = [
        norms[index] for index in range(6)
    ]

    local = jnp.arange(rows, dtype=jnp.int32)

    def positions(place_in_group):
        return (local // block * group + place_in_group) * block + local % block

    target_limit = take(target_len, which, 0)
    source_limit = take(source_len, which, 0)
    key_pos = jnp.stack([positions((inner + shift) % group) for shift in range(group)])
    self_keys = jnp.where(key_pos < target_limit, key_pos, NEVER)[..., None]
    cross_keys = jnp.where(key_pos < source_limit, key_pos, NEVER)[..., None]
    self_rows = positions(inner)[None]
    cross_rows = jnp.full((1, rows), ALWAYS, jnp.int32)

    kv_own = dot(inputs, w_kv).astype(BF16)
    kv_all = spread(kv_own)
    queries = dot(inputs, w_q).astype(BF16)
    mixed, totals = attend_forward(queries, kv_all, self_keys, self_rows, block, True)
    resid_one = inputs.astype(F32) + dot(mixed, w_o)
    first, centre_one, rstd_one = norm_forward(resid_one, gain_one, shift_one)
    first_low = first.astype(BF16)
    ckv_own = dot(memory, w_ckv).astype(BF16)
    ckv_all = spread(ckv_own)
    cross_q = dot(first_low, w_cq).astype(BF16)
    cross_mixed, cross_totals = attend_forward(
        cross_q, ckv_all, cross_keys, cross_rows, block, False
    )
    resid_two = first + dot(cross_mixed, w_co)
    second, centre_two, rstd_two = norm_forward(resid_two, gain_two, shift_two)
    second_low = second.astype(BF16)
    pre_ffn = dot(second_low, w_in)
    pre_adapter = dot(second_low, w_down)
    hidden_ffn, gelu_back_ffn = jax.vjp(gelu_exact, pre_ffn)
    hidden_adapter, gelu_back_adapter = jax.vjp(gelu_exact, pre_adapter)
    hidden_adapter = hidden_adapter.astype(BF16)
    resid_three = (
        second + dot(hidden_ffn.astype(BF16), w_out) + 4.0 * dot(hidden_adapter, w_up)
    )
    final, centre_three, rstd_three = norm_forward(resid_three, gain_three, shift_three)
    output = from_sequence(final.astype(BF16))

    d_three, d_gain_three, d_shift_three = norm_backward(
        resid_three, centre_three, rstd_three, gain_three, grad_out
    )
    d_branch = d_three.astype(BF16)
    d_adapter = gelu_back_adapter(4.0 * dot_nt(d_branch, w_up))[0].astype(BF16)
    d_ffn = gelu_back_ffn(dot_nt(d_branch, w_out))[0].astype(BF16)
    d_second = d_three + dot_nt(d_ffn, w_in) + dot_nt(d_adapter, w_down)
    d_two, d_gain_two, d_shift_two = norm_backward(
        resid_two, centre_two, rstd_two, gain_two, d_second
    )
    d_two_low = d_two.astype(BF16)
    grad_down = dot_tn(second_low, d_adapter).astype(BF16)
    grad_up = (4.0 * dot_tn(hidden_adapter, d_branch)).astype(BF16)
    grad_co = dot_tn(cross_mixed, d_two_low).astype(BF16)
    d_cross = dot_nt(d_two_low, w_co).astype(BF16)
    d_cq, *d_ckv = attend_backward(
        cross_q, ckv_all, cross_mixed, d_cross, cross_totals, cross_keys, cross_rows, block, False
    )
    d_ckv = collect(d_ckv[0], d_ckv[1:])
    d_first = d_two + dot_nt(d_cq, w_cq)
    d_one, d_gain_one, d_shift_one = norm_backward(
        resid_one, centre_one, rstd_one, gain_one, d_first
    )
    d_one_low = d_one.astype(BF16)
    d_mixed = dot_nt(d_one_low, w_o).astype(BF16)
    grad_source = from_sequence(
        (dot_nt(d_ckv[0], w_ckv[:, :width]) + dot_nt(d_ckv[1], w_ckv[:, width:])).astype(BF16)
    )
    grad_o = dot_tn(mixed, d_one_low).astype(BF16)
    grad_cq = dot_tn(first_low, d_cq).astype(BF16)
    grad_ck = dot_tn(memory, d_ckv[0]).astype(BF16)
    grad_cv = dot_tn(memory, d_ckv[1]).astype(BF16)
    norm_sums = scatter_norms(
        [d_gain_one, d_shift_one, d_gain_two, d_shift_two, d_gain_three, d_shift_three]
    )
    d_q, *d_kv = attend_backward(
        queries, kv_all, mixed, d_mixed, totals, self_keys, self_rows, block, True
    )
    d_kv = collect(d_kv[0], d_kv[1:])
    grad_target = from_sequence(
        (
            d_one
            + dot_nt(d_q, w_q)
            + dot_nt(d_kv[0], w_kv[:, :width])
            + dot_nt(d_kv[1], w_kv[:, width:])
        ).astype(BF16)
    )
    grad_q = dot_tn(inputs, d_q).astype(BF16)
    grad_k = dot_tn(inputs, d_kv[0]).astype(BF16)
    grad_v = dot_tn(inputs, d_kv[1]).astype(BF16)

    sum_up = scatter_sum(grad_up)
    early = scatter_sum(jnp.concatenate([grad_down, grad_co], axis=1))
    adapter_width = grad_down.shape[1]
    middle = scatter_sum(jnp.concatenate([grad_o, grad_cq, grad_ck, grad_cv], axis=1))
    late = scatter_sum(jnp.concatenate([grad_q, grad_k, grad_v], axis=1))
    return (
        output,
        grad_target,
        grad_source,
        late[:, :width],
        late[:, width : 2 * width],
        late[:, 2 * width :],
        middle[:, :width],
        middle[:, width : 2 * width],
        middle[:, 2 * width : 3 * width],
        middle[:, 3 * width :],
        early[:, adapter_width:],
        early[:, :adapter_width],
        sum_up,
        norm_sums[0],
        norm_sums[1],
        norm_sums[2],
        norm_sums[3],
        norm_sums[4],
        norm_sums[5],
    )


def solution(mesh):
    tokens = P("seq", "dp", None)
    rows = P("dp", None)
    vector = P("dp")
    both = P(("dp", "seq"), None)
    return jax.shard_map(
        body,
        mesh=mesh,
        in_specs=(tokens, tokens, vector, vector) + (rows,) * 12 + (vector,) * 6 + (tokens,),
        out_specs=(tokens,) * 3 + (both,) * 10 + (P(("dp", "seq")),) * 6,
        check_vma=False,
    )
```

```python
import functools

import jax
import jax.numpy as jnp
from jax import lax
from jax.experimental import pallas as pl
from jax.experimental.pallas import tpu as pltpu
from jax.sharding import PartitionSpec as P

HEAD = 64
PAIR = 2 * HEAD
SCALE = HEAD ** (-0.5)
MASKED_SCORE = -1e30
NEVER = 2**30
ALWAYS = 2**29
F32 = jnp.float32
BF16 = jnp.bfloat16
STRIP = 128
ROOT_HALF = 0.7071067811865476
PDF_SCALE = 0.3989422804014327


def dot(left, right):
    return jnp.dot(left, right, preferred_element_type=F32)


def dot_tn(left, right):
    return lax.dot_general(left, right, (((0,), (0,)), ((), ())), preferred_element_type=F32)


def dot_nt(left, right):
    return lax.dot_general(left, right, (((1,), (1,)), ((), ())), preferred_element_type=F32)


def gelu_pair(inputs):
    below_it = 0.5 * (1.0 + lax.erf(inputs * ROOT_HALF))
    density = PDF_SCALE * jnp.exp(-0.5 * inputs * inputs)
    return inputs * below_it, below_it + inputs * density


def norm_parts(inputs):
    centre = jnp.mean(inputs, axis=-1, keepdims=True)
    centred = inputs - centre
    spread = jnp.mean(centred * centred, axis=-1, keepdims=True)
    rstd = lax.rsqrt(spread + 1e-05)
    return centred * rstd, rstd


def norm_backward(normed, rstd, gain, grad):
    inner = grad * gain
    mean_one = jnp.mean(inner, axis=-1, keepdims=True)
    mean_two = jnp.mean(inner * normed, axis=-1, keepdims=True)
    return rstd * (inner - mean_one - normed * mean_two)


def strips(rows):
    return [slice(start, start + STRIP) for start in range(0, rows, STRIP)]


MIB = 1024 * 1024


def bytes_of(shape, kind):
    size = jnp.dtype(kind).itemsize
    for extent in shape:
        size *= extent
    return size


def params(blocks, scratch=0, spare=10):
    limit = 2 * sum(bytes_of(shape, kind) for shape, kind in blocks) + scratch + spare * MIB
    return pltpu.CompilerParams(vmem_limit_bytes=min(limit, 60 * MIB))


def cost(micros):
    return pl.CostEstimate(
        flops=int(micros * 1.15e9), bytes_accessed=int(micros * 3.6e6), transcendentals=0
    )


def tile_of(rows):
    return 128 if rows % 128 == 0 else rows


def key_rows(tile_end, rows, block, causal):
    if not causal:
        return rows
    return min(rows, ((tile_end - 1) // block + 1) * block)


def beside(top):
    row = lax.broadcasted_iota(jnp.int32, top.shape, 0)
    zero = jnp.zeros_like(top)
    return jnp.concatenate(
        [jnp.where(row < HEAD, top, zero), jnp.where(row < HEAD, zero, top)], axis=1
    )


def below(side):
    lane = lax.broadcasted_iota(jnp.int32, side.shape, 1)
    zero = jnp.zeros_like(side)
    return jnp.concatenate(
        [jnp.where(lane < HEAD, side, zero), jnp.where(lane < HEAD, zero, side)], axis=0
    )


def heads_back(wide, tile):
    return jnp.concatenate([wide[:HEAD, :tile], wide[HEAD:, tile:]], axis=0).T


def forward_kernel(pieces, block, causal, *refs):
    query_ref, key_pos_ref, query_pos_ref = refs[:3]
    key_refs = refs[3 : 3 + pieces]
    value_refs = refs[3 + pieces : 3 + 2 * pieces]
    out_ref, total_ref = refs[3 + 2 * pieces :]
    rows = query_ref.shape[0]
    tile = tile_of(rows)
    scaled = query_ref[...].astype(F32) * SCALE
    query_up = scaled.T.astype(BF16)
    values_up = [ref[...].astype(F32).T.astype(BF16) for ref in value_refs]
    for start in range(0, rows, tile):
        keys = key_rows(start + tile, rows, block, causal)
        wide = beside(query_up[:, start : start + tile])
        query_pos = query_pos_ref[:, start : start + tile]
        limit = jnp.concatenate([query_pos, query_pos], axis=1)
        scores = []
        for piece in range(pieces):
            score = dot(key_refs[piece][:keys, :], wide)
            allowed = key_pos_ref[piece, :keys, :] <= limit
            scores.append(jnp.where(allowed, score, MASKED_SCORE))
        highest = functools.reduce(
            jnp.maximum, [jnp.max(score, axis=0, keepdims=True) for score in scores]
        )
        summed = jnp.zeros_like(highest)
        mixed = jnp.zeros((PAIR, 2 * tile), F32)
        for piece in range(pieces):
            raised = jnp.exp(scores[piece] - highest)
            summed = summed + jnp.sum(raised, axis=0, keepdims=True)
            mixed = mixed + dot(values_up[piece][:, :keys], raised.astype(BF16))
        mixed = mixed / summed
        out_ref[start : start + tile, :] = heads_back(mixed, tile).astype(BF16)
        total = highest + jnp.log(summed)
        total_ref[0, 0:1, start : start + tile] = total[:, :tile]
        total_ref[0, 1:2, start : start + tile] = total[:, tile:]


def attend_forward(queries, keys_values, key_pos, query_pos, block, causal):
    rows, width = queries.shape
    pieces = len(keys_values)
    pairs = width // PAIR
    column = pl.BlockSpec((rows, PAIR), lambda p: (0, p))
    second = pl.BlockSpec((rows, PAIR), lambda p: (0, p + pairs))
    whole_pos = pl.BlockSpec((pieces, rows, 1), lambda p: (0, 0, 0))
    row_pos = pl.BlockSpec((1, rows), lambda p: (0, 0))
    return pl.pallas_call(
        functools.partial(forward_kernel, pieces, block, causal),
        grid=(pairs,),
        in_specs=[column, whole_pos, row_pos] + [column] * pieces + [second] * pieces,
        out_specs=[column, pl.BlockSpec((1, 2, rows), lambda p: (p, 0, 0))],
        out_shape=[
            jax.ShapeDtypeStruct((rows, width), BF16),
            jax.ShapeDtypeStruct((pairs, 2, rows), F32),
        ],
        compiler_params=params(
            [((rows, PAIR), BF16)] * (2 + 2 * pieces) + [((pieces, rows, 128), F32)],
            spare=10 + 4 * (pieces > 2),
        ),
        cost_estimate=cost(18 if causal else 22),
        name="attend_forward",
    )(queries, key_pos, query_pos, *keys_values, *keys_values)


def backward_kernel(pieces, block, causal, *refs):
    query_ref, out_ref, grad_ref, total_ref, key_pos_ref, query_pos_ref = refs[:6]
    key_refs = refs[6 : 6 + pieces]
    value_refs = refs[6 + pieces : 6 + 2 * pieces]
    dquery_ref, down_ref = refs[6 + 2 * pieces : 8 + 2 * pieces]
    dother_refs = refs[8 + 2 * pieces : 7 + 3 * pieces]
    dkey_ref, dvalue_ref = refs[7 + 3 * pieces :]
    rows = query_ref.shape[0]
    tile = tile_of(rows)
    scaled = query_ref[...].astype(F32) * SCALE
    query_up = scaled.T
    scaled = scaled.astype(BF16)
    grad_up = grad_ref[...].astype(F32).T
    out_up = out_ref[...].astype(F32).T
    keys_up = [ref[...].astype(F32).T.astype(BF16) for ref in key_refs]
    product_up = grad_up * out_up
    query_up = query_up.astype(BF16)
    grad_up = grad_up.astype(BF16)
    dkey_ref[...] = jnp.zeros_like(dkey_ref)
    dvalue_ref[...] = jnp.zeros_like(dvalue_ref)
    for start in range(0, rows, tile):
        stop = start + tile
        keys = key_rows(stop, rows, block, causal)
        query_wide = beside(query_up[:, start:stop])
        grad_wide = beside(grad_up[:, start:stop])
        query_tall = below(scaled[start:stop, :])
        grad_tall = below(grad_ref[start:stop, :])
        product = product_up[:, start:stop]
        centre = jnp.concatenate(
            [
                jnp.sum(product[:HEAD], axis=0, keepdims=True),
                jnp.sum(product[HEAD:], axis=0, keepdims=True),
            ],
            axis=1,
        )
        total = jnp.concatenate(
            [total_ref[0, 0:1, start:stop], total_ref[0, 1:2, start:stop]], axis=1
        )
        query_pos = query_pos_ref[:, start:stop]
        limit = jnp.concatenate([query_pos, query_pos], axis=1)
        dquery = jnp.zeros((PAIR, 2 * tile), F32)
        for piece in range(pieces):
            score = dot(key_refs[piece][:keys, :], query_wide)
            allowed = key_pos_ref[piece, :keys, :] <= limit
            probs = jnp.exp(jnp.where(allowed, score, MASKED_SCORE) - total)
            dprob = dot(value_refs[piece][:keys, :], grad_wide)
            dscore = (probs * (dprob - centre)).astype(BF16)
            dvalue_ref[piece, :keys, :] += dot(probs.astype(BF16), grad_tall)
            dkey_ref[piece, :keys, :] += dot(dscore, query_tall)
            dquery = dquery + dot(keys_up[piece][:, :keys], dscore)
        dquery_ref[start:stop, :] = (heads_back(dquery, tile) * SCALE).astype(BF16)
    down_ref[0] = dkey_ref[0]
    down_ref[1] = dvalue_ref[0]
    for piece in range(1, pieces):
        dother_refs[piece - 1][0] = dkey_ref[piece].astype(BF16)
        dother_refs[piece - 1][1] = dvalue_ref[piece].astype(BF16)


def attend_backward(
    queries, keys_values, outputs, grads, totals, key_pos, query_pos, block, causal, first, pairs
):
    rows, width = queries.shape
    pieces = len(keys_values)
    shift = width // PAIR
    column = pl.BlockSpec((rows, PAIR), lambda p: (0, p + first))
    second = pl.BlockSpec((rows, PAIR), lambda p: (0, p + first + shift))
    whole_pos = pl.BlockSpec((pieces, rows, 1), lambda p: (0, 0, 0))
    row_pos = pl.BlockSpec((1, rows), lambda p: (0, 0))
    both = pl.BlockSpec((2, rows, PAIR), lambda p: (0, 0, p))
    size = pairs * PAIR
    return pl.pallas_call(
        functools.partial(backward_kernel, pieces, block, causal),
        grid=(pairs,),
        in_specs=[
            column,
            column,
            column,
            pl.BlockSpec((1, 2, rows), lambda p: (p + first, 0, 0)),
            whole_pos,
            row_pos,
        ]
        + [column] * pieces
        + [second] * pieces,
        out_specs=[pl.BlockSpec((rows, PAIR), lambda p: (0, p)), both] + [both] * (pieces - 1),
        out_shape=[
            jax.ShapeDtypeStruct((rows, size), BF16),
            jax.ShapeDtypeStruct((2, rows, size), F32),
        ]
        + [jax.ShapeDtypeStruct((2, rows, size), BF16)] * (pieces - 1),
        scratch_shapes=[pltpu.VMEM((pieces, rows, PAIR), F32)] * 2,
        compiler_params=params(
            [((rows, PAIR), BF16)] * (6 + 4 * pieces) + [((pieces, rows, 128), F32)] * 2,
            spare=10 + 4 * (pieces > 2),
        ),
        cost_estimate=cost((24 if causal else 28) * size / width),
        name="attend_backward",
    )(queries, outputs, grads, totals, key_pos, query_pos, *keys_values, *keys_values)


def offset(slot, size):
    return pl.multiple_of(slot * size, size)


def row_parts(place, refs):
    if len(refs) == 1:
        return [(0, refs[0][...])]
    own, one, two, near, far = [ref[...] for ref in refs]
    near_first = jnp.concatenate([near, far], axis=0)
    far_first = jnp.concatenate([far, near], axis=0)
    diagonal = jnp.where(place[4] == 0, near_first, far_first)
    return [(place[0], own), (place[1], one), (place[2], two), (place[3], diagonal)]


def times(left_ref, place, refs):
    total = None
    for slot, part in row_parts(place, refs):
        rows = part.shape[0]
        term = dot(left_ref[:, pl.ds(offset(slot, rows), rows)], part)
        total = term if total is None else total + term
    return total


def times_up(left, place, refs, store):
    for slot, part in row_parts(place, refs):
        rows = part.shape[0]
        store(pl.ds(offset(slot, rows), rows), dot_nt(left, part))


def part_specs(arrays, columns, index):
    return [pl.BlockSpec((item.shape[0], columns), lambda *at: (0, index(*at))) for item in arrays]


def fixed(shape):
    zeros = (0,) * len(shape)
    return pl.BlockSpec(shape, lambda *at: zeros)


def view(item, columns, index):
    if item.ndim == 2:
        return (item, pl.BlockSpec((item.shape[0], columns), lambda *at: (0, index)))
    return (item, pl.BlockSpec((1, item.shape[1], columns), lambda *at: (index, 0, 0)))


def run(kernel, name, place, grid, ins, outs, micros, scratch=(), spare=10):
    kept = [bool(out[3:]) for out in outs]
    outs = [out[:3] for out in outs]
    blocks = [(spec.block_shape, item.dtype) for item, spec in ins]
    blocks += [(spec.block_shape, kind) for _, kind, spec in outs]
    held = sum(bytes_of(item.shape, item.dtype) for item in scratch)
    return pl.pallas_call(
        kernel,
        grid_spec=pltpu.PrefetchScalarGridSpec(
            num_scalar_prefetch=1,
            grid=grid,
            in_specs=[spec for _, spec in ins],
            out_specs=[spec for _, _, spec in outs],
            scratch_shapes=list(scratch),
        ),
        out_shape=[
            pltpu.HBM(shape, kind) if keep else jax.ShapeDtypeStruct(shape, kind)
            for keep, (shape, kind, _) in zip(kept, outs)
        ],
        compiler_params=params(blocks, held, spare),
        cost_estimate=cost(micros),
        name=name,
    )(place, *[item for item, _ in ins])


def project_kernel(place, left_ref, *refs):
    refs[-1][...] = times(left_ref, place, refs[:-1]).astype(BF16)


def project(place, left, weight, first, count, name):
    rows, depth = left[1].block_shape
    chunk = 512
    steps = count * 1024 // chunk
    base = first * 1024 // chunk
    return run(
        project_kernel,
        name,
        place,
        (steps,),
        [left]
        + list(zip(weight, part_specs(weight, chunk, lambda j, s: base + j))),
        [((rows, count * 1024), BF16, pl.BlockSpec((rows, chunk), lambda j, s: (0, j)))],
        2.5 * count,
    )[0]


def mix_kernel(parts, both, place, mixed_ref, resid_ref, norm_ref, *refs):
    out_parts = refs[:parts]
    query_parts = refs[parts : 2 * parts] if both else ()
    outs = refs[2 * parts :] if both else refs[parts:]
    summed_ref, normed_ref, low_ref = outs[:3]
    step = pl.program_id(0)
    rows, width = summed_ref.shape
    half = width // 2

    @pl.when(step < 2)
    def _():
        columns = pl.ds(offset(step, half), half)
        summed_ref[:, columns] = resid_ref[:, columns].astype(F32) + times(
            mixed_ref, place, out_parts
        )

    @pl.when(step == 1)
    def _():
        for strip in strips(rows):
            normed, _ = norm_parts(summed_ref[strip, :])
            value = normed * norm_ref[0:1, :] + norm_ref[1:2, :]
            normed_ref[strip, :] = value
            low_ref[strip, :] = value.astype(BF16)

    if both:

        @pl.when(step >= 2)
        def _():
            outs[3][...] = times(low_ref, place, query_parts).astype(BF16)


def mix(place, mixed, resid, norm, w_out, at_out, w_query, at_query, name):
    rows, width = mixed.shape
    half = width // 2
    both = w_query is not None
    ins = [(mixed, fixed(mixed.shape)), resid, (norm, fixed(norm.shape))]
    ins += zip(
        w_out, part_specs(w_out, half, lambda j, s: at_out * 2 + jnp.minimum(j, 1))
    )
    outs = [
        ((rows, width), F32, fixed((rows, width)), True),
        ((rows, width), F32, fixed((rows, width)), True),
        ((rows, width), BF16, fixed((rows, width)), True),
    ]
    if both:
        ins += zip(
            w_query,
            part_specs(w_query, half, lambda j, s: at_query * 2 + jnp.maximum(j - 2, 0)),
        )
        outs += [
            (
                (rows, width),
                BF16,
                pl.BlockSpec((rows, half), lambda j, s: (0, jnp.maximum(j - 2, 0))),
            )
        ]
    return run(
        functools.partial(mix_kernel, len(w_out), both),
        name,
        place,
        (4 if both else 2,),
        ins,
        outs,
        6.3 if both else 4,
    )


def up_parts(place, refs, packed):
    if not packed:
        return [(0, refs[0][...])]
    unpacked = []
    for slot, part in row_parts(place, refs):
        rows = part.shape[0] // 2
        unpacked.append((slot, jnp.concatenate([part[:rows], part[rows:]], axis=1)))
    return unpacked


def chunk_of(refs, step, counts, use):
    low = 0
    for ref, count in zip(refs, counts):

        @pl.when((step >= low) & (step < low + count))
        def _(ref=ref):
            use(ref)

        low += count


def feed_specs(w_in, w_out, counts, first, chunk, width):
    in_specs = part_specs(w_in, chunk, lambda j, s: s[8 + first + j])
    shift = first if len(w_in) == 1 else 0
    out_specs, start = [], 0
    for count in counts:
        out_specs.append(
            pl.BlockSpec(
                (chunk, width),
                lambda j, s, start=start, count=count: (
                    shift + jnp.clip(j - start, 0, count - 1),
                    0,
                ),
            )
        )
        start += count
    return in_specs, out_specs


def feed_first_kernel(
    sizes, counts, packed, place, low_ref, second_ref, *refs
):
    n_in, n_out, n_down, n_up = sizes
    in_refs, refs = refs[:n_in], refs[n_in:]
    out_refs, refs = refs[:n_out], refs[n_out:]
    down_refs, refs = refs[:n_down], refs[n_down:]
    up_refs, refs = refs[:n_up], refs[n_up:]
    total_ref, slope_ref, hidden_ref, aslope_ref = refs
    step = pl.program_id(0)

    @pl.when(step == 0)
    def _():
        hidden, slope = gelu_pair(times(low_ref, place, down_refs))
        hidden_ref[...] = hidden.astype(BF16)
        aslope_ref[...] = slope.astype(BF16)
        total = None
        for slot, part in up_parts(place, up_refs, packed):
            count = part.shape[0]
            term = dot(hidden_ref[:, pl.ds(offset(slot, count), count)], part)
            total = term if total is None else total + term
        total_ref[...] = second_ref[...] + 4.0 * total

    feed_chunk(place, low_ref, in_refs, out_refs, counts, total_ref, slope_ref)


def feed_chunk(place, low_ref, in_refs, out_refs, counts, total_ref, slope_ref):
    hidden, slope = gelu_pair(times(low_ref, place, in_refs))
    slope_ref[...] = slope.astype(BF16)
    hidden = hidden.astype(BF16)

    def use(ref):
        total_ref[...] += dot(hidden, ref[...])

    chunk_of(out_refs, pl.program_id(0), counts, use)


def feed_second_kernel(
    sizes, counts, steps, place, low_ref, first_ref, grad_ref, norm_ref, *refs
):
    n_in, n_out = sizes
    in_refs, refs = refs[:n_in], refs[n_in:]
    out_refs, refs = refs[:n_out], refs[n_out:]
    final_ref, d_ref, dlow_ref, dnorm_ref, slope_ref, total_ref = refs
    step = pl.program_id(0)
    rows, width = total_ref.shape

    @pl.when(step == 0)
    def _():
        total_ref[...] = first_ref[...]

    feed_chunk(place, low_ref, in_refs, out_refs, counts, total_ref, slope_ref)

    @pl.when(step == steps - 1)
    def _():
        gain, shift = norm_ref[0:1, :], norm_ref[1:2, :]
        dgain = jnp.zeros((1, width), F32)
        dshift = jnp.zeros((1, width), F32)
        for strip in strips(rows):
            normed, rstd = norm_parts(total_ref[strip, :])
            final_ref[strip, :] = (normed * gain + shift).astype(BF16)
            grad = grad_ref[strip, :].astype(F32)
            dgain += jnp.sum(grad * normed, axis=0, keepdims=True)
            dshift += jnp.sum(grad, axis=0, keepdims=True)
            back = norm_backward(normed, rstd, gain, grad)
            d_ref[strip, :] = back
            dlow_ref[strip, :] = back.astype(BF16)
        dnorm_ref[0:1, :] = dgain
        dnorm_ref[1:2, :] = dshift


CHUNK = 512


def feed_first(place, low, second, w_in, w_out, counts, w_down, at_down, w_up, at_up):
    rows, width = low.shape
    adapter = 512
    packed = len(w_up) > 1
    steps = sum(counts)
    in_specs, out_specs = feed_specs(w_in, w_out, counts, 0, CHUNK, width)
    up_columns = 512 if packed else width
    full = fixed((rows, width))
    ins = [(low, full), (second, full)]
    ins += zip(w_in, in_specs)
    ins += zip(w_out, out_specs)
    ins += zip(w_down, part_specs(w_down, adapter, lambda j, s: at_down))
    ins += zip(w_up, part_specs(w_up, up_columns, lambda j, s: at_up))
    return run(
        functools.partial(
            feed_first_kernel, (len(w_in), len(w_out), len(w_down), len(w_up)), counts, packed
        ),
        "feed_first",
        place,
        (steps,),
        ins,
        [
            ((rows, width), F32, full),
            ((rows, steps * CHUNK), BF16, pl.BlockSpec((rows, CHUNK), lambda j, s: (0, j)), True),
            ((rows, adapter), BF16, fixed((rows, adapter)), True),
            ((rows, adapter), BF16, fixed((rows, adapter)), True),
        ],
        13,
    )


def feed_second(place, low, first, grad, norm, w_in, w_out, counts, start):
    rows, width = low.shape
    steps = sum(counts)
    in_specs, out_specs = feed_specs(w_in, w_out, counts, start, CHUNK, width)
    full = fixed((rows, width))
    ins = [(low, full), (first, full), (grad, full), (norm, fixed(norm.shape))]
    ins += zip(w_in, in_specs)
    ins += zip(w_out, out_specs)
    return run(
        functools.partial(feed_second_kernel, (len(w_in), len(w_out)), counts, steps),
        "feed_second",
        place,
        (steps,),
        ins,
        [
            ((rows, width), BF16, full, True),
            ((rows, width), F32, full),
            ((rows, width), BF16, full),
            ((2, width), F32, fixed((2, width)), True),
            ((rows, steps * CHUNK), BF16, pl.BlockSpec((rows, CHUNK), lambda j, s: (0, j)), True),
        ],
        13.5,
        scratch=[pltpu.VMEM((rows, width), F32)],
    )


def feed_backward_kernel(
    sizes,
    counts,
    packed,
    steps,
    place,
    dlow_ref,
    d_ref,
    resid_ref,
    norm_ref,
    slope_ref,
    later_ref,
    aslope_ref,
    *refs,
):
    n_in, n_out, n_down, n_up, n_mix = sizes
    in_refs, refs = refs[:n_in], refs[n_in:]
    out_refs, refs = refs[:n_out], refs[n_out:]
    down_refs, refs = refs[:n_down], refs[n_down:]
    up_refs, refs = refs[:n_up], refs[n_up:]
    mix_refs, refs = refs[:n_mix], refs[n_mix:]
    dtwo_ref, dtwo_low_ref, dnorm_ref, dadapter_ref, dmixed_ref, total_ref, dhidden_ref = refs
    step = pl.program_id(0)
    rows, width = total_ref.shape

    def add(columns, value):
        total_ref[:, columns] += value

    @pl.when(step == 0)
    def _():
        total_ref[...] = d_ref[...]
        for slot, part in up_parts(place, up_refs, packed):
            count = part.shape[0]
            columns = pl.ds(offset(slot, count), count)
            back = 4.0 * dot_nt(dlow_ref[...], part)
            dadapter_ref[:, columns] = (aslope_ref[:, columns].astype(F32) * back).astype(BF16)
        times_up(dadapter_ref[...], place, down_refs, add)

    def use(ref):
        back = dot_nt(dlow_ref[...], ref[...])
        chosen = jnp.where(step < steps // 2, slope_ref[...], later_ref[...])
        dhidden_ref[...] = (chosen.astype(F32) * back).astype(BF16)

    chunk_of(out_refs, step, counts, use)
    times_up(dhidden_ref[...], place, in_refs, add)

    @pl.when(step == steps - 1)
    def _():
        finish_norm(total_ref, resid_ref, norm_ref, dtwo_ref, dtwo_low_ref, dnorm_ref)

        def keep(columns, value):
            dmixed_ref[:, columns] = value.astype(BF16)

        times_up(dtwo_low_ref[...], place, mix_refs, keep)


def finish_norm(grad_ref, resid_ref, norm_ref, d_ref, dlow_ref, dnorm_ref):
    rows, width = grad_ref.shape
    gain = norm_ref[0:1, :]
    dgain = jnp.zeros((1, width), F32)
    dshift = jnp.zeros((1, width), F32)
    for strip in strips(rows):
        grad = grad_ref[strip, :]
        normed, rstd = norm_parts(resid_ref[strip, :])
        dgain += jnp.sum(grad * normed, axis=0, keepdims=True)
        dshift += jnp.sum(grad, axis=0, keepdims=True)
        back = norm_backward(normed, rstd, gain, grad)
        d_ref[strip, :] = back
        dlow_ref[strip, :] = back.astype(BF16)
    dnorm_ref[0:1, :] = dgain
    dnorm_ref[1:2, :] = dshift


def feed_backward(
    place,
    dlow,
    d_three,
    resid,
    norm,
    slope,
    later,
    aslope,
    w_in,
    w_out,
    counts,
    w_down,
    at_down,
    w_up,
    at_up,
    w_mix,
    at_mix,
):
    rows, width = dlow.shape
    hidden = w_in[0].shape[1]
    adapter = 512
    packed = len(w_up) > 1
    chunk = CHUNK
    steps = hidden // chunk
    in_specs, out_specs = feed_specs(w_in, w_out, counts, 0, chunk, width)
    middle = steps // 2
    up_columns = 512 if packed else width
    full = fixed((rows, width))
    ins = [
        (dlow, full),
        (d_three, full),
        (resid, full),
        (norm, fixed(norm.shape)),
        (slope, pl.BlockSpec((rows, chunk), lambda j, s: (0, jnp.minimum(j, middle - 1)))),
        (later, pl.BlockSpec((rows, chunk), lambda j, s: (0, jnp.maximum(j - middle, 0)))),
        (aslope, fixed((rows, adapter))),
    ]
    ins += zip(w_in, in_specs)
    ins += zip(w_out, out_specs)
    ins += zip(w_down, part_specs(w_down, adapter, lambda j, s: at_down))
    ins += zip(w_up, part_specs(w_up, up_columns, lambda j, s: at_up))
    ins += zip(w_mix, part_specs(w_mix, width, lambda j, s: at_mix))
    return run(
        functools.partial(
            feed_backward_kernel,
            (len(w_in), len(w_out), len(w_down), len(w_up), len(w_mix)),
            counts,
            packed,
            steps,
        ),
        "feed_backward",
        place,
        (steps,),
        ins,
        [
            ((rows, width), F32, full, True),
            ((rows, width), BF16, full),
            ((2, width), F32, fixed((2, width)), True),
            ((rows, adapter), BF16, fixed((rows, adapter))),
            ((rows, width), BF16, full),
        ],
        29,
        scratch=[pltpu.VMEM((rows, width), F32), pltpu.VMEM((rows, chunk), BF16)],
    )


def norm_step_kernel(parts, place, dquery_ref, d_ref, resid_ref, norm_ref, *refs):
    query_refs, refs = refs[:parts], refs[parts:]
    out_refs, refs = refs[:parts], refs[parts:]
    done_ref, done_low_ref, dnorm_ref, dmixed_ref, total_ref = refs
    step = pl.program_id(0)

    @pl.when(step == 0)
    def _():
        def add(columns, value):
            total_ref[:, columns] = d_ref[:, columns] + value

        times_up(dquery_ref[...], place, query_refs, add)
        finish_norm(total_ref, resid_ref, norm_ref, done_ref, done_low_ref, dnorm_ref)

    @pl.when(step == 1)
    def _():
        def keep(columns, value):
            dmixed_ref[:, columns] = value.astype(BF16)

        times_up(done_low_ref[...], place, out_refs, keep)


def norm_step(place, dquery, d_two, resid, norm, w_query, at_query, w_out, at_out):
    rows, width = dquery.shape
    full = fixed((rows, width))
    ins = [(dquery, full), (d_two, full), (resid, full), (norm, fixed(norm.shape))]
    ins += zip(w_query, part_specs(w_query, width, lambda j, s: at_query))
    ins += zip(w_out, part_specs(w_out, width, lambda j, s: at_out))
    return run(
        functools.partial(norm_step_kernel, len(w_query)),
        "norm_step",
        place,
        (2,),
        ins,
        [
            ((rows, width), F32, full, True),
            ((rows, width), BF16, full),
            ((2, width), F32, fixed((2, width)), True),
            ((rows, width), BF16, full),
        ],
        6.6,
        scratch=[pltpu.VMEM((rows, width), F32)],
    )


def inputs_back_kernel(lefts, parts, extra, place, *refs):
    left_refs, refs = refs[:lefts], refs[lefts:]
    part_refs, refs = refs[:parts], refs[parts:]
    if extra:
        extra_ref, refs = refs[0], refs[1:]
    out_ref, total_ref = refs
    step = pl.program_id(0)
    width = total_ref.shape[1]

    @pl.when(step == 0)
    def _():
        if extra == "base":
            total_ref[...] = extra_ref[...]
        else:
            total_ref[...] = jnp.zeros_like(total_ref)
        if extra == "beside":
            out_ref[:, :width] = extra_ref[...]

    def add(columns, value):
        total_ref[:, columns] += value

    for which in range(lefts):

        @pl.when(step == which)
        def _(which=which):
            left = left_refs[which][...]
            times_up(left.reshape(left.shape[-2:]), place, part_refs, add)

    @pl.when(step == lefts - 1)
    def _():
        out_ref[:, out_ref.shape[1] - width :] = total_ref[...].astype(BF16)


def inputs_back(place, lefts, weight, blocks, extra, item, name):
    depth = lefts[0][1].block_shape[-1]
    rows = lefts[0][1].block_shape[-2]
    width = 1024
    first = blocks[0]
    strides = {blocks[k + 1] - blocks[k] for k in range(len(blocks) - 1)}

    def at(j, s):
        index = first
        for k in range(1, len(blocks)):
            index = jnp.where(j == k, blocks[k], index)
        return first + j if strides == {1} else index

    ins = list(lefts)
    ins += zip(weight, part_specs(weight, depth, at))
    if extra:
        ins += [(item, fixed((rows, width)))]
    size = 2 * width if extra == "beside" else width
    return run(
        functools.partial(inputs_back_kernel, len(lefts), len(weight), extra),
        name,
        place,
        (len(lefts),),
        ins,
        [((rows, size), BF16, fixed((rows, size)))],
        3 * len(lefts) * depth / width,
        scratch=[pltpu.VMEM((rows, width), F32)],
    )[0]


def laid_out_kernel(slots, item_ref, *refs):
    out_ref = refs[-1]
    out_ref[slots[0]] = item_ref[0]
    for index, ref in enumerate(refs[:-1], 1):
        out_ref[slots[index]] = ref[...]


def laid_out(slots, item, parts):
    part = parts[0].shape
    return run(
        laid_out_kernel,
        "laid_out",
        slots,
        (1,),
        [(item, pl.BlockSpec((1,) + part, lambda j, s: (s[0], 0, 0)))]
        + [(piece, fixed(part)) for piece in parts],
        [(item.shape, item.dtype, fixed(item.shape))],
        1.5,
    )[0]


def swap_pairs(size, bit):
    return [(index, index ^ bit) for index in range(size)]


def by_core(even, odd):
    return [
        (d * 8 + s, (d ^ (odd if s % 2 else even)) * 8 + s) for d in range(4) for s in range(8)
    ]


def after(item, *others):
    return lax.optimization_barrier((item,) + others)[0]


def gather_first(own):
    one = lax.ppermute(own, ("dp", "seq"), by_core(1, 2))
    return (own, one, lax.ppermute(one, "seq", swap_pairs(8, 1)))


def gather_rest(parts, core, *others):
    one = parts[1]
    half = one.shape[0] // 2
    half_one = lax.dynamic_slice_in_dim(after(one, *others), core * half, half, 0)
    near = lax.ppermute(half_one, ("dp", "seq"), by_core(2, 1))
    return parts + (near, lax.ppermute(near, "seq", swap_pairs(8, 1)))


def gather_dp(item):
    return (lax.all_gather(item, "dp", axis=0, tiled=True),)


def row_blocks(value, size):
    return [value[start : start + size] for start in range(0, value.shape[0], size)]


def wgrad_kernel(fresh, split, scales, extra, place, *refs):
    count = len(fresh)
    left_refs, right_refs = refs[:count], refs[count : 2 * count]
    outs, up_ref = refs[2 * count + extra : -1], refs[-1]
    step = pl.program_id(0)
    wide = outs[0].shape[1]
    if extra:

        @pl.when(step == count)
        def _():
            rows = jnp.concatenate([ref[...] for ref in refs[2 * count : 2 * count + extra]])
            filler = jnp.zeros((128 - rows.shape[0], rows.shape[1]), F32)
            columns = jnp.concatenate([rows, filler], axis=0).T.astype(BF16)
            for index, item in enumerate(row_blocks(columns, 32)):
                at = (index % 8 * 4 + index // 8) * 32
                outs[0][at : at + 32, :128] = item

    for which in range(count):

        @pl.when(step == which)
        def _(which=which):
            right = right_refs[which][...]
            right = right.reshape(right.shape[-2:])
            tall = left_refs[which].shape[-1]
            if fresh[which]:
                left = left_refs[which][...]
                up_ref[:tall, :] = left.reshape(left.shape[-2:]).T
            value = dot(up_ref[:tall, :], right)
            value = (value * scales[which] if scales[which] != 1.0 else value).astype(BF16)
            own = tall // 32
            blocks = row_blocks(value, own)
            if split:
                even = jnp.concatenate(blocks[0::2], axis=0)
                odd = jnp.concatenate(blocks[1::2], axis=0)
                outs[0][...] = jnp.where(place[4] == 0, odd, even)
                outs[1][...] = jnp.where(place[4] == 0, even, odd)
                return
            folds = right.shape[1] // wide
            for index, item in enumerate(blocks):
                at = (index % 8 * 4 + index // 8) * own * folds
                for fold in range(folds):
                    low = at + fold * own
                    outs[0][low : low + own, :] = item[:, fold * wide : (fold + 1) * wide]


def wgrad(place, lefts, rights, wide, split, scales, name, extra=()):
    fresh = []
    for index, (item, spec) in enumerate(lefts):
        before = lefts[index - 1] if index else (None, None)
        fresh.append(item is not before[0] or spec is not before[1])
    rows, tall = lefts[0][1].block_shape[-2:]
    high = tall // 2 if split else tall
    spec = pl.BlockSpec((high, wide), lambda j, s: (0, j))
    more = 1 if extra else 0
    return run(
        functools.partial(wgrad_kernel, tuple(fresh), split, scales, len(extra)),
        name,
        place,
        (len(lefts) + more,),
        list(lefts) + list(rights) + [(item, fixed(item.shape)) for item in extra],
        [((high, wide * len(lefts) + 128 * more), BF16, spec, True)] * (2 if split else 1),
        1.6 * len(lefts) * wide / 1024,
        scratch=[pltpu.VMEM((tall, rows), BF16)],
    )


def take(item, index, axis):
    return lax.dynamic_index_in_dim(item, index, axis, keepdims=False)


def add(kept, received, kind=BF16):
    return (kept.astype(F32) + received.astype(F32)).astype(kind)


def sum_over(partial, name):
    return lax.psum_scatter(partial, name, scatter_dimension=0, tiled=True)


class Scatter:
    def __init__(self, send, keep):
        here, there = lax.axis_index("dp"), lax.axis_index("seq")
        self.x, self.y = here % 2, here // 2
        self.low, self.high = (there // 2) % 2, there // 4
        self.send, self.keep = send, keep
        self.width = keep.shape[1]

    def core(self):
        received = lax.ppermute(self.send, "seq", swap_pairs(8, 1))
        item = add(self.keep, received).reshape(2, 2, 128, self.width)
        self.one, self.two = item[..., : self.width // 2], item[..., self.width // 2 :]
        return self.one

    def plane_one(self):
        x, y = self.x, self.y
        from_x = lax.ppermute(take(self.one, 1 - x, 1), "dp", swap_pairs(4, 1))
        from_y = lax.ppermute(take(self.two, 1 - y, 0), "dp", swap_pairs(4, 2))
        self.one = add(take(self.one, x, 1), from_x)
        self.two = add(take(self.two, y, 0), from_y)
        return self.one

    def plane_two(self):
        x, y = self.x, self.y
        from_y = lax.ppermute(take(self.one, 1 - y, 0), "dp", swap_pairs(4, 2))
        from_x = lax.ppermute(take(self.two, 1 - x, 0), "dp", swap_pairs(4, 1))
        one = add(take(self.one, y, 0), from_y)
        two = add(take(self.two, x, 0), from_x)
        self.item = jnp.concatenate([one, two], axis=1).reshape(2, 2, 32, self.width)
        return self.item

    def z_one(self):
        received = lax.ppermute(take(self.item, 1 - self.low, 1), "seq", swap_pairs(8, 2))
        self.item = add(take(self.item, self.low, 1), received)
        return self.item

    def z_two(self):
        received = lax.ppermute(take(self.item, 1 - self.high, 0), "seq", swap_pairs(8, 4))
        self.item = add(take(self.item, self.high, 0), received, F32)
        return self.item


def sum_all(partial):
    return lax.psum_scatter(
        partial.astype(BF16), ("dp", "seq"), scatter_dimension=0, tiled=True
    ).astype(F32)


def body(
    target,
    source,
    target_len,
    source_len,
    self_query,
    self_key,
    self_value,
    self_output,
    cross_query,
    cross_key,
    cross_value,
    cross_output,
    feed_in,
    feed_out,
    adapter_down,
    adapter_up,
    self_gain,
    self_shift,
    cross_gain,
    cross_shift,
    final_gain,
    final_shift,
    cotangent,
):
    block, seqs, width = target.shape
    dp, seq = lax.axis_size("dp"), lax.axis_size("seq")
    group = seq // seqs
    rows = seqs * block
    here, there = lax.axis_index("dp"), lax.axis_index("seq")
    inner, which = there % group, there // group
    core = there % 2
    halving = dp == 4 and seq == 8
    apart = [[start + group * step for step in range(seqs)] for start in range(group)]

    def to_sequence(item):
        return lax.all_to_all(
            item.swapaxes(0, 1), "seq", 0, 0, axis_index_groups=apart, tiled=True
        ).reshape(rows, item.shape[-1])

    slots = jnp.stack([which ^ bit for bit in range(seqs)]).astype(jnp.int32)

    def send_back(item):
        item = item.reshape(seqs, block, item.shape[-1])
        parts = [item]
        for bit in range(1, seqs):
            pairs = [(index, (index // group ^ bit) * group + index % group) for index in range(seq)]
            parts.append(lax.ppermute(take(item, which ^ bit, 0), "seq", pairs))
        return parts

    def set_down(parts, *others):
        item, *parts = lax.optimization_barrier((*parts, *others))[: len(parts)]
        return laid_out(slots, item, parts).swapaxes(0, 1)

    def near(shift):
        return [
            (k * group + c, k * group + (c + shift) % group)
            for k in range(seqs)
            for c in range(group)
        ]

    def spread(item):
        return [item] + [lax.ppermute(item, "seq", near(-s)) for s in range(1, group)]

    def collect(own, others):
        for shift, other in enumerate(others, 1):
            own = own + lax.ppermute(other, "seq", near(shift)).astype(F32)
        return own.astype(BF16)

    own_inputs, own_memory = to_sequence(target), to_sequence(source)
    inputs, memory = view(own_inputs, width, 0), view(own_memory, width, 0)
    grad_out = to_sequence(cotangent)
    vectors = jnp.stack([self_gain, self_shift, cross_gain, cross_shift, final_gain, final_shift])
    if halving:
        one = jnp.where(core == 0, here ^ 1, here ^ 2)
        two = jnp.where(core == 0, here ^ 2, here ^ 1)
        diagonal = here ^ 3
        chunks = [item * 2 + part for item in (here, one, two) for part in (0, 1)]
        chunks += [diagonal * 2 + core, diagonal * 2 + 1 - core]
        place = jnp.stack([here, one, two, diagonal, core, core, core, core] + chunks)
        first_group = jnp.concatenate(
            [self_query, self_key, self_value, cross_key, cross_value], axis=1
        )
        half = width // 2
        up_packed = jnp.concatenate([adapter_up[:, :half], adapter_up[:, half:]], axis=0)
        second_group = jnp.concatenate(
            [self_output, cross_query, cross_output, adapter_down, up_packed], axis=1
        )
        vector_parts = [vectors] + [
            lax.ppermute(vectors, "dp", swap_pairs(4, bit)) for bit in (1, 2, 3)
        ]
        w_self = gather_rest(gather_first(first_group), core, own_inputs, *vector_parts)
        w_mid = gather_first(after(second_group, w_self[3]))
        at_q, at_kv, at_ckv = (w_self, 0), (w_self, 1), (w_self, 3)
        parts = jnp.stack(vector_parts)
        vectors = jnp.concatenate([take(parts, here ^ slot, 0) for slot in range(4)], axis=1)
        counts_first, counts_second = (2, 2), (2, 1, 1)
    else:
        steps = feed_in.shape[1] // CHUNK
        place = jnp.stack([jnp.int32(0)] * 8 + [jnp.int32(j) for j in range(steps)])
        at_q = (gather_dp(self_query), 0)
        at_kv = (gather_dp(jnp.concatenate([self_key, self_value], axis=1)), 0)
        at_o, at_cq = (gather_dp(self_output), 0), (gather_dp(cross_query), 0)
        at_ckv = (gather_dp(jnp.concatenate([cross_key, cross_value], axis=1)), 0)
        at_co = (gather_dp(cross_output), 0)
        w_in, w_out = gather_dp(feed_in), gather_dp(feed_out)
        at_down, at_up = (gather_dp(adapter_down), 0), (gather_dp(adapter_up), 0)
        vectors = lax.all_gather(vectors, "dp", axis=1, tiled=True)
        out_first = out_second = w_out
        counts_first, counts_second = (steps // 2,), (steps - steps // 2,)
    place = place.astype(jnp.int32)
    vectors = vectors.astype(F32)
    norm_one, norm_two, norm_three = vectors[0:2], vectors[2:4], vectors[4:6]

    local = jnp.arange(rows, dtype=jnp.int32)

    def positions(place_in_group):
        return (local // block * group + place_in_group) * block + local % block

    target_limit = take(target_len, which, 0)
    source_limit = take(source_len, which, 0)
    key_pos = jnp.stack([positions((inner + shift) % group) for shift in range(group)])
    self_keys = jnp.where(key_pos < target_limit, key_pos, NEVER)[..., None]
    cross_keys = jnp.where(key_pos < source_limit, key_pos, NEVER)[..., None]
    self_rows = positions(inner)[None]
    cross_rows = jnp.full((1, rows), ALWAYS, jnp.int32)

    kv_own = project(place, inputs, *at_kv, 2, "self_kv")
    kv_all = spread(kv_own)
    queries = project(place, inputs, *at_q, 1, "self_q")
    if halving:
        w_mid = gather_rest(w_mid, core, queries)
        w_in = gather_first(after(feed_in, w_mid[1], queries))
    mixed, totals = attend_forward(queries, kv_all, self_keys, self_rows, block, True)
    ckv_own = project(
        place, (after(own_memory, mixed), memory[1]), *at_ckv, 2, "cross_kv"
    )
    ckv_all = spread(ckv_own)
    mixed = after(mixed, ckv_own)
    if halving:
        w_out = gather_first(after(feed_out, w_mid[1], mixed))
        at_o, at_cq, at_co = (w_mid, 0), (w_mid, 1), (w_mid, 2)
        at_down, at_up = (w_mid, 6), (w_mid, 7)
    resid_one, first, first_low, cross_q = mix(
        place, mixed, inputs, norm_one, *at_o, *at_cq, "mix_self"
    )
    if halving:
        w_in = gather_rest(w_in, core, cross_q)
    cross_mixed, cross_totals = attend_forward(
        cross_q, ckv_all, cross_keys, cross_rows, block, False
    )
    if halving:
        w_out = gather_rest(w_out, core, cross_mixed)
        out_first, out_second = w_out[:2], w_out[2:]
    resid_two, second, second_low = mix(
        place, cross_mixed, view(first, width, 0), norm_two, *at_co, None, None, "mix_cross"
    )
    partial, slope, hidden, adapter_slope = feed_first(
        place, second_low, second, w_in, out_first, counts_first, *at_down, *at_up
    )
    final, d_three, d_branch, d_norm_three, later = feed_second(
        place,
        second_low,
        partial,
        grad_out,
        norm_three,
        w_in,
        out_second,
        counts_second,
        sum(counts_first),
    )
    output = send_back(final)

    d_two, d_two_low, d_norm_two, d_adapter, d_cross = feed_backward(
        place,
        d_branch,
        d_three,
        resid_two,
        norm_two,
        slope,
        later,
        adapter_slope,
        w_in,
        w_out,
        counts_first + counts_second if halving else (steps,),
        *at_down,
        *at_up,
        *at_co,
    )

    d_two_low = after(d_two_low, output[1], output[2])

    def whole(item, layer=0):
        return view(item, item.shape[-1], layer)

    pairs = width // PAIR
    if halving:
        half = width // 2
        left = whole(cross_mixed)
        early = wgrad(
            place,
            [left, left, whole(second_low), whole(hidden)],
            [view(d_two_low, half, 0), view(d_two_low, half, 1), whole(d_adapter), whole(d_branch)],
            half,
            False,
            (1.0, 1.0, 1.0, 4.0),
            "wgrad_early",
        )[0]
        d_cross = after(d_cross, early)
        early = sum_over(early, "seq")
    d_cq, *d_ckv = attend_backward(
        cross_q,
        ckv_all,
        cross_mixed,
        d_cross,
        cross_totals,
        cross_keys,
        cross_rows,
        block,
        False,
        0,
        pairs,
    )
    d_cq = after(d_cq, output[3])
    output = set_down(output, d_cq)
    d_one, d_one_low, d_norm_one, d_mixed = norm_step(
        place, d_cq, d_two, resid_one, norm_one, *at_cq, *at_o
    )
    d_ckv = collect(after(d_ckv[0], d_one_low), d_ckv[1:])
    if halving:
        middle = wgrad(
            place,
            [memory, memory],
            [whole(d_ckv, 0), whole(d_ckv, 1)],
            width,
            False,
            (1.0,) * 2,
            "wgrad_memory",
            [d_norm_one, d_norm_two, d_norm_three],
        )[0]
        d_one_low = after(d_one_low, middle)
        middle = sum_over(after(middle, early), "seq")
        d_one_low = after(d_one_low, early)
        inner_sums = Scatter(
            *wgrad(
                place,
                [whole(mixed), whole(first_low)],
                [whole(d_one_low), whole(d_cq)],
                width,
                True,
                (1.0,) * 2,
                "wgrad_inner",
            )
        )
        d_ckv = after(d_ckv, inner_sums.send)
    grad_source = inputs_back(
        place,
        [whole(d_ckv, 0), whole(d_ckv, 1)],
        at_ckv[0],
        [at_ckv[1], at_ckv[1] + 1],
        None,
        None,
        "source_back",
    )
    d_mixed = after(d_mixed, grad_source)
    if halving:
        d_mixed = after(d_mixed, inner_sums.core())
    grad_source = send_back(grad_source)

    def self_backward(grads, first_pair):
        return attend_backward(
            queries,
            kv_all,
            mixed,
            grads,
            totals,
            self_keys,
            self_rows,
            block,
            True,
            first_pair,
            pairs // 2,
        )

    def self_sums(d_q, d_kv):
        return Scatter(
            *wgrad(
                place,
                [inputs] * 3,
                [whole(d_q), whole(d_kv, 0), whole(d_kv, 1)],
                width // 2,
                True,
                (1.0,) * 3,
                "wgrad_self",
            )
        )

    d_q_one, *d_kv_one = self_backward(d_mixed, 0)
    d_mixed = after(d_mixed, d_q_one, grad_source[1])
    if halving:
        d_mixed = after(d_mixed, inner_sums.plane_one())
    d_q_two, *d_kv_two = self_backward(d_mixed, pairs // 2)
    d_kv_one = collect(after(d_kv_one[0], d_q_two), d_kv_one[1:])
    if halving:
        d_q_one = after(d_q_one, d_q_two, grad_source[2], inner_sums.plane_two())
        late_one = self_sums(d_q_one, d_kv_one)
        d_kv_two[0] = after(d_kv_two[0], late_one.send)
    d_kv_two = collect(d_kv_two[0], d_kv_two[1:])
    if halving:
        d_q_two = after(d_q_two, late_one.core(), inner_sums.z_one(), middle)
        late_two = self_sums(d_q_two, d_kv_two)
        grad_source = set_down(grad_source, late_two.send)
        d_q_one = after(d_q_one, late_two.send, grad_source)
    at_self = at_q if halving else ((jnp.concatenate([at_q[0][0], at_kv[0][0]], axis=1),), 0)
    grad_target = inputs_back(
        place,
        [
            whole(d_q_one),
            whole(d_q_two),
            whole(d_kv_one, 0),
            whole(d_kv_two, 0),
            whole(d_kv_one, 1),
            whole(d_kv_two, 1),
        ],
        at_self[0],
        [2 * at_self[1] + index for index in range(6)],
        "base",
        d_one,
        "target_back",
    )
    grad_target = send_back(grad_target)
    if not halving:
        grad_source = set_down(grad_source)
        grad_target = set_down(grad_target)
    if halving:
        both = sum_over(jnp.concatenate([early, middle], axis=1), "dp").astype(F32)
        early, middle = both[:, : early.shape[1]], both[:, early.shape[1] :]
        grad_co, grad_down = early[:, :width], early[:, width : width + half]
        lifted = early[:, width + half :]
        folded = lifted.shape[0] // 2
        grad_up = jnp.concatenate([lifted[:folded], lifted[folded:]], axis=1)
        grad_ck, grad_cv = middle[:, :width], middle[:, width : 2 * width]
        norm_sums = middle[:, 2 * width : 2 * width + 6].T
        late_one.plane_one()
        late_two.core()
        late_one.plane_two()
        late_two.plane_one()
        inner_sums.z_two()
        late_two.plane_two()
        grad_target = set_down(grad_target, late_two.item, both)
        for late in (late_one, late_two):
            late.z_one()
            late.z_two()
        grad_o, grad_cq = inner_sums.item[:, :width], inner_sums.item[:, width:]
        grad_q, grad_k, grad_v = [
            jnp.concatenate(
                [late.item[:, index * half : (index + 1) * half] for late in (late_one, late_two)],
                axis=1,
            )
            for index in range(3)
        ]
    else:
        norm_sums = jnp.concatenate([d_norm_one, d_norm_two, d_norm_three], axis=0)
        norm_sums = lax.psum_scatter(norm_sums, ("dp", "seq"), scatter_dimension=1, tiled=True)
        grad_down = sum_all(dot_tn(second_low, d_adapter))
        grad_up = sum_all(4.0 * dot_tn(hidden, d_branch))
        grad_co = sum_all(dot_tn(cross_mixed, d_two_low))
        grad_o = sum_all(dot_tn(mixed, d_one_low))
        grad_cq = sum_all(dot_tn(first_low, d_cq))
        grad_ck = sum_all(dot_tn(own_memory, d_ckv[0]))
        grad_cv = sum_all(dot_tn(own_memory, d_ckv[1]))
        d_q = jnp.concatenate([d_q_one, d_q_two], axis=1)
        d_kv = jnp.concatenate([d_kv_one, d_kv_two], axis=2)
        grad_q = sum_all(dot_tn(own_inputs, d_q))
        grad_k = sum_all(dot_tn(own_inputs, d_kv[0]))
        grad_v = sum_all(dot_tn(own_inputs, d_kv[1]))
    return (
        output,
        grad_target,
        grad_source,
        grad_q,
        grad_k,
        grad_v,
        grad_o,
        grad_cq,
        grad_ck,
        grad_cv,
        grad_co,
        grad_down,
        grad_up,
        *[norm_sums[index] for index in range(6)],
    )


def solution(mesh):
    tokens = P("seq", "dp", None)
    rows = P("dp", None)
    vector = P("dp")
    both = P(("dp", "seq"), None)
    return jax.shard_map(
        body,
        mesh=mesh,
        in_specs=(tokens, tokens, vector, vector) + (rows,) * 12 + (vector,) * 6 + (tokens,),
        out_specs=(tokens,) * 3 + (both,) * 10 + (P(("dp", "seq")),) * 6,
        check_vma=False,
    )
```

```python
import functools

import jax
import jax.numpy as jnp
from jax import lax
from jax.experimental import pallas as pl
from jax.experimental.pallas import tpu as pltpu
from jax.sharding import PartitionSpec as P

HEAD = 64
PAIR = 2 * HEAD
SCALE = HEAD ** (-0.5)
MASKED_SCORE = -1e30
NEVER = 2**30
ALWAYS = 2**29
F32 = jnp.float32
BF16 = jnp.bfloat16
STRIP = 128
ROOT_HALF = 0.7071067811865476
PDF_SCALE = 0.3989422804014327


def dot(left, right):
    return jnp.dot(left, right, preferred_element_type=F32)


def dot_tn(left, right):
    return lax.dot_general(left, right, (((0,), (0,)), ((), ())), preferred_element_type=F32)


def dot_nt(left, right):
    return lax.dot_general(left, right, (((1,), (1,)), ((), ())), preferred_element_type=F32)


def gelu_pair(inputs):
    below_it = 0.5 * (1.0 + lax.erf(inputs * ROOT_HALF))
    density = PDF_SCALE * jnp.exp(-0.5 * inputs * inputs)
    return inputs * below_it, below_it + inputs * density


def norm_parts(inputs):
    centre = jnp.mean(inputs, axis=-1, keepdims=True)
    centred = inputs - centre
    spread = jnp.mean(centred * centred, axis=-1, keepdims=True)
    rstd = lax.rsqrt(spread + 1e-05)
    return centred * rstd, rstd


def norm_backward(normed, rstd, gain, grad):
    inner = grad * gain
    mean_one = jnp.mean(inner, axis=-1, keepdims=True)
    mean_two = jnp.mean(inner * normed, axis=-1, keepdims=True)
    return rstd * (inner - mean_one - normed * mean_two)


def strips(rows):
    return [slice(start, start + STRIP) for start in range(0, rows, STRIP)]


MIB = 1024 * 1024


def bytes_of(shape, kind):
    size = jnp.dtype(kind).itemsize
    for extent in shape:
        size *= extent
    return size


def in_hbm(item):
    if item.size * item.dtype.itemsize < 256 * 1024:
        return item
    return pltpu.with_memory_space_constraint(item, pltpu.HBM)


def params(blocks, scratch=0, spare=10):
    limit = 2 * sum(bytes_of(shape, kind) for shape, kind in blocks) + scratch + spare * MIB
    return pltpu.CompilerParams(vmem_limit_bytes=min(limit, 60 * MIB))


def cost(micros):
    return pl.CostEstimate(
        flops=int(micros * 1.15e9), bytes_accessed=int(micros * 3.6e6), transcendentals=0
    )


def tile_of(rows):
    return 128 if rows % 128 == 0 else rows


def key_rows(tile_end, rows, block, causal):
    if not causal:
        return rows
    return min(rows, ((tile_end - 1) // block + 1) * block)


def beside(top):
    row = lax.broadcasted_iota(jnp.int32, top.shape, 0)
    zero = jnp.zeros_like(top)
    return jnp.concatenate(
        [jnp.where(row < HEAD, top, zero), jnp.where(row < HEAD, zero, top)], axis=1
    )


def below(side):
    lane = lax.broadcasted_iota(jnp.int32, side.shape, 1)
    zero = jnp.zeros_like(side)
    return jnp.concatenate(
        [jnp.where(lane < HEAD, side, zero), jnp.where(lane < HEAD, zero, side)], axis=0
    )


def heads_back(wide, tile):
    return jnp.concatenate([wide[:HEAD, :tile], wide[HEAD:, tile:]], axis=0).T


def forward_kernel(pieces, block, causal, *refs):
    query_ref, key_pos_ref, query_pos_ref = refs[:3]
    key_refs = refs[3 : 3 + pieces]
    value_refs = refs[3 + pieces : 3 + 2 * pieces]
    out_ref, total_ref = refs[3 + 2 * pieces :]
    rows = query_ref.shape[0]
    tile = tile_of(rows)
    scaled = query_ref[...].astype(F32) * SCALE
    query_up = scaled.T.astype(BF16)
    values_up = [ref[...].astype(F32).T.astype(BF16) for ref in value_refs]
    for start in range(0, rows, tile):
        keys = key_rows(start + tile, rows, block, causal)
        wide = beside(query_up[:, start : start + tile])
        query_pos = query_pos_ref[:, start : start + tile]
        limit = jnp.concatenate([query_pos, query_pos], axis=1)
        scores = []
        for piece in range(pieces):
            score = dot(key_refs[piece][:keys, :], wide)
            allowed = key_pos_ref[piece, :keys, :] <= limit
            scores.append(jnp.where(allowed, score, MASKED_SCORE))
        highest = functools.reduce(
            jnp.maximum, [jnp.max(score, axis=0, keepdims=True) for score in scores]
        )
        summed = jnp.zeros_like(highest)
        mixed = jnp.zeros((PAIR, 2 * tile), F32)
        for piece in range(pieces):
            raised = jnp.exp(scores[piece] - highest)
            summed = summed + jnp.sum(raised, axis=0, keepdims=True)
            mixed = mixed + dot(values_up[piece][:, :keys], raised.astype(BF16))
        mixed = mixed / summed
        out_ref[start : start + tile, :] = heads_back(mixed, tile).astype(BF16)
        total = highest + jnp.log(summed)
        total_ref[0, 0:1, start : start + tile] = total[:, :tile]
        total_ref[0, 1:2, start : start + tile] = total[:, tile:]


def attend_forward(queries, keys_values, key_pos, query_pos, block, causal):
    rows, width = queries.shape
    pieces = len(keys_values)
    pairs = width // PAIR
    column = pl.BlockSpec((rows, PAIR), lambda p: (0, p))
    second = pl.BlockSpec((rows, PAIR), lambda p: (0, p + pairs))
    whole_pos = pl.BlockSpec((pieces, rows, 1), lambda p: (0, 0, 0))
    row_pos = pl.BlockSpec((1, rows), lambda p: (0, 0))
    return pl.pallas_call(
        functools.partial(forward_kernel, pieces, block, causal),
        grid=(pairs,),
        in_specs=[column, whole_pos, row_pos] + [column] * pieces + [second] * pieces,
        out_specs=[column, pl.BlockSpec((1, 2, rows), lambda p: (p, 0, 0))],
        out_shape=[
            jax.ShapeDtypeStruct((rows, width), BF16),
            jax.ShapeDtypeStruct((pairs, 2, rows), F32),
        ],
        compiler_params=params(
            [((rows, PAIR), BF16)] * (2 + 2 * pieces) + [((pieces, rows, 128), F32)],
            spare=10 + 4 * (pieces > 2),
        ),
        cost_estimate=cost(18 if causal else 22),
        name="attend_forward",
    )(queries, key_pos, query_pos, *keys_values, *keys_values)


def backward_kernel(pieces, block, causal, begun, *refs):
    refs = refs[: 6 + 2 * pieces] + refs[6 + 2 * pieces + begun :]
    query_ref, out_ref, grad_ref, total_ref, key_pos_ref, query_pos_ref = refs[:6]
    key_refs = refs[6 : 6 + pieces]
    value_refs = refs[6 + pieces : 6 + 2 * pieces]
    dquery_ref, down_ref = refs[6 + 2 * pieces : 8 + 2 * pieces]
    dother_refs = refs[8 + 2 * pieces : 7 + 3 * pieces]
    dkey_ref, dvalue_ref = refs[7 + 3 * pieces :]
    rows = query_ref.shape[0]
    tile = tile_of(rows)
    scaled = query_ref[...].astype(F32) * SCALE
    query_up = scaled.T
    scaled = scaled.astype(BF16)
    grad_up = grad_ref[...].astype(F32).T
    out_up = out_ref[...].astype(F32).T
    keys_up = [ref[...].astype(F32).T.astype(BF16) for ref in key_refs]
    product_up = grad_up * out_up
    query_up = query_up.astype(BF16)
    grad_up = grad_up.astype(BF16)
    dkey_ref[...] = jnp.zeros_like(dkey_ref)
    dvalue_ref[...] = jnp.zeros_like(dvalue_ref)
    for start in range(0, rows, tile):
        stop = start + tile
        keys = key_rows(stop, rows, block, causal)
        query_wide = beside(query_up[:, start:stop])
        grad_wide = beside(grad_up[:, start:stop])
        query_tall = below(scaled[start:stop, :])
        grad_tall = below(grad_ref[start:stop, :])
        product = product_up[:, start:stop]
        centre = jnp.concatenate(
            [
                jnp.sum(product[:HEAD], axis=0, keepdims=True),
                jnp.sum(product[HEAD:], axis=0, keepdims=True),
            ],
            axis=1,
        )
        total = jnp.concatenate(
            [total_ref[0, 0:1, start:stop], total_ref[0, 1:2, start:stop]], axis=1
        )
        query_pos = query_pos_ref[:, start:stop]
        limit = jnp.concatenate([query_pos, query_pos], axis=1)
        dquery = jnp.zeros((PAIR, 2 * tile), F32)
        for piece in range(pieces):
            score = dot(key_refs[piece][:keys, :], query_wide)
            allowed = key_pos_ref[piece, :keys, :] <= limit
            probs = jnp.exp(jnp.where(allowed, score, MASKED_SCORE) - total)
            dprob = dot(value_refs[piece][:keys, :], grad_wide)
            dscore = (probs * (dprob - centre)).astype(BF16)
            dvalue_ref[piece, :keys, :] += dot(probs.astype(BF16), grad_tall)
            dkey_ref[piece, :keys, :] += dot(dscore, query_tall)
            dquery = dquery + dot(keys_up[piece][:, :keys], dscore)
        dquery_ref[start:stop, :] = (heads_back(dquery, tile) * SCALE).astype(BF16)
    down_ref[0] = dkey_ref[0]
    down_ref[1] = dvalue_ref[0]
    for piece in range(1, pieces):
        dother_refs[piece - 1][0] = dkey_ref[piece].astype(BF16)
        dother_refs[piece - 1][1] = dvalue_ref[piece].astype(BF16)


def attend_backward(
    queries, keys_values, outputs, grads, totals, key_pos, query_pos, block, causal, span, begun=()
):
    first, pairs = span
    rows, width = queries.shape
    pieces = len(keys_values)
    shift = width // PAIR
    column = pl.BlockSpec((rows, PAIR), lambda p: (0, p + first))
    second = pl.BlockSpec((rows, PAIR), lambda p: (0, p + first + shift))
    whole_pos = pl.BlockSpec((pieces, rows, 1), lambda p: (0, 0, 0))
    row_pos = pl.BlockSpec((1, rows), lambda p: (0, 0))
    both = pl.BlockSpec((2, rows, PAIR), lambda p: (0, 0, p + first))
    held = 6 + 2 * pieces
    return pl.pallas_call(
        functools.partial(backward_kernel, pieces, block, causal, len(begun)),
        grid=(pairs,),
        in_specs=[
            column,
            column,
            column,
            pl.BlockSpec((1, 2, rows), lambda p: (p + first, 0, 0)),
            whole_pos,
            row_pos,
        ]
        + [column] * pieces
        + [second] * pieces
        + [pl.BlockSpec(memory_space=pl.ANY)] * len(begun),
        out_specs=[column, both] + [both] * (pieces - 1),
        out_shape=[
            pltpu.HBM((rows, width), BF16),
            pltpu.HBM((2, rows, width), F32),
        ]
        + [pltpu.HBM((2, rows, width), BF16)] * (pieces - 1),
        input_output_aliases={held + index: index for index in range(len(begun))},
        scratch_shapes=[pltpu.VMEM((pieces, rows, PAIR), F32)] * 2,
        compiler_params=params(
            [((rows, PAIR), BF16)] * (6 + 4 * pieces) + [((pieces, rows, 128), F32)] * 2,
            spare=10 + 4 * (pieces > 2),
        ),
        cost_estimate=cost((24 if causal else 28) * pairs * PAIR / width),
        name="attend_backward",
    )(queries, outputs, grads, totals, key_pos, query_pos, *keys_values, *keys_values, *begun)


def offset(slot, size):
    return pl.multiple_of(slot * size, size)


def row_parts(place, refs):
    if len(refs) == 1:
        return [(0, refs[0][...])]
    own, one, two, near, far = [ref[...] for ref in refs]
    near_first = jnp.concatenate([near, far], axis=0)
    far_first = jnp.concatenate([far, near], axis=0)
    diagonal = jnp.where(place[4] == 0, near_first, far_first)
    return [(place[0], own), (place[1], one), (place[2], two), (place[3], diagonal)]


def times(left_ref, place, refs):
    total = None
    for slot, part in row_parts(place, refs):
        rows = part.shape[0]
        term = dot(left_ref[:, pl.ds(offset(slot, rows), rows)], part)
        total = term if total is None else total + term
    return total


def times_up(left, place, refs, store):
    for slot, part in row_parts(place, refs):
        rows = part.shape[0]
        store(pl.ds(offset(slot, rows), rows), dot_nt(left, part))


def part_specs(arrays, columns, index):
    return [pl.BlockSpec((item.shape[0], columns), lambda *at: (0, index(*at))) for item in arrays]


def fixed(shape):
    zeros = (0,) * len(shape)
    return pl.BlockSpec(shape, lambda *at: zeros)


def view(item, columns, index):
    if item.ndim == 2:
        return (item, pl.BlockSpec((item.shape[0], columns), lambda *at: (0, index)))
    return (item, pl.BlockSpec((1, item.shape[1], columns), lambda *at: (index, 0, 0)))


def run(kernel, name, place, grid, ins, outs, micros, scratch=(), spare=10):
    kept = [bool(out[3:]) for out in outs]
    outs = [out[:3] for out in outs]
    blocks = [(spec.block_shape, item.dtype) for item, spec in ins]
    blocks += [(spec.block_shape, kind) for _, kind, spec in outs]
    held = sum(bytes_of(item.shape, item.dtype) for item in scratch)
    return pl.pallas_call(
        kernel,
        grid_spec=pltpu.PrefetchScalarGridSpec(
            num_scalar_prefetch=1,
            grid=grid,
            in_specs=[spec for _, spec in ins],
            out_specs=[spec for _, _, spec in outs],
            scratch_shapes=list(scratch),
        ),
        out_shape=[
            pltpu.HBM(shape, kind) if keep else jax.ShapeDtypeStruct(shape, kind)
            for keep, (shape, kind, _) in zip(kept, outs)
        ],
        compiler_params=params(blocks, held, spare),
        cost_estimate=cost(micros),
        name=name,
    )(place, *[in_hbm(item) for item, _ in ins])


def project_kernel(place, left_ref, *refs):
    refs[-1][...] = times(left_ref, place, refs[:-1]).astype(BF16)


def project(place, left, weight, first, count, name):
    rows, depth = left[1].block_shape
    chunk = 512
    steps = count * 1024 // chunk
    base = first * 1024 // chunk
    return run(
        project_kernel,
        name,
        place,
        (steps,),
        [left]
        + list(zip(weight, part_specs(weight, chunk, lambda j, s: base + j))),
        [((rows, count * 1024), BF16, pl.BlockSpec((rows, chunk), lambda j, s: (0, j)))],
        2.5 * count,
    )[0]


def mix_kernel(parts, both, place, mixed_ref, resid_ref, norm_ref, *refs):
    out_parts = refs[:parts]
    query_parts = refs[parts : 2 * parts] if both else ()
    outs = refs[2 * parts :] if both else refs[parts:]
    summed_ref, normed_ref, low_ref = outs[:3]
    step = pl.program_id(0)
    rows, width = summed_ref.shape
    half = width // 2

    @pl.when(step < 2)
    def _():
        columns = pl.ds(offset(step, half), half)
        summed_ref[:, columns] = resid_ref[:, columns].astype(F32) + times(
            mixed_ref, place, out_parts
        )

    @pl.when(step == 1)
    def _():
        for strip in strips(rows):
            normed, _ = norm_parts(summed_ref[strip, :])
            value = normed * norm_ref[0:1, :] + norm_ref[1:2, :]
            normed_ref[strip, :] = value
            low_ref[strip, :] = value.astype(BF16)

    if both:

        @pl.when(step >= 2)
        def _():
            outs[3][...] = times(low_ref, place, query_parts).astype(BF16)


def mix(place, mixed, resid, norm, w_out, at_out, w_query, at_query, name):
    rows, width = mixed.shape
    half = width // 2
    both = w_query is not None
    ins = [(mixed, fixed(mixed.shape)), resid, (norm, fixed(norm.shape))]
    ins += zip(
        w_out, part_specs(w_out, half, lambda j, s: at_out * 2 + jnp.minimum(j, 1))
    )
    outs = [
        ((rows, width), F32, fixed((rows, width)), True),
        ((rows, width), F32, fixed((rows, width)), True),
        ((rows, width), BF16, fixed((rows, width)), True),
    ]
    if both:
        ins += zip(
            w_query,
            part_specs(w_query, half, lambda j, s: at_query * 2 + jnp.maximum(j - 2, 0)),
        )
        outs += [
            (
                (rows, width),
                BF16,
                pl.BlockSpec((rows, half), lambda j, s: (0, jnp.maximum(j - 2, 0))),
            )
        ]
    return run(
        functools.partial(mix_kernel, len(w_out), both),
        name,
        place,
        (4 if both else 2,),
        ins,
        outs,
        6.3 if both else 4,
    )


def up_parts(place, refs, packed):
    if not packed:
        return [(0, refs[0][...])]
    unpacked = []
    for slot, part in row_parts(place, refs):
        rows = part.shape[0] // 2
        unpacked.append((slot, jnp.concatenate([part[:rows], part[rows:]], axis=1)))
    return unpacked


def chunk_of(refs, step, counts, use):
    low = 0
    for ref, count in zip(refs, counts):

        @pl.when((step >= low) & (step < low + count))
        def _(ref=ref):
            use(ref)

        low += count


def feed_specs(w_in, w_out, counts, first, chunk, width):
    in_specs = part_specs(w_in, chunk, lambda j, s: s[8 + first + j])
    shift = first if len(w_in) == 1 else 0
    out_specs, start = [], 0
    for count in counts:
        out_specs.append(
            pl.BlockSpec(
                (chunk, width),
                lambda j, s, start=start, count=count: (
                    shift + jnp.clip(j - start, 0, count - 1),
                    0,
                ),
            )
        )
        start += count
    return in_specs, out_specs


def feed_first_kernel(
    sizes, counts, packed, place, low_ref, second_ref, *refs
):
    n_in, n_out, n_down, n_up = sizes
    in_refs, refs = refs[:n_in], refs[n_in:]
    out_refs, refs = refs[:n_out], refs[n_out:]
    down_refs, refs = refs[:n_down], refs[n_down:]
    up_refs, refs = refs[:n_up], refs[n_up:]
    total_ref, slope_ref, hidden_ref, aslope_ref = refs
    step = pl.program_id(0)

    @pl.when(step == 0)
    def _():
        hidden, slope = gelu_pair(times(low_ref, place, down_refs))
        hidden_ref[...] = hidden.astype(BF16)
        aslope_ref[...] = slope.astype(BF16)
        total = None
        for slot, part in up_parts(place, up_refs, packed):
            count = part.shape[0]
            term = dot(hidden_ref[:, pl.ds(offset(slot, count), count)], part)
            total = term if total is None else total + term
        total_ref[...] = second_ref[...] + 4.0 * total

    feed_chunk(place, low_ref, in_refs, out_refs, counts, total_ref, slope_ref)


def feed_chunk(place, low_ref, in_refs, out_refs, counts, total_ref, slope_ref):
    hidden, slope = gelu_pair(times(low_ref, place, in_refs))
    slope_ref[...] = slope.astype(BF16)
    hidden = hidden.astype(BF16)

    def use(ref):
        total_ref[...] += dot(hidden, ref[...])

    chunk_of(out_refs, pl.program_id(0), counts, use)


def feed_second_kernel(
    sizes, counts, steps, place, low_ref, first_ref, grad_ref, norm_ref, *refs
):
    n_in, n_out = sizes
    in_refs, refs = refs[:n_in], refs[n_in:]
    out_refs, refs = refs[:n_out], refs[n_out:]
    final_ref, d_ref, dlow_ref, dnorm_ref, slope_ref, total_ref = refs
    step = pl.program_id(0)
    rows, width = total_ref.shape

    @pl.when(step == 0)
    def _():
        total_ref[...] = first_ref[...]

    feed_chunk(place, low_ref, in_refs, out_refs, counts, total_ref, slope_ref)

    @pl.when(step == steps - 1)
    def _():
        gain, shift = norm_ref[0:1, :], norm_ref[1:2, :]
        dgain = jnp.zeros((1, width), F32)
        dshift = jnp.zeros((1, width), F32)
        for strip in strips(rows):
            normed, rstd = norm_parts(total_ref[strip, :])
            final_ref[strip, :] = (normed * gain + shift).astype(BF16)
            grad = grad_ref[strip, :].astype(F32)
            dgain += jnp.sum(grad * normed, axis=0, keepdims=True)
            dshift += jnp.sum(grad, axis=0, keepdims=True)
            back = norm_backward(normed, rstd, gain, grad)
            d_ref[strip, :] = back
            dlow_ref[strip, :] = back.astype(BF16)
        dnorm_ref[0:1, :] = dgain
        dnorm_ref[1:2, :] = dshift


CHUNK = 512


def feed_first(place, low, second, w_in, w_out, counts, w_down, at_down, w_up, at_up):
    rows, width = low.shape
    adapter = 512
    packed = len(w_up) > 1
    steps = sum(counts)
    in_specs, out_specs = feed_specs(w_in, w_out, counts, 0, CHUNK, width)
    up_columns = 512 if packed else width
    full = fixed((rows, width))
    ins = [(low, full), (second, full)]
    ins += zip(w_in, in_specs)
    ins += zip(w_out, out_specs)
    ins += zip(w_down, part_specs(w_down, adapter, lambda j, s: at_down))
    ins += zip(w_up, part_specs(w_up, up_columns, lambda j, s: at_up))
    return run(
        functools.partial(
            feed_first_kernel, (len(w_in), len(w_out), len(w_down), len(w_up)), counts, packed
        ),
        "feed_first",
        place,
        (steps,),
        ins,
        [
            ((rows, width), F32, full),
            ((rows, steps * CHUNK), BF16, pl.BlockSpec((rows, CHUNK), lambda j, s: (0, j)), True),
            ((rows, adapter), BF16, fixed((rows, adapter)), True),
            ((rows, adapter), BF16, fixed((rows, adapter)), True),
        ],
        13,
    )


def feed_second(place, low, first, grad, norm, w_in, w_out, counts, start):
    rows, width = low.shape
    steps = sum(counts)
    in_specs, out_specs = feed_specs(w_in, w_out, counts, start, CHUNK, width)
    full = fixed((rows, width))
    ins = [(low, full), (first, full), (grad, full), (norm, fixed(norm.shape))]
    ins += zip(w_in, in_specs)
    ins += zip(w_out, out_specs)
    return run(
        functools.partial(feed_second_kernel, (len(w_in), len(w_out)), counts, steps),
        "feed_second",
        place,
        (steps,),
        ins,
        [
            ((rows, width), BF16, full, True),
            ((rows, width), F32, full),
            ((rows, width), BF16, full),
            ((2, width), F32, fixed((2, width)), True),
            ((rows, steps * CHUNK), BF16, pl.BlockSpec((rows, CHUNK), lambda j, s: (0, j)), True),
        ],
        13.5,
        scratch=[pltpu.VMEM((rows, width), F32)],
    )


def feed_backward_kernel(
    sizes,
    counts,
    packed,
    steps,
    place,
    dlow_ref,
    d_ref,
    resid_ref,
    norm_ref,
    slope_ref,
    later_ref,
    aslope_ref,
    *refs,
):
    n_in, n_out, n_down, n_up, n_mix = sizes
    in_refs, refs = refs[:n_in], refs[n_in:]
    out_refs, refs = refs[:n_out], refs[n_out:]
    down_refs, refs = refs[:n_down], refs[n_down:]
    up_refs, refs = refs[:n_up], refs[n_up:]
    mix_refs, refs = refs[:n_mix], refs[n_mix:]
    dtwo_ref, dtwo_low_ref, dnorm_ref, dadapter_ref, dmixed_ref, total_ref, dhidden_ref = refs
    step = pl.program_id(0)
    rows, width = total_ref.shape

    def add(columns, value):
        total_ref[:, columns] += value

    @pl.when(step == 0)
    def _():
        total_ref[...] = d_ref[...]
        for slot, part in up_parts(place, up_refs, packed):
            count = part.shape[0]
            columns = pl.ds(offset(slot, count), count)
            back = 4.0 * dot_nt(dlow_ref[...], part)
            dadapter_ref[:, columns] = (aslope_ref[:, columns].astype(F32) * back).astype(BF16)
        times_up(dadapter_ref[...], place, down_refs, add)

    def use(ref):
        back = dot_nt(dlow_ref[...], ref[...])
        chosen = jnp.where(step < steps // 2, slope_ref[...], later_ref[...])
        dhidden_ref[...] = (chosen.astype(F32) * back).astype(BF16)

    chunk_of(out_refs, step, counts, use)
    times_up(dhidden_ref[...], place, in_refs, add)

    @pl.when(step == steps - 1)
    def _():
        finish_norm(total_ref, resid_ref, norm_ref, dtwo_ref, dtwo_low_ref, dnorm_ref)

        def keep(columns, value):
            dmixed_ref[:, columns] = value.astype(BF16)

        times_up(dtwo_low_ref[...], place, mix_refs, keep)


def finish_norm(grad_ref, resid_ref, norm_ref, d_ref, dlow_ref, dnorm_ref):
    rows, width = grad_ref.shape
    gain = norm_ref[0:1, :]
    dgain = jnp.zeros((1, width), F32)
    dshift = jnp.zeros((1, width), F32)
    for strip in strips(rows):
        grad = grad_ref[strip, :]
        normed, rstd = norm_parts(resid_ref[strip, :])
        dgain += jnp.sum(grad * normed, axis=0, keepdims=True)
        dshift += jnp.sum(grad, axis=0, keepdims=True)
        back = norm_backward(normed, rstd, gain, grad)
        d_ref[strip, :] = back
        dlow_ref[strip, :] = back.astype(BF16)
    dnorm_ref[0:1, :] = dgain
    dnorm_ref[1:2, :] = dshift


def feed_backward(
    place,
    dlow,
    d_three,
    resid,
    norm,
    slope,
    later,
    aslope,
    w_in,
    w_out,
    counts,
    w_down,
    at_down,
    w_up,
    at_up,
    w_mix,
    at_mix,
):
    rows, width = dlow.shape
    hidden = w_in[0].shape[1]
    adapter = 512
    packed = len(w_up) > 1
    chunk = CHUNK
    steps = hidden // chunk
    in_specs, out_specs = feed_specs(w_in, w_out, counts, 0, chunk, width)
    middle = steps // 2
    up_columns = 512 if packed else width
    full = fixed((rows, width))
    ins = [
        (dlow, full),
        (d_three, full),
        (resid, full),
        (norm, fixed(norm.shape)),
        (slope, pl.BlockSpec((rows, chunk), lambda j, s: (0, jnp.minimum(j, middle - 1)))),
        (later, pl.BlockSpec((rows, chunk), lambda j, s: (0, jnp.maximum(j - middle, 0)))),
        (aslope, fixed((rows, adapter))),
    ]
    ins += zip(w_in, in_specs)
    ins += zip(w_out, out_specs)
    ins += zip(w_down, part_specs(w_down, adapter, lambda j, s: at_down))
    ins += zip(w_up, part_specs(w_up, up_columns, lambda j, s: at_up))
    ins += zip(w_mix, part_specs(w_mix, width, lambda j, s: at_mix))
    return run(
        functools.partial(
            feed_backward_kernel,
            (len(w_in), len(w_out), len(w_down), len(w_up), len(w_mix)),
            counts,
            packed,
            steps,
        ),
        "feed_backward",
        place,
        (steps,),
        ins,
        [
            ((rows, width), F32, full, True),
            ((rows, width), BF16, full),
            ((2, width), F32, fixed((2, width)), True),
            ((rows, adapter), BF16, fixed((rows, adapter))),
            ((rows, width), BF16, full),
        ],
        29,
        scratch=[pltpu.VMEM((rows, width), F32), pltpu.VMEM((rows, chunk), BF16)],
    )


def norm_step_kernel(parts, place, dquery_ref, d_ref, resid_ref, norm_ref, *refs):
    query_refs, refs = refs[:parts], refs[parts:]
    out_refs, refs = refs[:parts], refs[parts:]
    done_ref, done_low_ref, dnorm_ref, dmixed_ref, total_ref = refs
    step = pl.program_id(0)

    @pl.when(step == 0)
    def _():
        def add(columns, value):
            total_ref[:, columns] = d_ref[:, columns] + value

        times_up(dquery_ref[...], place, query_refs, add)
        finish_norm(total_ref, resid_ref, norm_ref, done_ref, done_low_ref, dnorm_ref)

    @pl.when(step == 1)
    def _():
        def keep(columns, value):
            dmixed_ref[:, columns] = value.astype(BF16)

        times_up(done_low_ref[...], place, out_refs, keep)


def norm_step(place, dquery, d_two, resid, norm, w_query, at_query, w_out, at_out):
    rows, width = dquery.shape
    full = fixed((rows, width))
    ins = [(dquery, full), (d_two, full), (resid, full), (norm, fixed(norm.shape))]
    ins += zip(w_query, part_specs(w_query, width, lambda j, s: at_query))
    ins += zip(w_out, part_specs(w_out, width, lambda j, s: at_out))
    return run(
        functools.partial(norm_step_kernel, len(w_query)),
        "norm_step",
        place,
        (2,),
        ins,
        [
            ((rows, width), F32, full, True),
            ((rows, width), BF16, full),
            ((2, width), F32, fixed((2, width)), True),
            ((rows, width), BF16, full),
        ],
        6.6,
        scratch=[pltpu.VMEM((rows, width), F32)],
    )


def inputs_back_kernel(lefts, parts, extra, place, *refs):
    left_refs, refs = refs[:lefts], refs[lefts:]
    part_refs, refs = refs[:parts], refs[parts:]
    if extra:
        extra_ref, refs = refs[0], refs[1:]
    out_ref, total_ref = refs
    step = pl.program_id(0)
    width = total_ref.shape[1]

    @pl.when(step == 0)
    def _():
        if extra == "base":
            total_ref[...] = extra_ref[...]
        else:
            total_ref[...] = jnp.zeros_like(total_ref)
        if extra == "beside":
            out_ref[:, :width] = extra_ref[...]

    def add(columns, value):
        total_ref[:, columns] += value

    for which in range(lefts):

        @pl.when(step == which)
        def _(which=which):
            left = left_refs[which][...]
            times_up(left.reshape(left.shape[-2:]), place, part_refs, add)

    @pl.when(step == lefts - 1)
    def _():
        out_ref[:, out_ref.shape[1] - width :] = total_ref[...].astype(BF16)


def inputs_back(place, lefts, weight, blocks, extra, item, name):
    depth = lefts[0][1].block_shape[-1]
    rows = lefts[0][1].block_shape[-2]
    width = 1024
    first = blocks[0]
    strides = {blocks[k + 1] - blocks[k] for k in range(len(blocks) - 1)}

    def at(j, s):
        index = first
        for k in range(1, len(blocks)):
            index = jnp.where(j == k, blocks[k], index)
        return first + j if strides == {1} else index

    ins = list(lefts)
    ins += zip(weight, part_specs(weight, depth, at))
    if extra:
        ins += [(item, fixed((rows, width)))]
    size = 2 * width if extra == "beside" else width
    return run(
        functools.partial(inputs_back_kernel, len(lefts), len(weight), extra),
        name,
        place,
        (len(lefts),),
        ins,
        [((rows, size), BF16, fixed((rows, size)))],
        3 * len(lefts) * depth / width,
        scratch=[pltpu.VMEM((rows, width), F32)],
    )[0]


def laid_out_kernel(slots, item_ref, *refs):
    out_ref = refs[-1]
    out_ref[slots[0]] = item_ref[0]
    for index, ref in enumerate(refs[:-1], 1):
        out_ref[slots[index]] = ref[...]


def laid_out(slots, item, parts):
    part = parts[0].shape
    return run(
        laid_out_kernel,
        "laid_out",
        slots,
        (1,),
        [(item, pl.BlockSpec((1,) + part, lambda j, s: (s[0], 0, 0)))]
        + [(piece, fixed(part)) for piece in parts],
        [(item.shape, item.dtype, fixed(item.shape))],
        1.5,
    )[0]


def swap_pairs(size, bit):
    return [(index, index ^ bit) for index in range(size)]


def by_core(even, odd):
    return [
        (d * 8 + s, (d ^ (odd if s % 2 else even)) * 8 + s) for d in range(4) for s in range(8)
    ]


def after(item, *others):
    return lax.optimization_barrier((item,) + others)[0]


def gather_first(own):
    return (own, lax.ppermute(own, ("dp", "seq"), by_core(1, 2)))


def gather_swap(parts, *others):
    return parts + (lax.ppermute(after(parts[1], *others), "seq", swap_pairs(8, 1)),)


def gather_near(parts, core, *others):
    one = parts[1]
    half = one.shape[0] // 2
    half_one = lax.dynamic_slice_in_dim(after(one, *others), core * half, half, 0)
    return parts + (lax.ppermute(half_one, ("dp", "seq"), by_core(2, 1)),)


def gather_far(parts, *others):
    return parts + (lax.ppermute(after(parts[3], *others), "seq", swap_pairs(8, 1)),)


def gather_dp(item):
    return (lax.all_gather(item, "dp", axis=0, tiled=True),)


def row_blocks(value, size):
    return [value[start : start + size] for start in range(0, value.shape[0], size)]


def wgrad_kernel(fresh, split, scales, extra, place, *refs):
    count = len(fresh)
    left_refs, right_refs = refs[:count], refs[count : 2 * count]
    outs, up_ref = refs[2 * count + extra : -1], refs[-1]
    step = pl.program_id(0)
    wide = outs[0].shape[1]
    if extra:

        @pl.when(step == count)
        def _():
            rows = jnp.concatenate([ref[...] for ref in refs[2 * count : 2 * count + extra]])
            filler = jnp.zeros((128 - rows.shape[0], rows.shape[1]), F32)
            columns = jnp.concatenate([rows, filler], axis=0).T.astype(BF16)
            for index, item in enumerate(row_blocks(columns, 32)):
                at = (index % 8 * 4 + index // 8) * 32
                outs[0][at : at + 32, :128] = item

    for which in range(count):

        @pl.when(step == which)
        def _(which=which):
            right = right_refs[which][...]
            right = right.reshape(right.shape[-2:])
            tall = left_refs[which].shape[-1]
            if fresh[which]:
                left = left_refs[which][...]
                up_ref[:tall, :] = left.reshape(left.shape[-2:]).T
            value = dot(up_ref[:tall, :], right)
            value = (value * scales[which] if scales[which] != 1.0 else value).astype(BF16)
            own = tall // 32
            blocks = row_blocks(value, own)
            if split:
                even = jnp.concatenate(blocks[0::2], axis=0)
                odd = jnp.concatenate(blocks[1::2], axis=0)
                outs[0][...] = jnp.where(place[4] == 0, odd, even)
                outs[1][...] = jnp.where(place[4] == 0, even, odd)
                return
            folds = right.shape[1] // wide
            for index, item in enumerate(blocks):
                at = (index % 8 * 4 + index // 8) * own * folds
                for fold in range(folds):
                    low = at + fold * own
                    outs[0][low : low + own, :] = item[:, fold * wide : (fold + 1) * wide]


def wgrad(place, lefts, rights, wide, split, scales, name, extra=()):
    fresh = []
    for index, (item, spec) in enumerate(lefts):
        before = lefts[index - 1] if index else (None, None)
        fresh.append(item is not before[0] or spec is not before[1])
    rows, tall = lefts[0][1].block_shape[-2:]
    high = tall // 2 if split else tall
    spec = pl.BlockSpec((high, wide), lambda j, s: (0, j))
    more = 1 if extra else 0
    return run(
        functools.partial(wgrad_kernel, tuple(fresh), split, scales, len(extra)),
        name,
        place,
        (len(lefts) + more,),
        list(lefts) + list(rights) + [(item, fixed(item.shape)) for item in extra],
        [((high, wide * len(lefts) + 128 * more), BF16, spec, True)] * (2 if split else 1),
        1.6 * len(lefts) * wide / 1024,
        scratch=[pltpu.VMEM((tall, rows), BF16)],
    )


def take(item, index, axis):
    return lax.dynamic_index_in_dim(item, index, axis, keepdims=False)


def add(kept, received, kind=BF16):
    return (kept.astype(F32) + received.astype(F32)).astype(kind)


def sum_over(partial, name):
    return lax.psum_scatter(partial, name, scatter_dimension=0, tiled=True)


class Scatter:
    def __init__(self, send, keep):
        here, there = lax.axis_index("dp"), lax.axis_index("seq")
        self.x, self.y = here % 2, here // 2
        self.low, self.high = (there // 2) % 2, there // 4
        self.send, self.keep = send, keep
        self.width = keep.shape[1]

    def core(self):
        received = lax.ppermute(self.send, "seq", swap_pairs(8, 1))
        item = add(self.keep, received).reshape(2, 2, 128, self.width)
        self.one, self.two = item[..., : self.width // 2], item[..., self.width // 2 :]
        return self.one

    def plane_one(self):
        x, y = self.x, self.y
        from_x = lax.ppermute(take(self.one, 1 - x, 1), "dp", swap_pairs(4, 1))
        from_y = lax.ppermute(take(self.two, 1 - y, 0), "dp", swap_pairs(4, 2))
        self.one = add(take(self.one, x, 1), from_x)
        self.two = add(take(self.two, y, 0), from_y)
        return self.one

    def plane_two(self):
        x, y = self.x, self.y
        from_y = lax.ppermute(take(self.one, 1 - y, 0), "dp", swap_pairs(4, 2))
        from_x = lax.ppermute(take(self.two, 1 - x, 0), "dp", swap_pairs(4, 1))
        one = add(take(self.one, y, 0), from_y)
        two = add(take(self.two, x, 0), from_x)
        self.item = jnp.concatenate([one, two], axis=1)
        return self.item

    def z_one(self):
        self.item = self.item.reshape(2, 2, 32, self.width)
        received = lax.ppermute(take(self.item, 1 - self.low, 1), "seq", swap_pairs(8, 2))
        self.item = add(take(self.item, self.low, 1), received)
        return self.item

    def z_two(self):
        received = lax.ppermute(take(self.item, 1 - self.high, 0), "seq", swap_pairs(8, 4))
        self.item = add(take(self.item, self.high, 0), received, F32)
        return self.item


def sum_all(partial):
    return lax.psum_scatter(
        partial.astype(BF16), ("dp", "seq"), scatter_dimension=0, tiled=True
    ).astype(F32)


def body(
    target,
    source,
    target_len,
    source_len,
    self_query,
    self_key,
    self_value,
    self_output,
    cross_query,
    cross_key,
    cross_value,
    cross_output,
    feed_in,
    feed_out,
    adapter_down,
    adapter_up,
    self_gain,
    self_shift,
    cross_gain,
    cross_shift,
    final_gain,
    final_shift,
    cotangent,
):
    block, seqs, width = target.shape
    dp, seq = lax.axis_size("dp"), lax.axis_size("seq")
    group = seq // seqs
    rows = seqs * block
    here, there = lax.axis_index("dp"), lax.axis_index("seq")
    inner, which = there % group, there // group
    core = there % 2
    halving = dp == 4 and seq == 8
    apart = [[start + group * step for step in range(seqs)] for start in range(group)]

    def to_sequence(item):
        return lax.all_to_all(
            item.swapaxes(0, 1), "seq", 0, 0, axis_index_groups=apart, tiled=True
        ).reshape(rows, item.shape[-1])

    slots = jnp.stack([which ^ bit for bit in range(seqs)]).astype(jnp.int32)

    def send_back(item):
        item = item.reshape(seqs, block, item.shape[-1])
        parts = [item]
        for bit in range(1, seqs):
            pairs = [(index, (index // group ^ bit) * group + index % group) for index in range(seq)]
            parts.append(lax.ppermute(take(item, which ^ bit, 0), "seq", pairs))
        return parts

    def set_down(parts, *others):
        item, *parts = lax.optimization_barrier((*parts, *others))[: len(parts)]
        return laid_out(slots, item, parts).swapaxes(0, 1)

    def near(shift):
        return [
            (k * group + c, k * group + (c + shift) % group)
            for k in range(seqs)
            for c in range(group)
        ]

    def spread(item):
        return [item] + [lax.ppermute(item, "seq", near(-s)) for s in range(1, group)]

    def collect(own, others):
        for shift, other in enumerate(others, 1):
            own = own + lax.ppermute(other, "seq", near(shift)).astype(F32)
        return own.astype(BF16)

    own_inputs, own_memory = to_sequence(target), to_sequence(source)
    inputs, memory = view(own_inputs, width, 0), view(own_memory, width, 0)
    grad_out = to_sequence(cotangent)
    vectors = jnp.stack([self_gain, self_shift, cross_gain, cross_shift, final_gain, final_shift])
    if halving:
        one = jnp.where(core == 0, here ^ 1, here ^ 2)
        two = jnp.where(core == 0, here ^ 2, here ^ 1)
        diagonal = here ^ 3
        chunks = [item * 2 + part for item in (here, one, two) for part in (0, 1)]
        chunks += [diagonal * 2 + core, diagonal * 2 + 1 - core]
        place = jnp.stack([here, one, two, diagonal, core, core, core, core] + chunks)
        first_group = jnp.concatenate(
            [self_query, self_key, self_value, cross_key, cross_value], axis=1
        )
        half = width // 2
        up_packed = jnp.concatenate([adapter_up[:, :half], adapter_up[:, half:]], axis=0)
        second_group = jnp.concatenate(
            [self_output, cross_query, cross_output, adapter_down, up_packed], axis=1
        )
        vector_parts = [vectors] + [
            lax.ppermute(vectors, "dp", swap_pairs(4, bit)) for bit in (1, 2, 3)
        ]
        w_self = gather_swap(gather_first(first_group))
        w_self = gather_far(
            gather_near(w_self, core, own_inputs, second_group, *vector_parts)
        )
        w_mid = gather_swap(gather_first(after(second_group, w_self[3])))
        w_in = gather_first(after(feed_in, w_mid[1]))
        at_q, at_kv, at_ckv = (w_self, 0), (w_self, 1), (w_self, 3)
        parts = jnp.stack(vector_parts)
        vectors = jnp.concatenate([take(parts, here ^ slot, 0) for slot in range(4)], axis=1)
        counts_first, counts_second = (2, 2), (2, 1, 1)
    else:
        steps = feed_in.shape[1] // CHUNK
        place = jnp.stack([jnp.int32(0)] * 8 + [jnp.int32(j) for j in range(steps)])
        at_q = (gather_dp(self_query), 0)
        at_kv = (gather_dp(jnp.concatenate([self_key, self_value], axis=1)), 0)
        at_o, at_cq = (gather_dp(self_output), 0), (gather_dp(cross_query), 0)
        at_ckv = (gather_dp(jnp.concatenate([cross_key, cross_value], axis=1)), 0)
        at_co = (gather_dp(cross_output), 0)
        w_in, w_out = gather_dp(feed_in), gather_dp(feed_out)
        at_down, at_up = (gather_dp(adapter_down), 0), (gather_dp(adapter_up), 0)
        vectors = lax.all_gather(vectors, "dp", axis=1, tiled=True)
        out_first = out_second = w_out
        counts_first, counts_second = (steps // 2,), (steps - steps // 2,)
    place = place.astype(jnp.int32)
    vectors = vectors.astype(F32)
    norm_one, norm_two, norm_three = vectors[0:2], vectors[2:4], vectors[4:6]

    local = jnp.arange(rows, dtype=jnp.int32)

    def positions(place_in_group):
        return (local // block * group + place_in_group) * block + local % block

    target_limit = take(target_len, which, 0)
    source_limit = take(source_len, which, 0)
    key_pos = jnp.stack([positions((inner + shift) % group) for shift in range(group)])
    self_keys = jnp.where(key_pos < target_limit, key_pos, NEVER)[..., None]
    cross_keys = jnp.where(key_pos < source_limit, key_pos, NEVER)[..., None]
    self_rows = positions(inner)[None]
    cross_rows = jnp.full((1, rows), ALWAYS, jnp.int32)

    kv_own = project(place, inputs, *at_kv, 2, "self_kv")
    kv_all = spread(kv_own)
    queries = project(place, inputs, *at_q, 1, "self_q")
    if halving:
        w_mid = gather_near(w_mid, core, queries)
        queries = after(queries, w_mid[1])
    mixed, totals = attend_forward(queries, kv_all, self_keys, self_rows, block, True)
    ckv_own = project(
        place, (after(own_memory, mixed), memory[1]), *at_ckv, 2, "cross_kv"
    )
    ckv_all = spread(ckv_own)
    mixed = after(mixed, ckv_own)
    if halving:
        w_mid = gather_far(w_mid, mixed)
        w_out = gather_first(after(feed_out, mixed))
        mixed = after(mixed, w_in[1])
        at_o, at_cq, at_co = (w_mid, 0), (w_mid, 1), (w_mid, 2)
        at_down, at_up = (w_mid, 6), (w_mid, 7)
    resid_one, first, first_low, cross_q = mix(
        place, mixed, inputs, norm_one, *at_o, *at_cq, "mix_self"
    )
    if halving:
        w_in = gather_near(gather_swap(w_in, cross_q), core, cross_q)
    cross_mixed, cross_totals = attend_forward(
        cross_q, ckv_all, cross_keys, cross_rows, block, False
    )
    if halving:
        w_in = gather_far(w_in, cross_mixed)
        w_out = gather_far(gather_near(gather_swap(w_out, cross_mixed), core, cross_mixed))
        out_first, out_second = w_out[:2], w_out[2:]
    resid_two, second, second_low = mix(
        place, cross_mixed, view(first, width, 0), norm_two, *at_co, None, None, "mix_cross"
    )
    partial, slope, hidden, adapter_slope = feed_first(
        place, second_low, second, w_in, out_first, counts_first, *at_down, *at_up
    )
    final, d_three, d_branch, d_norm_three, later = feed_second(
        place,
        second_low,
        partial,
        grad_out,
        norm_three,
        w_in,
        out_second,
        counts_second,
        sum(counts_first),
    )
    output = send_back(final)

    d_two, d_two_low, d_norm_two, d_adapter, d_cross = feed_backward(
        place,
        d_branch,
        d_three,
        resid_two,
        norm_two,
        slope,
        later,
        adapter_slope,
        w_in,
        w_out,
        counts_first + counts_second if halving else (steps,),
        *at_down,
        *at_up,
        *at_co,
    )

    d_two_low = after(d_two_low, *output[1:])

    def whole(item, layer=0):
        return view(item, item.shape[-1], layer)

    pairs = width // PAIR
    if halving:
        half = width // 2
        left = whole(cross_mixed)
        early = wgrad(
            place,
            [left, left, whole(second_low), whole(hidden)],
            [view(d_two_low, half, 0), view(d_two_low, half, 1), whole(d_adapter), whole(d_branch)],
            half,
            False,
            (1.0, 1.0, 1.0, 4.0),
            "wgrad_early",
        )[0]
        d_cross = after(d_cross, early)
        early = sum_over(early, "seq")
    d_cq, *d_ckv = attend_backward(
        cross_q,
        ckv_all,
        cross_mixed,
        d_cross,
        cross_totals,
        cross_keys,
        cross_rows,
        block,
        False,
        (0, pairs),
    )
    output = set_down(output, d_cq)
    d_one, d_one_low, d_norm_one, d_mixed = norm_step(
        place, d_cq, d_two, resid_one, norm_one, *at_cq, *at_o
    )
    d_ckv = collect(after(d_ckv[0], d_one_low), d_ckv[1:])
    grad_source = inputs_back(
        place,
        [whole(d_ckv, 0), whole(d_ckv, 1)],
        at_ckv[0],
        [at_ckv[1], at_ckv[1] + 1],
        None,
        None,
        "source_back",
    )
    d_ckv = after(d_ckv, grad_source)
    grad_source = send_back(grad_source)
    if halving:
        middle = wgrad(
            place,
            [memory, memory],
            [whole(d_ckv, 0), whole(d_ckv, 1)],
            width,
            False,
            (1.0,) * 2,
            "wgrad_memory",
            [d_norm_one, d_norm_two, d_norm_three],
        )[0]
        d_one_low = after(d_one_low, middle)
        middle = sum_over(after(middle, early), "seq")
        d_one_low = after(d_one_low, early)
        early = sum_over(early, "dp")
        inner_sums = Scatter(
            *wgrad(
                place,
                [whole(mixed), whole(first_low)],
                [whole(d_one_low), whole(d_cq)],
                width,
                True,
                (1.0,) * 2,
                "wgrad_inner",
            )
        )
    if halving:
        d_mixed = after(d_mixed, inner_sums.core())
    else:
        d_mixed = after(d_mixed, grad_source[0])

    begun = ()
    split = pairs * 3 // 4
    for span in ((0, split), (split, pairs - split)):
        begun = attend_backward(
            queries,
            kv_all,
            mixed,
            d_mixed,
            totals,
            self_keys,
            self_rows,
            block,
            True,
            span,
            begun,
        )
        if halving and span[0] == 0:
            d_mixed = after(d_mixed, begun[0], inner_sums.plane_one(), *grad_source[1:3])
    d_q, *d_kv = begun
    d_kv = collect(d_kv[0], d_kv[1:])
    if halving:
        late = Scatter(
            *wgrad(
                place,
                [inputs] * 3,
                [whole(d_q), whole(d_kv, 0), whole(d_kv, 1)],
                width,
                True,
                (1.0,) * 3,
                "wgrad_self",
            )
        )
        late.keep = after(late.keep, inner_sums.plane_two(), grad_source[3])
        d_q = after(d_q, late.send, late.core(), middle)
    at_self = at_q if halving else ((jnp.concatenate([at_q[0][0], at_kv[0][0]], axis=1),), 0)
    grad_target = inputs_back(
        place,
        [whole(d_q), whole(d_kv, 0), whole(d_kv, 1)],
        at_self[0],
        [at_self[1] + index for index in range(3)],
        "base",
        d_one,
        "target_back",
    )
    grad_source = set_down(grad_source, grad_target)
    grad_target = send_back(grad_target)
    if not halving:
        grad_target = set_down(grad_target)
    if halving:
        late.plane_one()
        late.one, late.two, *_ = lax.optimization_barrier((late.one, late.two, *grad_target))
        inner_sums.z_one()
        late.plane_two()
        inner_sums.z_two()
        late.z_one()
        late.z_two()
        middle = sum_over(middle, "dp").astype(F32)
        grad_target = set_down(grad_target, late.item)
        early = early.astype(F32)
        grad_co, grad_down = early[:, :width], early[:, width : width + half]
        lifted = early[:, width + half :]
        folded = lifted.shape[0] // 2
        grad_up = jnp.concatenate([lifted[:folded], lifted[folded:]], axis=1)
        grad_ck, grad_cv = middle[:, :width], middle[:, width : 2 * width]
        norm_sums = middle[:, 2 * width : 2 * width + 6].T
        grad_o, grad_cq = inner_sums.item[:, :width], inner_sums.item[:, width:]
        grad_q, grad_k, grad_v = [
            late.item[:, index * width : (index + 1) * width] for index in range(3)
        ]
    else:
        norm_sums = jnp.concatenate([d_norm_one, d_norm_two, d_norm_three], axis=0)
        norm_sums = lax.psum_scatter(norm_sums, ("dp", "seq"), scatter_dimension=1, tiled=True)
        grad_down = sum_all(dot_tn(second_low, d_adapter))
        grad_up = sum_all(4.0 * dot_tn(hidden, d_branch))
        grad_co = sum_all(dot_tn(cross_mixed, d_two_low))
        grad_o = sum_all(dot_tn(mixed, d_one_low))
        grad_cq = sum_all(dot_tn(first_low, d_cq))
        grad_ck = sum_all(dot_tn(own_memory, d_ckv[0]))
        grad_cv = sum_all(dot_tn(own_memory, d_ckv[1]))
        grad_q = sum_all(dot_tn(own_inputs, d_q))
        grad_k = sum_all(dot_tn(own_inputs, d_kv[0]))
        grad_v = sum_all(dot_tn(own_inputs, d_kv[1]))
    return (
        output,
        grad_target,
        grad_source,
        grad_q,
        grad_k,
        grad_v,
        grad_o,
        grad_cq,
        grad_ck,
        grad_cv,
        grad_co,
        grad_down,
        grad_up,
        *[norm_sums[index] for index in range(6)],
    )


def solution(mesh):
    tokens = P("seq", "dp", None)
    rows = P("dp", None)
    vector = P("dp")
    both = P(("dp", "seq"), None)
    return jax.shard_map(
        body,
        mesh=mesh,
        in_specs=(tokens, tokens, vector, vector) + (rows,) * 12 + (vector,) * 6 + (tokens,),
        out_specs=(tokens,) * 3 + (both,) * 10 + (P(("dp", "seq")),) * 6,
        check_vma=False,
    )
```

```python
import functools

import jax
import jax.numpy as jnp
from jax import lax
from jax.experimental import pallas as pl
from jax.experimental.pallas import tpu as pltpu
from jax.sharding import PartitionSpec as P

HEAD = 64
PAIR = 2 * HEAD
SCALE = HEAD ** (-0.5)
MASKED_SCORE = -1e30
NEVER = 2**30
ALWAYS = 2**29
F32 = jnp.float32
BF16 = jnp.bfloat16
STRIP = 128
ROOT_HALF = 0.7071067811865476
PDF_SCALE = 0.3989422804014327


def dot(left, right):
    return jnp.dot(left, right, preferred_element_type=F32)


def dot_tn(left, right):
    return lax.dot_general(left, right, (((0,), (0,)), ((), ())), preferred_element_type=F32)


def dot_nt(left, right):
    return lax.dot_general(left, right, (((1,), (1,)), ((), ())), preferred_element_type=F32)


def gelu_pair(inputs):
    below_it = 0.5 * (1.0 + lax.erf(inputs * ROOT_HALF))
    density = PDF_SCALE * jnp.exp(-0.5 * inputs * inputs)
    return inputs * below_it, below_it + inputs * density


def norm_parts(inputs):
    centre = jnp.mean(inputs, axis=-1, keepdims=True)
    centred = inputs - centre
    spread = jnp.mean(centred * centred, axis=-1, keepdims=True)
    rstd = lax.rsqrt(spread + 1e-05)
    return centred * rstd, rstd


def norm_backward(normed, rstd, gain, grad):
    inner = grad * gain
    mean_one = jnp.mean(inner, axis=-1, keepdims=True)
    mean_two = jnp.mean(inner * normed, axis=-1, keepdims=True)
    return rstd * (inner - mean_one - normed * mean_two)


def strips(rows):
    return [slice(start, start + STRIP) for start in range(0, rows, STRIP)]


MIB = 1024 * 1024


def bytes_of(shape, kind):
    size = jnp.dtype(kind).itemsize
    for extent in shape:
        size *= extent
    return size


def in_hbm(item):
    if item.size * item.dtype.itemsize < 256 * 1024:
        return item
    return pltpu.with_memory_space_constraint(item, pltpu.HBM)


def params(blocks, scratch=0, spare=10):
    limit = 2 * sum(bytes_of(shape, kind) for shape, kind in blocks) + scratch + spare * MIB
    return pltpu.CompilerParams(vmem_limit_bytes=min(limit, 60 * MIB))


def cost(micros):
    return pl.CostEstimate(
        flops=int(micros * 1.15e9), bytes_accessed=int(micros * 3.6e6), transcendentals=0
    )


def tile_of(rows):
    return 128 if rows % 128 == 0 else rows


def key_rows(tile_end, rows, block, causal):
    if not causal:
        return rows
    return min(rows, ((tile_end - 1) // block + 1) * block)


def beside(top):
    row = lax.broadcasted_iota(jnp.int32, top.shape, 0)
    zero = jnp.zeros_like(top)
    return jnp.concatenate(
        [jnp.where(row < HEAD, top, zero), jnp.where(row < HEAD, zero, top)], axis=1
    )


def below(side):
    lane = lax.broadcasted_iota(jnp.int32, side.shape, 1)
    zero = jnp.zeros_like(side)
    return jnp.concatenate(
        [jnp.where(lane < HEAD, side, zero), jnp.where(lane < HEAD, zero, side)], axis=0
    )


def heads_back(wide, tile):
    return jnp.concatenate([wide[:HEAD, :tile], wide[HEAD:, tile:]], axis=0).T


def forward_kernel(pieces, block, causal, *refs):
    query_ref, key_pos_ref, query_pos_ref = refs[:3]
    key_refs = refs[3 : 3 + pieces]
    value_refs = refs[3 + pieces : 3 + 2 * pieces]
    out_ref, total_ref = refs[3 + 2 * pieces :]
    rows = query_ref.shape[0]
    tile = tile_of(rows)
    scaled = query_ref[...].astype(F32) * SCALE
    query_up = scaled.T.astype(BF16)
    values_up = [ref[...].astype(F32).T.astype(BF16) for ref in value_refs]
    for start in range(0, rows, tile):
        keys = key_rows(start + tile, rows, block, causal)
        wide = beside(query_up[:, start : start + tile])
        query_pos = query_pos_ref[:, start : start + tile]
        limit = jnp.concatenate([query_pos, query_pos], axis=1)
        scores = []
        for piece in range(pieces):
            score = dot(key_refs[piece][:keys, :], wide)
            allowed = key_pos_ref[piece, :keys, :] <= limit
            scores.append(jnp.where(allowed, score, MASKED_SCORE))
        highest = functools.reduce(
            jnp.maximum, [jnp.max(score, axis=0, keepdims=True) for score in scores]
        )
        summed = jnp.zeros_like(highest)
        mixed = jnp.zeros((PAIR, 2 * tile), F32)
        for piece in range(pieces):
            raised = jnp.exp(scores[piece] - highest)
            summed = summed + jnp.sum(raised, axis=0, keepdims=True)
            mixed = mixed + dot(values_up[piece][:, :keys], raised.astype(BF16))
        mixed = mixed / summed
        out_ref[start : start + tile, :] = heads_back(mixed, tile).astype(BF16)
        total = highest + jnp.log(summed)
        total_ref[0, 0:1, start : start + tile] = total[:, :tile]
        total_ref[0, 1:2, start : start + tile] = total[:, tile:]


def attend_forward(queries, keys_values, key_pos, query_pos, block, causal):
    rows, width = queries.shape
    pieces = len(keys_values)
    pairs = width // PAIR
    column = pl.BlockSpec((rows, PAIR), lambda p: (0, p))
    second = pl.BlockSpec((rows, PAIR), lambda p: (0, p + pairs))
    whole_pos = pl.BlockSpec((pieces, rows, 1), lambda p: (0, 0, 0))
    row_pos = pl.BlockSpec((1, rows), lambda p: (0, 0))
    return pl.pallas_call(
        functools.partial(forward_kernel, pieces, block, causal),
        grid=(pairs,),
        in_specs=[column, whole_pos, row_pos] + [column] * pieces + [second] * pieces,
        out_specs=[column, pl.BlockSpec((1, 2, rows), lambda p: (p, 0, 0))],
        out_shape=[
            jax.ShapeDtypeStruct((rows, width), BF16),
            jax.ShapeDtypeStruct((pairs, 2, rows), F32),
        ],
        compiler_params=params(
            [((rows, PAIR), BF16)] * (2 + 2 * pieces) + [((pieces, rows, 128), F32)],
            spare=10 + 4 * (pieces > 2),
        ),
        cost_estimate=cost(18 if causal else 22),
        name="attend_forward",
    )(queries, key_pos, query_pos, *keys_values, *keys_values)


def backward_kernel(pieces, block, causal, begun, *refs):
    refs = refs[: 6 + 2 * pieces] + refs[6 + 2 * pieces + begun :]
    query_ref, out_ref, grad_ref, total_ref, key_pos_ref, query_pos_ref = refs[:6]
    key_refs = refs[6 : 6 + pieces]
    value_refs = refs[6 + pieces : 6 + 2 * pieces]
    dquery_ref, down_ref = refs[6 + 2 * pieces : 8 + 2 * pieces]
    dother_refs = refs[8 + 2 * pieces : 7 + 3 * pieces]
    dkey_ref, dvalue_ref = refs[7 + 3 * pieces :]
    rows = query_ref.shape[0]
    tile = tile_of(rows)
    scaled = query_ref[...].astype(F32) * SCALE
    query_up = scaled.T
    scaled = scaled.astype(BF16)
    grad_up = grad_ref[...].astype(F32).T
    out_up = out_ref[...].astype(F32).T
    keys_up = [ref[...].astype(F32).T.astype(BF16) for ref in key_refs]
    product_up = grad_up * out_up
    query_up = query_up.astype(BF16)
    grad_up = grad_up.astype(BF16)
    dkey_ref[...] = jnp.zeros_like(dkey_ref)
    dvalue_ref[...] = jnp.zeros_like(dvalue_ref)
    for start in range(0, rows, tile):
        stop = start + tile
        keys = key_rows(stop, rows, block, causal)
        query_wide = beside(query_up[:, start:stop])
        grad_wide = beside(grad_up[:, start:stop])
        query_tall = below(scaled[start:stop, :])
        grad_tall = below(grad_ref[start:stop, :])
        product = product_up[:, start:stop]
        centre = jnp.concatenate(
            [
                jnp.sum(product[:HEAD], axis=0, keepdims=True),
                jnp.sum(product[HEAD:], axis=0, keepdims=True),
            ],
            axis=1,
        )
        total = jnp.concatenate(
            [total_ref[0, 0:1, start:stop], total_ref[0, 1:2, start:stop]], axis=1
        )
        query_pos = query_pos_ref[:, start:stop]
        limit = jnp.concatenate([query_pos, query_pos], axis=1)
        dquery = jnp.zeros((PAIR, 2 * tile), F32)
        for piece in range(pieces):
            score = dot(key_refs[piece][:keys, :], query_wide)
            allowed = key_pos_ref[piece, :keys, :] <= limit
            probs = jnp.exp(jnp.where(allowed, score, MASKED_SCORE) - total)
            dprob = dot(value_refs[piece][:keys, :], grad_wide)
            dscore = (probs * (dprob - centre)).astype(BF16)
            dvalue_ref[piece, :keys, :] += dot(probs.astype(BF16), grad_tall)
            dkey_ref[piece, :keys, :] += dot(dscore, query_tall)
            dquery = dquery + dot(keys_up[piece][:, :keys], dscore)
        dquery_ref[start:stop, :] = (heads_back(dquery, tile) * SCALE).astype(BF16)
    down_ref[0] = dkey_ref[0]
    down_ref[1] = dvalue_ref[0]
    for piece in range(1, pieces):
        dother_refs[piece - 1][0] = dkey_ref[piece].astype(BF16)
        dother_refs[piece - 1][1] = dvalue_ref[piece].astype(BF16)


def attend_backward(
    queries, keys_values, outputs, grads, totals, key_pos, query_pos, block, causal, span, begun=()
):
    first, pairs = span
    rows, width = queries.shape
    pieces = len(keys_values)
    shift = width // PAIR
    column = pl.BlockSpec((rows, PAIR), lambda p: (0, p + first))
    second = pl.BlockSpec((rows, PAIR), lambda p: (0, p + first + shift))
    whole_pos = pl.BlockSpec((pieces, rows, 1), lambda p: (0, 0, 0))
    row_pos = pl.BlockSpec((1, rows), lambda p: (0, 0))
    both = pl.BlockSpec((2, rows, PAIR), lambda p: (0, 0, p + first))
    held = 6 + 2 * pieces
    return pl.pallas_call(
        functools.partial(backward_kernel, pieces, block, causal, len(begun)),
        grid=(pairs,),
        in_specs=[
            column,
            column,
            column,
            pl.BlockSpec((1, 2, rows), lambda p: (p + first, 0, 0)),
            whole_pos,
            row_pos,
        ]
        + [column] * pieces
        + [second] * pieces
        + [pl.BlockSpec(memory_space=pl.ANY)] * len(begun),
        out_specs=[column, both] + [both] * (pieces - 1),
        out_shape=[
            pltpu.HBM((rows, width), BF16),
            pltpu.HBM((2, rows, width), F32),
        ]
        + [pltpu.HBM((2, rows, width), BF16)] * (pieces - 1),
        input_output_aliases={held + index: index for index in range(len(begun))},
        scratch_shapes=[pltpu.VMEM((pieces, rows, PAIR), F32)] * 2,
        compiler_params=params(
            [((rows, PAIR), BF16)] * (6 + 4 * pieces) + [((pieces, rows, 128), F32)] * 2,
            spare=10 + 4 * (pieces > 2),
        ),
        cost_estimate=cost((24 if causal else 28) * pairs * PAIR / width),
        name="attend_backward",
    )(queries, outputs, grads, totals, key_pos, query_pos, *keys_values, *keys_values, *begun)


def offset(slot, size):
    return pl.multiple_of(slot * size, size)


def row_parts(place, refs):
    if len(refs) == 1:
        return [(0, refs[0][...])]
    own, one, two, near, far = [ref[...] for ref in refs]
    near_first = jnp.concatenate([near, far], axis=0)
    far_first = jnp.concatenate([far, near], axis=0)
    diagonal = jnp.where(place[4] == 0, near_first, far_first)
    return [(place[0], own), (place[1], one), (place[2], two), (place[3], diagonal)]


def times(left_ref, place, refs):
    total = None
    for slot, part in row_parts(place, refs):
        rows = part.shape[0]
        term = dot(left_ref[:, pl.ds(offset(slot, rows), rows)], part)
        total = term if total is None else total + term
    return total


def times_up(left, place, refs, store):
    for slot, part in row_parts(place, refs):
        rows = part.shape[0]
        store(pl.ds(offset(slot, rows), rows), dot_nt(left, part))


def part_specs(arrays, columns, index):
    return [pl.BlockSpec((item.shape[0], columns), lambda *at: (0, index(*at))) for item in arrays]


def fixed(shape):
    zeros = (0,) * len(shape)
    return pl.BlockSpec(shape, lambda *at: zeros)


def view(item, columns, index):
    if item.ndim == 2:
        return (item, pl.BlockSpec((item.shape[0], columns), lambda *at: (0, index)))
    return (item, pl.BlockSpec((1, item.shape[1], columns), lambda *at: (index, 0, 0)))


def run(kernel, name, place, grid, ins, outs, micros, scratch=(), spare=10):
    kept = [bool(out[3:]) for out in outs]
    outs = [out[:3] for out in outs]
    blocks = [(spec.block_shape, item.dtype) for item, spec in ins]
    blocks += [(spec.block_shape, kind) for _, kind, spec in outs]
    held = sum(bytes_of(item.shape, item.dtype) for item in scratch)
    return pl.pallas_call(
        kernel,
        grid_spec=pltpu.PrefetchScalarGridSpec(
            num_scalar_prefetch=1,
            grid=grid,
            in_specs=[spec for _, spec in ins],
            out_specs=[spec for _, _, spec in outs],
            scratch_shapes=list(scratch),
        ),
        out_shape=[
            pltpu.HBM(shape, kind) if keep else jax.ShapeDtypeStruct(shape, kind)
            for keep, (shape, kind, _) in zip(kept, outs)
        ],
        compiler_params=params(blocks, held, spare),
        cost_estimate=cost(micros),
        name=name,
    )(place, *[in_hbm(item) for item, _ in ins])


def project_kernel(place, left_ref, *refs):
    refs[-1][...] = times(left_ref, place, refs[:-1]).astype(BF16)


def project(place, left, weight, first, count, name):
    rows, depth = left[1].block_shape
    chunk = 512
    steps = count * 1024 // chunk
    base = first * 1024 // chunk
    return run(
        project_kernel,
        name,
        place,
        (steps,),
        [left]
        + list(zip(weight, part_specs(weight, chunk, lambda j, s: base + j))),
        [((rows, count * 1024), BF16, pl.BlockSpec((rows, chunk), lambda j, s: (0, j)))],
        2.5 * count,
    )[0]


def mix_kernel(parts, both, place, mixed_ref, resid_ref, norm_ref, *refs):
    out_parts = refs[:parts]
    query_parts = refs[parts : 2 * parts] if both else ()
    outs = refs[2 * parts :] if both else refs[parts:]
    summed_ref, normed_ref, low_ref = outs[:3]
    step = pl.program_id(0)
    rows, width = summed_ref.shape
    half = width // 2

    @pl.when(step < 2)
    def _():
        columns = pl.ds(offset(step, half), half)
        summed_ref[:, columns] = resid_ref[:, columns].astype(F32) + times(
            mixed_ref, place, out_parts
        )

    @pl.when(step == 1)
    def _():
        for strip in strips(rows):
            normed, _ = norm_parts(summed_ref[strip, :])
            value = normed * norm_ref[0:1, :] + norm_ref[1:2, :]
            normed_ref[strip, :] = value
            low_ref[strip, :] = value.astype(BF16)

    if both:

        @pl.when(step >= 2)
        def _():
            outs[3][...] = times(low_ref, place, query_parts).astype(BF16)


def mix(place, mixed, resid, norm, w_out, at_out, w_query, at_query, name):
    rows, width = mixed.shape
    half = width // 2
    both = w_query is not None
    ins = [(mixed, fixed(mixed.shape)), resid, (norm, fixed(norm.shape))]
    ins += zip(
        w_out, part_specs(w_out, half, lambda j, s: at_out * 2 + jnp.minimum(j, 1))
    )
    outs = [
        ((rows, width), F32, fixed((rows, width)), True),
        ((rows, width), F32, fixed((rows, width)), True),
        ((rows, width), BF16, fixed((rows, width)), True),
    ]
    if both:
        ins += zip(
            w_query,
            part_specs(w_query, half, lambda j, s: at_query * 2 + jnp.maximum(j - 2, 0)),
        )
        outs += [
            (
                (rows, width),
                BF16,
                pl.BlockSpec((rows, half), lambda j, s: (0, jnp.maximum(j - 2, 0))),
            )
        ]
    return run(
        functools.partial(mix_kernel, len(w_out), both),
        name,
        place,
        (4 if both else 2,),
        ins,
        outs,
        6.3 if both else 4,
    )


def up_parts(place, refs, packed):
    if not packed:
        return [(0, refs[0][...])]
    unpacked = []
    for slot, part in row_parts(place, refs):
        rows = part.shape[0] // 2
        unpacked.append((slot, jnp.concatenate([part[:rows], part[rows:]], axis=1)))
    return unpacked


def chunk_of(refs, step, counts, use):
    low = 0
    for ref, count in zip(refs, counts):

        @pl.when((step >= low) & (step < low + count))
        def _(ref=ref):
            use(ref)

        low += count


def feed_specs(w_in, w_out, counts, first, chunk, width):
    in_specs = part_specs(w_in, chunk, lambda j, s: s[8 + first + j])
    shift = first if len(w_in) == 1 else 0
    out_specs, start = [], 0
    for count in counts:
        out_specs.append(
            pl.BlockSpec(
                (chunk, width),
                lambda j, s, start=start, count=count: (
                    shift + jnp.clip(j - start, 0, count - 1),
                    0,
                ),
            )
        )
        start += count
    return in_specs, out_specs


def feed_first_kernel(
    sizes, counts, packed, place, low_ref, second_ref, *refs
):
    n_in, n_out, n_down, n_up = sizes
    in_refs, refs = refs[:n_in], refs[n_in:]
    out_refs, refs = refs[:n_out], refs[n_out:]
    down_refs, refs = refs[:n_down], refs[n_down:]
    up_refs, refs = refs[:n_up], refs[n_up:]
    total_ref, slope_ref, hidden_ref, aslope_ref = refs
    step = pl.program_id(0)

    @pl.when(step == 0)
    def _():
        hidden, slope = gelu_pair(times(low_ref, place, down_refs))
        hidden_ref[...] = hidden.astype(BF16)
        aslope_ref[...] = slope.astype(BF16)
        total = None
        for slot, part in up_parts(place, up_refs, packed):
            count = part.shape[0]
            term = dot(hidden_ref[:, pl.ds(offset(slot, count), count)], part)
            total = term if total is None else total + term
        total_ref[...] = second_ref[...] + 4.0 * total

    feed_chunk(place, low_ref, in_refs, out_refs, counts, total_ref, slope_ref)


def feed_chunk(place, low_ref, in_refs, out_refs, counts, total_ref, slope_ref):
    hidden, slope = gelu_pair(times(low_ref, place, in_refs))
    slope_ref[...] = slope.astype(BF16)
    hidden = hidden.astype(BF16)

    def use(ref):
        total_ref[...] += dot(hidden, ref[...])

    chunk_of(out_refs, pl.program_id(0), counts, use)


def feed_second_kernel(
    sizes, counts, steps, place, low_ref, first_ref, grad_ref, norm_ref, *refs
):
    n_in, n_out = sizes
    in_refs, refs = refs[:n_in], refs[n_in:]
    out_refs, refs = refs[:n_out], refs[n_out:]
    final_ref, d_ref, dlow_ref, dnorm_ref, slope_ref, total_ref = refs
    step = pl.program_id(0)
    rows, width = total_ref.shape

    @pl.when(step == 0)
    def _():
        total_ref[...] = first_ref[...]

    feed_chunk(place, low_ref, in_refs, out_refs, counts, total_ref, slope_ref)

    @pl.when(step == steps - 1)
    def _():
        gain, shift = norm_ref[0:1, :], norm_ref[1:2, :]
        dgain = jnp.zeros((1, width), F32)
        dshift = jnp.zeros((1, width), F32)
        for strip in strips(rows):
            normed, rstd = norm_parts(total_ref[strip, :])
            final_ref[strip, :] = (normed * gain + shift).astype(BF16)
            grad = grad_ref[strip, :].astype(F32)
            dgain += jnp.sum(grad * normed, axis=0, keepdims=True)
            dshift += jnp.sum(grad, axis=0, keepdims=True)
            back = norm_backward(normed, rstd, gain, grad)
            d_ref[strip, :] = back
            dlow_ref[strip, :] = back.astype(BF16)
        dnorm_ref[0:1, :] = dgain
        dnorm_ref[1:2, :] = dshift


CHUNK = 512


def feed_first(place, low, second, w_in, w_out, counts, w_down, at_down, w_up, at_up):
    rows, width = low.shape
    adapter = 512
    packed = len(w_up) > 1
    steps = sum(counts)
    in_specs, out_specs = feed_specs(w_in, w_out, counts, 0, CHUNK, width)
    up_columns = 512 if packed else width
    full = fixed((rows, width))
    ins = [(low, full), (second, full)]
    ins += zip(w_in, in_specs)
    ins += zip(w_out, out_specs)
    ins += zip(w_down, part_specs(w_down, adapter, lambda j, s: at_down))
    ins += zip(w_up, part_specs(w_up, up_columns, lambda j, s: at_up))
    return run(
        functools.partial(
            feed_first_kernel, (len(w_in), len(w_out), len(w_down), len(w_up)), counts, packed
        ),
        "feed_first",
        place,
        (steps,),
        ins,
        [
            ((rows, width), F32, full),
            ((rows, steps * CHUNK), BF16, pl.BlockSpec((rows, CHUNK), lambda j, s: (0, j)), True),
            ((rows, adapter), BF16, fixed((rows, adapter)), True),
            ((rows, adapter), BF16, fixed((rows, adapter)), True),
        ],
        13,
    )


def feed_second(place, low, first, grad, norm, w_in, w_out, counts, start):
    rows, width = low.shape
    steps = sum(counts)
    in_specs, out_specs = feed_specs(w_in, w_out, counts, start, CHUNK, width)
    full = fixed((rows, width))
    ins = [(low, full), (first, full), (grad, full), (norm, fixed(norm.shape))]
    ins += zip(w_in, in_specs)
    ins += zip(w_out, out_specs)
    return run(
        functools.partial(feed_second_kernel, (len(w_in), len(w_out)), counts, steps),
        "feed_second",
        place,
        (steps,),
        ins,
        [
            ((rows, width), BF16, full, True),
            ((rows, width), F32, full),
            ((rows, width), BF16, full),
            ((2, width), F32, fixed((2, width)), True),
            ((rows, steps * CHUNK), BF16, pl.BlockSpec((rows, CHUNK), lambda j, s: (0, j)), True),
        ],
        13.5,
        scratch=[pltpu.VMEM((rows, width), F32)],
    )


def feed_backward_kernel(
    sizes,
    counts,
    packed,
    steps,
    place,
    dlow_ref,
    d_ref,
    resid_ref,
    norm_ref,
    slope_ref,
    later_ref,
    aslope_ref,
    *refs,
):
    n_in, n_out, n_down, n_up, n_mix = sizes
    in_refs, refs = refs[:n_in], refs[n_in:]
    out_refs, refs = refs[:n_out], refs[n_out:]
    down_refs, refs = refs[:n_down], refs[n_down:]
    up_refs, refs = refs[:n_up], refs[n_up:]
    mix_refs, refs = refs[:n_mix], refs[n_mix:]
    dtwo_ref, dtwo_low_ref, dnorm_ref, dadapter_ref, dmixed_ref, total_ref, dhidden_ref = refs
    step = pl.program_id(0)
    rows, width = total_ref.shape

    def add(columns, value):
        total_ref[:, columns] += value

    @pl.when(step == 0)
    def _():
        total_ref[...] = d_ref[...]
        for slot, part in up_parts(place, up_refs, packed):
            count = part.shape[0]
            columns = pl.ds(offset(slot, count), count)
            back = 4.0 * dot_nt(dlow_ref[...], part)
            dadapter_ref[:, columns] = (aslope_ref[:, columns].astype(F32) * back).astype(BF16)
        times_up(dadapter_ref[...], place, down_refs, add)

    def use(ref):
        back = dot_nt(dlow_ref[...], ref[...])
        chosen = jnp.where(step < steps // 2, slope_ref[...], later_ref[...])
        dhidden_ref[...] = (chosen.astype(F32) * back).astype(BF16)

    chunk_of(out_refs, step, counts, use)
    times_up(dhidden_ref[...], place, in_refs, add)

    @pl.when(step == steps - 1)
    def _():
        finish_norm(total_ref, resid_ref, norm_ref, dtwo_ref, dtwo_low_ref, dnorm_ref)

        def keep(columns, value):
            dmixed_ref[:, columns] = value.astype(BF16)

        times_up(dtwo_low_ref[...], place, mix_refs, keep)


def finish_norm(grad_ref, resid_ref, norm_ref, d_ref, dlow_ref, dnorm_ref):
    rows, width = grad_ref.shape
    gain = norm_ref[0:1, :]
    dgain = jnp.zeros((1, width), F32)
    dshift = jnp.zeros((1, width), F32)
    for strip in strips(rows):
        grad = grad_ref[strip, :]
        normed, rstd = norm_parts(resid_ref[strip, :])
        dgain += jnp.sum(grad * normed, axis=0, keepdims=True)
        dshift += jnp.sum(grad, axis=0, keepdims=True)
        back = norm_backward(normed, rstd, gain, grad)
        d_ref[strip, :] = back
        dlow_ref[strip, :] = back.astype(BF16)
    dnorm_ref[0:1, :] = dgain
    dnorm_ref[1:2, :] = dshift


def feed_backward(
    place,
    dlow,
    d_three,
    resid,
    norm,
    slope,
    later,
    aslope,
    w_in,
    w_out,
    counts,
    w_down,
    at_down,
    w_up,
    at_up,
    w_mix,
    at_mix,
):
    rows, width = dlow.shape
    hidden = w_in[0].shape[1]
    adapter = 512
    packed = len(w_up) > 1
    chunk = CHUNK
    steps = hidden // chunk
    in_specs, out_specs = feed_specs(w_in, w_out, counts, 0, chunk, width)
    middle = steps // 2
    up_columns = 512 if packed else width
    full = fixed((rows, width))
    ins = [
        (dlow, full),
        (d_three, full),
        (resid, full),
        (norm, fixed(norm.shape)),
        (slope, pl.BlockSpec((rows, chunk), lambda j, s: (0, jnp.minimum(j, middle - 1)))),
        (later, pl.BlockSpec((rows, chunk), lambda j, s: (0, jnp.maximum(j - middle, 0)))),
        (aslope, fixed((rows, adapter))),
    ]
    ins += zip(w_in, in_specs)
    ins += zip(w_out, out_specs)
    ins += zip(w_down, part_specs(w_down, adapter, lambda j, s: at_down))
    ins += zip(w_up, part_specs(w_up, up_columns, lambda j, s: at_up))
    ins += zip(w_mix, part_specs(w_mix, width, lambda j, s: at_mix))
    return run(
        functools.partial(
            feed_backward_kernel,
            (len(w_in), len(w_out), len(w_down), len(w_up), len(w_mix)),
            counts,
            packed,
            steps,
        ),
        "feed_backward",
        place,
        (steps,),
        ins,
        [
            ((rows, width), F32, full, True),
            ((rows, width), BF16, full),
            ((2, width), F32, fixed((2, width)), True),
            ((rows, adapter), BF16, fixed((rows, adapter))),
            ((rows, width), BF16, full),
        ],
        29,
        scratch=[pltpu.VMEM((rows, width), F32), pltpu.VMEM((rows, chunk), BF16)],
    )


def norm_step_kernel(parts, place, dquery_ref, d_ref, resid_ref, norm_ref, *refs):
    query_refs, refs = refs[:parts], refs[parts:]
    out_refs, refs = refs[:parts], refs[parts:]
    done_ref, done_low_ref, dnorm_ref, dmixed_ref, total_ref = refs
    step = pl.program_id(0)

    @pl.when(step == 0)
    def _():
        def add(columns, value):
            total_ref[:, columns] = d_ref[:, columns] + value

        times_up(dquery_ref[...], place, query_refs, add)
        finish_norm(total_ref, resid_ref, norm_ref, done_ref, done_low_ref, dnorm_ref)

    @pl.when(step == 1)
    def _():
        def keep(columns, value):
            dmixed_ref[:, columns] = value.astype(BF16)

        times_up(done_low_ref[...], place, out_refs, keep)


def norm_step(place, dquery, d_two, resid, norm, w_query, at_query, w_out, at_out):
    rows, width = dquery.shape
    full = fixed((rows, width))
    ins = [(dquery, full), (d_two, full), (resid, full), (norm, fixed(norm.shape))]
    ins += zip(w_query, part_specs(w_query, width, lambda j, s: at_query))
    ins += zip(w_out, part_specs(w_out, width, lambda j, s: at_out))
    return run(
        functools.partial(norm_step_kernel, len(w_query)),
        "norm_step",
        place,
        (2,),
        ins,
        [
            ((rows, width), F32, full, True),
            ((rows, width), BF16, full),
            ((2, width), F32, fixed((2, width)), True),
            ((rows, width), BF16, full),
        ],
        6.6,
        scratch=[pltpu.VMEM((rows, width), F32)],
    )


def inputs_back_kernel(lefts, parts, extra, place, *refs):
    left_refs, refs = refs[:lefts], refs[lefts:]
    part_refs, refs = refs[:parts], refs[parts:]
    if extra:
        extra_ref, refs = refs[0], refs[1:]
    out_ref, total_ref = refs
    step = pl.program_id(0)
    width = total_ref.shape[1]

    @pl.when(step == 0)
    def _():
        if extra == "base":
            total_ref[...] = extra_ref[...]
        else:
            total_ref[...] = jnp.zeros_like(total_ref)
        if extra == "beside":
            out_ref[:, :width] = extra_ref[...]

    def add(columns, value):
        total_ref[:, columns] += value

    for which in range(lefts):

        @pl.when(step == which)
        def _(which=which):
            left = left_refs[which][...]
            times_up(left.reshape(left.shape[-2:]), place, part_refs, add)

    @pl.when(step == lefts - 1)
    def _():
        out_ref[:, out_ref.shape[1] - width :] = total_ref[...].astype(BF16)


def inputs_back(place, lefts, weight, blocks, extra, item, name):
    depth = lefts[0][1].block_shape[-1]
    rows = lefts[0][1].block_shape[-2]
    width = 1024
    first = blocks[0]
    strides = {blocks[k + 1] - blocks[k] for k in range(len(blocks) - 1)}

    def at(j, s):
        index = first
        for k in range(1, len(blocks)):
            index = jnp.where(j == k, blocks[k], index)
        return first + j if strides == {1} else index

    ins = list(lefts)
    ins += zip(weight, part_specs(weight, depth, at))
    if extra:
        ins += [(item, fixed((rows, width)))]
    size = 2 * width if extra == "beside" else width
    return run(
        functools.partial(inputs_back_kernel, len(lefts), len(weight), extra),
        name,
        place,
        (len(lefts),),
        ins,
        [((rows, size), BF16, fixed((rows, size)))],
        3 * len(lefts) * depth / width,
        scratch=[pltpu.VMEM((rows, width), F32)],
    )[0]


def laid_out_kernel(slots, item_ref, *refs):
    out_ref = refs[-1]
    out_ref[slots[0]] = item_ref[0]
    for index, ref in enumerate(refs[:-1], 1):
        out_ref[slots[index]] = ref[...]


def laid_out(slots, item, parts):
    part = parts[0].shape
    return run(
        laid_out_kernel,
        "laid_out",
        slots,
        (1,),
        [(item, pl.BlockSpec((1,) + part, lambda j, s: (s[0], 0, 0)))]
        + [(piece, fixed(part)) for piece in parts],
        [(item.shape, item.dtype, fixed(item.shape))],
        1.5,
    )[0]


def swap_pairs(size, bit):
    return [(index, index ^ bit) for index in range(size)]


def by_core(even, odd):
    return [
        (d * 8 + s, (d ^ (odd if s % 2 else even)) * 8 + s) for d in range(4) for s in range(8)
    ]


def after(item, *others):
    return lax.optimization_barrier((item,) + others)[0]


def gather_first(own):
    return (own, lax.ppermute(own, ("dp", "seq"), by_core(1, 2)))


def gather_swap(parts, *others):
    return parts + (lax.ppermute(after(parts[1], *others), "seq", swap_pairs(8, 1)),)


def gather_near(parts, core, *others):
    one = parts[1]
    half = one.shape[0] // 2
    half_one = lax.dynamic_slice_in_dim(after(one, *others), core * half, half, 0)
    return parts + (lax.ppermute(half_one, ("dp", "seq"), by_core(2, 1)),)


def gather_far(parts, *others):
    return parts + (lax.ppermute(after(parts[3], *others), "seq", swap_pairs(8, 1)),)


def gather_dp(item):
    return (lax.all_gather(item, "dp", axis=0, tiled=True),)


def row_blocks(value, size):
    return [value[start : start + size] for start in range(0, value.shape[0], size)]


def wgrad_kernel(fresh, split, scales, extra, place, *refs):
    count = len(fresh)
    left_refs, right_refs = refs[:count], refs[count : 2 * count]
    outs, up_ref = refs[2 * count + extra : -1], refs[-1]
    step = pl.program_id(0)
    wide = outs[0].shape[1]
    if extra:

        @pl.when(step == count)
        def _():
            rows = jnp.concatenate([ref[...] for ref in refs[2 * count : 2 * count + extra]])
            filler = jnp.zeros((128 - rows.shape[0], rows.shape[1]), F32)
            columns = jnp.concatenate([rows, filler], axis=0).T.astype(BF16)
            blocks = row_blocks(columns, 32)
            even = jnp.concatenate(blocks[0::2], axis=0)
            odd = jnp.concatenate(blocks[1::2], axis=0)
            outs[0][:, :128] = jnp.where(place[4] == 0, odd, even)
            outs[1][:, :128] = jnp.where(place[4] == 0, even, odd)
            for out in outs:
                out[:, 128:256] = jnp.zeros(even.shape, BF16)

    for which in range(count):

        @pl.when(step == which)
        def _(which=which):
            right = right_refs[which][...]
            right = right.reshape(right.shape[-2:])
            tall = left_refs[which].shape[-1]
            if fresh[which]:
                left = left_refs[which][...]
                up_ref[:tall, :] = left.reshape(left.shape[-2:]).T
            value = dot(up_ref[:tall, :], right)
            value = (value * scales[which] if scales[which] != 1.0 else value).astype(BF16)
            own = tall // 32
            blocks = row_blocks(value, own)
            if split:
                even = jnp.concatenate(blocks[0::2], axis=0)
                odd = jnp.concatenate(blocks[1::2], axis=0)
                outs[0][...] = jnp.where(place[4] == 0, odd, even)
                outs[1][...] = jnp.where(place[4] == 0, even, odd)
                return
            folds = right.shape[1] // wide
            for index, item in enumerate(blocks):
                at = (index % 8 * 4 + index // 8) * own * folds
                for fold in range(folds):
                    low = at + fold * own
                    outs[0][low : low + own, :] = item[:, fold * wide : (fold + 1) * wide]


def wgrad(place, lefts, rights, wide, split, scales, name, extra=()):
    fresh = []
    for index, (item, spec) in enumerate(lefts):
        before = lefts[index - 1] if index else (None, None)
        fresh.append(item is not before[0] or spec is not before[1])
    rows, tall = lefts[0][1].block_shape[-2:]
    high = tall // 2 if split else tall
    spec = pl.BlockSpec((high, wide), lambda j, s: (0, j))
    more = 1 if extra else 0
    return run(
        functools.partial(wgrad_kernel, tuple(fresh), split, scales, len(extra)),
        name,
        place,
        (len(lefts) + more,),
        list(lefts) + list(rights) + [(item, fixed(item.shape)) for item in extra],
        [((high, wide * len(lefts) + 256 * more), BF16, spec, True)] * (2 if split else 1),
        1.6 * len(lefts) * wide / 1024,
        scratch=[pltpu.VMEM((tall, rows), BF16)],
    )


def take(item, index, axis):
    return lax.dynamic_index_in_dim(item, index, axis, keepdims=False)


def add(kept, received, kind=BF16):
    return (kept.astype(F32) + received.astype(F32)).astype(kind)


def sum_over(partial, name):
    return lax.psum_scatter(partial, name, scatter_dimension=0, tiled=True)


class Scatter:
    def __init__(self, send, keep):
        here, there = lax.axis_index("dp"), lax.axis_index("seq")
        self.x, self.y = here % 2, here // 2
        self.low, self.high = (there // 2) % 2, there // 4
        self.send, self.keep = send, keep
        self.width = keep.shape[1]

    def core(self):
        received = lax.ppermute(self.send, "seq", swap_pairs(8, 1))
        item = add(self.keep, received).reshape(2, 2, 128, self.width)
        self.one, self.two = item[..., : self.width // 2], item[..., self.width // 2 :]
        return self.one

    def plane_one(self):
        x, y = self.x, self.y
        from_x = lax.ppermute(take(self.one, 1 - x, 1), "dp", swap_pairs(4, 1))
        from_y = lax.ppermute(take(self.two, 1 - y, 0), "dp", swap_pairs(4, 2))
        self.one = add(take(self.one, x, 1), from_x)
        self.two = add(take(self.two, y, 0), from_y)
        return self.one

    def plane_two(self):
        x, y = self.x, self.y
        from_y = lax.ppermute(take(self.one, 1 - y, 0), "dp", swap_pairs(4, 2))
        from_x = lax.ppermute(take(self.two, 1 - x, 0), "dp", swap_pairs(4, 1))
        one = add(take(self.one, y, 0), from_y)
        two = add(take(self.two, x, 0), from_x)
        self.item = jnp.concatenate([one, two], axis=1)
        return self.item

    def z_one(self):
        self.item = self.item.reshape(2, 2, 32, self.width)
        received = lax.ppermute(take(self.item, 1 - self.low, 1), "seq", swap_pairs(8, 2))
        self.item = add(take(self.item, self.low, 1), received)
        return self.item

    def z_two(self):
        received = lax.ppermute(take(self.item, 1 - self.high, 0), "seq", swap_pairs(8, 4))
        self.item = add(take(self.item, self.high, 0), received, F32)
        return self.item


def sum_all(partial):
    return lax.psum_scatter(
        partial.astype(BF16), ("dp", "seq"), scatter_dimension=0, tiled=True
    ).astype(F32)


def body(
    target,
    source,
    target_len,
    source_len,
    self_query,
    self_key,
    self_value,
    self_output,
    cross_query,
    cross_key,
    cross_value,
    cross_output,
    feed_in,
    feed_out,
    adapter_down,
    adapter_up,
    self_gain,
    self_shift,
    cross_gain,
    cross_shift,
    final_gain,
    final_shift,
    cotangent,
):
    block, seqs, width = target.shape
    dp, seq = lax.axis_size("dp"), lax.axis_size("seq")
    group = seq // seqs
    rows = seqs * block
    here, there = lax.axis_index("dp"), lax.axis_index("seq")
    inner, which = there % group, there // group
    core = there % 2
    halving = dp == 4 and seq == 8
    apart = [[start + group * step for step in range(seqs)] for start in range(group)]

    def to_sequence(item):
        return lax.all_to_all(
            item.swapaxes(0, 1), "seq", 0, 0, axis_index_groups=apart, tiled=True
        ).reshape(rows, item.shape[-1])

    slots = jnp.stack([which ^ bit for bit in range(seqs)]).astype(jnp.int32)

    def send_back(item):
        item = item.reshape(seqs, block, item.shape[-1])
        parts = [item]
        for bit in range(1, seqs):
            pairs = [(index, (index // group ^ bit) * group + index % group) for index in range(seq)]
            parts.append(lax.ppermute(take(item, which ^ bit, 0), "seq", pairs))
        return parts

    def set_down(parts, *others):
        item, *parts = lax.optimization_barrier((*parts, *others))[: len(parts)]
        return laid_out(slots, item, parts).swapaxes(0, 1)

    def near(shift):
        return [
            (k * group + c, k * group + (c + shift) % group)
            for k in range(seqs)
            for c in range(group)
        ]

    def spread(item):
        return [item] + [lax.ppermute(item, "seq", near(-s)) for s in range(1, group)]

    def collect(own, others):
        for shift, other in enumerate(others, 1):
            own = own + lax.ppermute(other, "seq", near(shift)).astype(F32)
        return own.astype(BF16)

    own_inputs, own_memory = to_sequence(target), to_sequence(source)
    inputs, memory = view(own_inputs, width, 0), view(own_memory, width, 0)
    grad_out = to_sequence(cotangent)
    vectors = jnp.stack([self_gain, self_shift, cross_gain, cross_shift, final_gain, final_shift])
    if halving:
        one = jnp.where(core == 0, here ^ 1, here ^ 2)
        two = jnp.where(core == 0, here ^ 2, here ^ 1)
        diagonal = here ^ 3
        chunks = [item * 2 + part for item in (here, one, two) for part in (0, 1)]
        chunks += [diagonal * 2 + core, diagonal * 2 + 1 - core]
        place = jnp.stack([here, one, two, diagonal, core, core, core, core] + chunks)
        first_group = jnp.concatenate(
            [self_query, self_key, self_value, cross_key, cross_value], axis=1
        )
        half = width // 2
        up_packed = jnp.concatenate([adapter_up[:, :half], adapter_up[:, half:]], axis=0)
        second_group = jnp.concatenate(
            [self_output, cross_query, cross_output, adapter_down, up_packed], axis=1
        )
        vector_parts = [vectors] + [
            lax.ppermute(vectors, "dp", swap_pairs(4, bit)) for bit in (1, 2, 3)
        ]
        w_self = gather_swap(gather_first(first_group))
        w_self = gather_far(
            gather_near(w_self, core, own_inputs, second_group, *vector_parts)
        )
        w_mid = gather_swap(gather_first(after(second_group, w_self[3])))
        w_in = gather_first(after(feed_in, w_mid[1]))
        at_q, at_kv, at_ckv = (w_self, 0), (w_self, 1), (w_self, 3)
        parts = jnp.stack(vector_parts)
        vectors = jnp.concatenate([take(parts, here ^ slot, 0) for slot in range(4)], axis=1)
        counts_first, counts_second = (2, 2), (2, 1, 1)
    else:
        steps = feed_in.shape[1] // CHUNK
        place = jnp.stack([jnp.int32(0)] * 8 + [jnp.int32(j) for j in range(steps)])
        at_q = (gather_dp(self_query), 0)
        at_kv = (gather_dp(jnp.concatenate([self_key, self_value], axis=1)), 0)
        at_o, at_cq = (gather_dp(self_output), 0), (gather_dp(cross_query), 0)
        at_ckv = (gather_dp(jnp.concatenate([cross_key, cross_value], axis=1)), 0)
        at_co = (gather_dp(cross_output), 0)
        w_in, w_out = gather_dp(feed_in), gather_dp(feed_out)
        at_down, at_up = (gather_dp(adapter_down), 0), (gather_dp(adapter_up), 0)
        vectors = lax.all_gather(vectors, "dp", axis=1, tiled=True)
        out_first = out_second = w_out
        counts_first, counts_second = (steps // 2,), (steps - steps // 2,)
    place = place.astype(jnp.int32)
    vectors = vectors.astype(F32)
    norm_one, norm_two, norm_three = vectors[0:2], vectors[2:4], vectors[4:6]

    local = jnp.arange(rows, dtype=jnp.int32)

    def positions(place_in_group):
        return (local // block * group + place_in_group) * block + local % block

    target_limit = take(target_len, which, 0)
    source_limit = take(source_len, which, 0)
    key_pos = jnp.stack([positions((inner + shift) % group) for shift in range(group)])
    self_keys = jnp.where(key_pos < target_limit, key_pos, NEVER)[..., None]
    cross_keys = jnp.where(key_pos < source_limit, key_pos, NEVER)[..., None]
    self_rows = positions(inner)[None]
    cross_rows = jnp.full((1, rows), ALWAYS, jnp.int32)

    kv_own = project(place, inputs, *at_kv, 2, "self_kv")
    kv_all = spread(kv_own)
    queries = project(place, inputs, *at_q, 1, "self_q")
    if halving:
        w_mid = gather_near(w_mid, core, queries)
        queries = after(queries, w_mid[1])
    mixed, totals = attend_forward(queries, kv_all, self_keys, self_rows, block, True)
    ckv_own = project(
        place, (after(own_memory, mixed), memory[1]), *at_ckv, 2, "cross_kv"
    )
    ckv_all = spread(ckv_own)
    mixed = after(mixed, ckv_own)
    if halving:
        w_mid = gather_far(w_mid, mixed)
        w_out = gather_first(after(feed_out, mixed))
        mixed = after(mixed, w_in[1])
        at_o, at_cq, at_co = (w_mid, 0), (w_mid, 1), (w_mid, 2)
        at_down, at_up = (w_mid, 6), (w_mid, 7)
    resid_one, first, first_low, cross_q = mix(
        place, mixed, inputs, norm_one, *at_o, *at_cq, "mix_self"
    )
    if halving:
        w_in = gather_near(gather_swap(w_in, cross_q), core, cross_q)
    cross_mixed, cross_totals = attend_forward(
        cross_q, ckv_all, cross_keys, cross_rows, block, False
    )
    if halving:
        w_in = gather_far(w_in, cross_mixed)
        w_out = gather_far(gather_near(gather_swap(w_out, cross_mixed), core, cross_mixed))
        out_first, out_second = w_out[:2], w_out[2:]
    resid_two, second, second_low = mix(
        place, cross_mixed, view(first, width, 0), norm_two, *at_co, None, None, "mix_cross"
    )
    partial, slope, hidden, adapter_slope = feed_first(
        place, second_low, second, w_in, out_first, counts_first, *at_down, *at_up
    )
    final, d_three, d_branch, d_norm_three, later = feed_second(
        place,
        second_low,
        partial,
        grad_out,
        norm_three,
        w_in,
        out_second,
        counts_second,
        sum(counts_first),
    )
    output = send_back(final)

    d_two, d_two_low, d_norm_two, d_adapter, d_cross = feed_backward(
        place,
        d_branch,
        d_three,
        resid_two,
        norm_two,
        slope,
        later,
        adapter_slope,
        w_in,
        w_out,
        counts_first + counts_second if halving else (steps,),
        *at_down,
        *at_up,
        *at_co,
    )

    d_two_low = after(d_two_low, *output[1:])

    def whole(item, layer=0):
        return view(item, item.shape[-1], layer)

    pairs = width // PAIR
    if halving:
        half = width // 2
        left = whole(cross_mixed)
        early = wgrad(
            place,
            [left, left, whole(second_low), whole(hidden)],
            [view(d_two_low, half, 0), view(d_two_low, half, 1), whole(d_adapter), whole(d_branch)],
            half,
            False,
            (1.0, 1.0, 1.0, 4.0),
            "wgrad_early",
        )[0]
        d_cross = after(d_cross, early)
        early = sum_over(early, "seq")
    d_cq, *d_ckv = attend_backward(
        cross_q,
        ckv_all,
        cross_mixed,
        d_cross,
        cross_totals,
        cross_keys,
        cross_rows,
        block,
        False,
        (0, pairs),
    )
    output = set_down(output, d_cq)
    d_one, d_one_low, d_norm_one, d_mixed = norm_step(
        place, d_cq, d_two, resid_one, norm_one, *at_cq, *at_o
    )
    d_ckv = collect(after(d_ckv[0], d_one_low), d_ckv[1:])
    grad_source = inputs_back(
        place,
        [whole(d_ckv, 0), whole(d_ckv, 1)],
        at_ckv[0],
        [at_ckv[1], at_ckv[1] + 1],
        None,
        None,
        "source_back",
    )
    d_ckv = after(d_ckv, grad_source)
    grad_source = send_back(grad_source)
    if halving:
        d_one_low = after(d_one_low, early)
        early = sum_over(early, "dp").astype(F32)
        inner_sums = Scatter(
            *wgrad(
                place,
                [memory, memory, whole(mixed), whole(first_low)],
                [whole(d_ckv, 0), whole(d_ckv, 1), whole(d_one_low), whole(d_cq)],
                width,
                True,
                (1.0,) * 4,
                "wgrad_inner",
                [d_norm_one, d_norm_two, d_norm_three],
            )
        )
    if halving:
        d_mixed = after(d_mixed, inner_sums.core())
    else:
        d_mixed = after(d_mixed, grad_source[0])

    begun = ()
    split = pairs * 3 // 4
    for span in ((0, split), (split, pairs - split)):
        begun = attend_backward(
            queries,
            kv_all,
            mixed,
            d_mixed,
            totals,
            self_keys,
            self_rows,
            block,
            True,
            span,
            begun,
        )
        if halving and span[0] == 0:
            d_mixed = after(d_mixed, begun[0], inner_sums.plane_one(), *grad_source[1:3])
    d_q, *d_kv = begun
    d_kv = collect(d_kv[0], d_kv[1:])
    at_self = at_q if halving else ((jnp.concatenate([at_q[0][0], at_kv[0][0]], axis=1),), 0)
    grad_target = inputs_back(
        place,
        [whole(d_q), whole(d_kv, 0), whole(d_kv, 1)],
        at_self[0],
        [at_self[1] + index for index in range(3)],
        "base",
        d_one,
        "target_back",
    )
    d_q = after(d_q, grad_target)
    grad_target = send_back(grad_target)
    if not halving:
        grad_source = set_down(grad_source)
        grad_target = set_down(grad_target)
    if halving:
        d_q = after(d_q, inner_sums.plane_two())
        late = Scatter(
            *wgrad(
                place,
                [inputs] * 3,
                [whole(d_q), whole(d_kv, 0), whole(d_kv, 1)],
                width,
                True,
                (1.0,) * 3,
                "wgrad_self",
            )
        )
        grad_source = set_down(grad_source, late.send)
        late.keep = after(late.keep, inner_sums.z_one(), grad_source, grad_target[1])
        late.core()
        late.plane_one()
        late.one, late.two, *_ = lax.optimization_barrier(
            (late.one, late.two, inner_sums.z_two(), *grad_target)
        )
        grad_target = set_down(grad_target, late.one)
        late.plane_two()
        late.item = after(late.item, grad_target)
        late.z_one()
        late.z_two()
        grad_co, grad_down = early[:, :width], early[:, width : width + half]
        lifted = early[:, width + half :]
        folded = lifted.shape[0] // 2
        grad_up = jnp.concatenate([lifted[:folded], lifted[folded:]], axis=1)
        norm_sums = inner_sums.item[:, 4 * width : 4 * width + 6].T
        grad_ck, grad_cv, grad_o, grad_cq = [
            inner_sums.item[:, index * width : (index + 1) * width] for index in range(4)
        ]
        grad_q, grad_k, grad_v = [
            late.item[:, index * width : (index + 1) * width] for index in range(3)
        ]
    else:
        norm_sums = jnp.concatenate([d_norm_one, d_norm_two, d_norm_three], axis=0)
        norm_sums = lax.psum_scatter(norm_sums, ("dp", "seq"), scatter_dimension=1, tiled=True)
        grad_down = sum_all(dot_tn(second_low, d_adapter))
        grad_up = sum_all(4.0 * dot_tn(hidden, d_branch))
        grad_co = sum_all(dot_tn(cross_mixed, d_two_low))
        grad_o = sum_all(dot_tn(mixed, d_one_low))
        grad_cq = sum_all(dot_tn(first_low, d_cq))
        grad_ck = sum_all(dot_tn(own_memory, d_ckv[0]))
        grad_cv = sum_all(dot_tn(own_memory, d_ckv[1]))
        grad_q = sum_all(dot_tn(own_inputs, d_q))
        grad_k = sum_all(dot_tn(own_inputs, d_kv[0]))
        grad_v = sum_all(dot_tn(own_inputs, d_kv[1]))
    return (
        output,
        grad_target,
        grad_source,
        grad_q,
        grad_k,
        grad_v,
        grad_o,
        grad_cq,
        grad_ck,
        grad_cv,
        grad_co,
        grad_down,
        grad_up,
        *[norm_sums[index] for index in range(6)],
    )


def solution(mesh):
    tokens = P("seq", "dp", None)
    rows = P("dp", None)
    vector = P("dp")
    both = P(("dp", "seq"), None)
    return jax.shard_map(
        body,
        mesh=mesh,
        in_specs=(tokens, tokens, vector, vector) + (rows,) * 12 + (vector,) * 6 + (tokens,),
        out_specs=(tokens,) * 3 + (both,) * 10 + (P(("dp", "seq")),) * 6,
        check_vma=False,
    )
```

```python
import functools

import jax
import jax.numpy as jnp
from jax import lax
from jax.experimental import pallas as pl
from jax.experimental.pallas import tpu as pltpu
from jax.sharding import PartitionSpec as P

HEAD = 64
PAIR = 2 * HEAD
SCALE = HEAD ** (-0.5)
MASKED_SCORE = -1e30
NEVER = 2**30
ALWAYS = 2**29
F32 = jnp.float32
BF16 = jnp.bfloat16
STRIP = 128
ROOT_HALF = 0.7071067811865476
PDF_SCALE = 0.3989422804014327


def dot(left, right):
    return jnp.dot(left, right, preferred_element_type=F32)


def dot_tn(left, right):
    return lax.dot_general(left, right, (((0,), (0,)), ((), ())), preferred_element_type=F32)


def dot_nt(left, right):
    return lax.dot_general(left, right, (((1,), (1,)), ((), ())), preferred_element_type=F32)


def gelu_pair(inputs):
    below_it = 0.5 * (1.0 + lax.erf(inputs * ROOT_HALF))
    density = PDF_SCALE * jnp.exp(-0.5 * inputs * inputs)
    return inputs * below_it, below_it + inputs * density


def norm_parts(inputs):
    centre = jnp.mean(inputs, axis=-1, keepdims=True)
    centred = inputs - centre
    spread = jnp.mean(centred * centred, axis=-1, keepdims=True)
    rstd = lax.rsqrt(spread + 1e-05)
    return centred * rstd, rstd


def norm_backward(normed, rstd, gain, grad):
    inner = grad * gain
    mean_one = jnp.mean(inner, axis=-1, keepdims=True)
    mean_two = jnp.mean(inner * normed, axis=-1, keepdims=True)
    return rstd * (inner - mean_one - normed * mean_two)


def strips(rows):
    return [slice(start, start + STRIP) for start in range(0, rows, STRIP)]


MIB = 1024 * 1024


def bytes_of(shape, kind):
    size = jnp.dtype(kind).itemsize
    for extent in shape:
        size *= extent
    return size


def in_hbm(item):
    if item.size * item.dtype.itemsize < 256 * 1024:
        return item
    return pltpu.with_memory_space_constraint(item, pltpu.HBM)


def params(blocks, scratch=0, spare=10):
    limit = 2 * sum(bytes_of(shape, kind) for shape, kind in blocks) + scratch + spare * MIB
    return pltpu.CompilerParams(vmem_limit_bytes=min(limit, 60 * MIB))


def cost(micros):
    return pl.CostEstimate(
        flops=int(micros * 1.15e9), bytes_accessed=int(micros * 3.6e6), transcendentals=0
    )


def tile_of(rows):
    return 128 if rows % 128 == 0 else rows


def key_rows(tile_end, rows, block, causal):
    if not causal:
        return rows
    return min(rows, ((tile_end - 1) // block + 1) * block)


def beside(top):
    row = lax.broadcasted_iota(jnp.int32, top.shape, 0)
    zero = jnp.zeros_like(top)
    return jnp.concatenate(
        [jnp.where(row < HEAD, top, zero), jnp.where(row < HEAD, zero, top)], axis=1
    )


def below(side):
    lane = lax.broadcasted_iota(jnp.int32, side.shape, 1)
    zero = jnp.zeros_like(side)
    return jnp.concatenate(
        [jnp.where(lane < HEAD, side, zero), jnp.where(lane < HEAD, zero, side)], axis=0
    )


def heads_back(wide, tile):
    return jnp.concatenate([wide[:HEAD, :tile], wide[HEAD:, tile:]], axis=0).T


def forward_kernel(pieces, block, causal, *refs):
    query_ref, key_pos_ref, query_pos_ref = refs[:3]
    key_refs = refs[3 : 3 + pieces]
    value_refs = refs[3 + pieces : 3 + 2 * pieces]
    out_ref, total_ref = refs[3 + 2 * pieces :]
    rows = query_ref.shape[0]
    tile = tile_of(rows)
    scaled = query_ref[...].astype(F32) * SCALE
    query_up = scaled.T.astype(BF16)
    values_up = [ref[...].astype(F32).T.astype(BF16) for ref in value_refs]
    for start in range(0, rows, tile):
        keys = key_rows(start + tile, rows, block, causal)
        wide = beside(query_up[:, start : start + tile])
        query_pos = query_pos_ref[:, start : start + tile]
        limit = jnp.concatenate([query_pos, query_pos], axis=1)
        scores = []
        for piece in range(pieces):
            score = dot(key_refs[piece][:keys, :], wide)
            allowed = key_pos_ref[piece, :keys, :] <= limit
            scores.append(jnp.where(allowed, score, MASKED_SCORE))
        highest = functools.reduce(
            jnp.maximum, [jnp.max(score, axis=0, keepdims=True) for score in scores]
        )
        summed = jnp.zeros_like(highest)
        mixed = jnp.zeros((PAIR, 2 * tile), F32)
        for piece in range(pieces):
            raised = jnp.exp(scores[piece] - highest)
            summed = summed + jnp.sum(raised, axis=0, keepdims=True)
            mixed = mixed + dot(values_up[piece][:, :keys], raised.astype(BF16))
        mixed = mixed / summed
        out_ref[start : start + tile, :] = heads_back(mixed, tile).astype(BF16)
        total = highest + jnp.log(summed)
        total_ref[0, 0:1, start : start + tile] = total[:, :tile]
        total_ref[0, 1:2, start : start + tile] = total[:, tile:]


def attend_forward(queries, keys_values, key_pos, query_pos, block, causal):
    rows, width = queries.shape
    pieces = len(keys_values)
    pairs = width // PAIR
    column = pl.BlockSpec((rows, PAIR), lambda p: (0, p))
    second = pl.BlockSpec((rows, PAIR), lambda p: (0, p + pairs))
    whole_pos = pl.BlockSpec((pieces, rows, 1), lambda p: (0, 0, 0))
    row_pos = pl.BlockSpec((1, rows), lambda p: (0, 0))
    return pl.pallas_call(
        functools.partial(forward_kernel, pieces, block, causal),
        grid=(pairs,),
        in_specs=[column, whole_pos, row_pos] + [column] * pieces + [second] * pieces,
        out_specs=[column, pl.BlockSpec((1, 2, rows), lambda p: (p, 0, 0))],
        out_shape=[
            jax.ShapeDtypeStruct((rows, width), BF16),
            jax.ShapeDtypeStruct((pairs, 2, rows), F32),
        ],
        compiler_params=params(
            [((rows, PAIR), BF16)] * (2 + 2 * pieces) + [((pieces, rows, 128), F32)],
            spare=10 + 4 * (pieces > 2),
        ),
        cost_estimate=cost(18 if causal else 22),
        name="attend_forward",
    )(queries, key_pos, query_pos, *keys_values, *keys_values)


def backward_kernel(pieces, block, causal, begun, *refs):
    refs = refs[: 6 + 2 * pieces] + refs[6 + 2 * pieces + begun :]
    query_ref, out_ref, grad_ref, total_ref, key_pos_ref, query_pos_ref = refs[:6]
    key_refs = refs[6 : 6 + pieces]
    value_refs = refs[6 + pieces : 6 + 2 * pieces]
    dquery_ref, down_ref = refs[6 + 2 * pieces : 8 + 2 * pieces]
    dother_refs = refs[8 + 2 * pieces : 7 + 3 * pieces]
    dkey_ref, dvalue_ref = refs[7 + 3 * pieces :]
    rows = query_ref.shape[0]
    tile = tile_of(rows)
    scaled = query_ref[...].astype(F32) * SCALE
    query_up = scaled.T
    scaled = scaled.astype(BF16)
    grad_up = grad_ref[...].astype(F32).T
    out_up = out_ref[...].astype(F32).T
    keys_up = [ref[...].astype(F32).T.astype(BF16) for ref in key_refs]
    product_up = grad_up * out_up
    query_up = query_up.astype(BF16)
    grad_up = grad_up.astype(BF16)
    dkey_ref[...] = jnp.zeros_like(dkey_ref)
    dvalue_ref[...] = jnp.zeros_like(dvalue_ref)
    for start in range(0, rows, tile):
        stop = start + tile
        keys = key_rows(stop, rows, block, causal)
        query_wide = beside(query_up[:, start:stop])
        grad_wide = beside(grad_up[:, start:stop])
        query_tall = below(scaled[start:stop, :])
        grad_tall = below(grad_ref[start:stop, :])
        product = product_up[:, start:stop]
        centre = jnp.concatenate(
            [
                jnp.sum(product[:HEAD], axis=0, keepdims=True),
                jnp.sum(product[HEAD:], axis=0, keepdims=True),
            ],
            axis=1,
        )
        total = jnp.concatenate(
            [total_ref[0, 0:1, start:stop], total_ref[0, 1:2, start:stop]], axis=1
        )
        query_pos = query_pos_ref[:, start:stop]
        limit = jnp.concatenate([query_pos, query_pos], axis=1)
        dquery = jnp.zeros((PAIR, 2 * tile), F32)
        for piece in range(pieces):
            score = dot(key_refs[piece][:keys, :], query_wide)
            allowed = key_pos_ref[piece, :keys, :] <= limit
            probs = jnp.exp(jnp.where(allowed, score, MASKED_SCORE) - total)
            dprob = dot(value_refs[piece][:keys, :], grad_wide)
            dscore = (probs * (dprob - centre)).astype(BF16)
            dvalue_ref[piece, :keys, :] += dot(probs.astype(BF16), grad_tall)
            dkey_ref[piece, :keys, :] += dot(dscore, query_tall)
            dquery = dquery + dot(keys_up[piece][:, :keys], dscore)
        dquery_ref[start:stop, :] = (heads_back(dquery, tile) * SCALE).astype(BF16)
    down_ref[0] = dkey_ref[0]
    down_ref[1] = dvalue_ref[0]
    for piece in range(1, pieces):
        dother_refs[piece - 1][0] = dkey_ref[piece].astype(BF16)
        dother_refs[piece - 1][1] = dvalue_ref[piece].astype(BF16)


def attend_backward(
    queries, keys_values, outputs, grads, totals, key_pos, query_pos, block, causal, span, begun=()
):
    first, pairs = span
    rows, width = queries.shape
    pieces = len(keys_values)
    shift = width // PAIR
    column = pl.BlockSpec((rows, PAIR), lambda p: (0, p + first))
    second = pl.BlockSpec((rows, PAIR), lambda p: (0, p + first + shift))
    whole_pos = pl.BlockSpec((pieces, rows, 1), lambda p: (0, 0, 0))
    row_pos = pl.BlockSpec((1, rows), lambda p: (0, 0))
    both = pl.BlockSpec((2, rows, PAIR), lambda p: (0, 0, p + first))
    held = 6 + 2 * pieces
    return pl.pallas_call(
        functools.partial(backward_kernel, pieces, block, causal, len(begun)),
        grid=(pairs,),
        in_specs=[
            column,
            column,
            column,
            pl.BlockSpec((1, 2, rows), lambda p: (p + first, 0, 0)),
            whole_pos,
            row_pos,
        ]
        + [column] * pieces
        + [second] * pieces
        + [pl.BlockSpec(memory_space=pl.ANY)] * len(begun),
        out_specs=[column, both] + [both] * (pieces - 1),
        out_shape=[
            pltpu.HBM((rows, width), BF16),
            pltpu.HBM((2, rows, width), F32),
        ]
        + [pltpu.HBM((2, rows, width), BF16)] * (pieces - 1),
        input_output_aliases={held + index: index for index in range(len(begun))},
        scratch_shapes=[pltpu.VMEM((pieces, rows, PAIR), F32)] * 2,
        compiler_params=params(
            [((rows, PAIR), BF16)] * (6 + 4 * pieces) + [((pieces, rows, 128), F32)] * 2,
            spare=10 + 4 * (pieces > 2),
        ),
        cost_estimate=cost((24 if causal else 28) * pairs * PAIR / width),
        name="attend_backward",
    )(queries, outputs, grads, totals, key_pos, query_pos, *keys_values, *keys_values, *begun)


def offset(slot, size):
    return pl.multiple_of(slot * size, size)


def row_parts(place, refs):
    if len(refs) == 1:
        return [(0, refs[0][...])]
    own, one, two, near, far = [ref[...] for ref in refs]
    near_first = jnp.concatenate([near, far], axis=0)
    far_first = jnp.concatenate([far, near], axis=0)
    diagonal = jnp.where(place[4] == 0, near_first, far_first)
    return [(place[0], own), (place[1], one), (place[2], two), (place[3], diagonal)]


def times(left_ref, place, refs):
    total = None
    for slot, part in row_parts(place, refs):
        rows = part.shape[0]
        term = dot(left_ref[:, pl.ds(offset(slot, rows), rows)], part)
        total = term if total is None else total + term
    return total


def times_up(left, place, refs, store):
    for slot, part in row_parts(place, refs):
        rows = part.shape[0]
        store(pl.ds(offset(slot, rows), rows), dot_nt(left, part))


def part_specs(arrays, columns, index):
    return [pl.BlockSpec((item.shape[0], columns), lambda *at: (0, index(*at))) for item in arrays]


def fixed(shape):
    zeros = (0,) * len(shape)
    return pl.BlockSpec(shape, lambda *at: zeros)


def view(item, columns, index):
    if item.ndim == 2:
        return (item, pl.BlockSpec((item.shape[0], columns), lambda *at: (0, index)))
    return (item, pl.BlockSpec((1, item.shape[1], columns), lambda *at: (index, 0, 0)))


def run(kernel, name, place, grid, ins, outs, micros, scratch=(), spare=10):
    kept = [bool(out[3:]) for out in outs]
    outs = [out[:3] for out in outs]
    blocks = [(spec.block_shape, item.dtype) for item, spec in ins]
    blocks += [(spec.block_shape, kind) for _, kind, spec in outs]
    held = sum(bytes_of(item.shape, item.dtype) for item in scratch)
    return pl.pallas_call(
        kernel,
        grid_spec=pltpu.PrefetchScalarGridSpec(
            num_scalar_prefetch=1,
            grid=grid,
            in_specs=[spec for _, spec in ins],
            out_specs=[spec for _, _, spec in outs],
            scratch_shapes=list(scratch),
        ),
        out_shape=[
            pltpu.HBM(shape, kind) if keep else jax.ShapeDtypeStruct(shape, kind)
            for keep, (shape, kind, _) in zip(kept, outs)
        ],
        compiler_params=params(blocks, held, spare),
        cost_estimate=cost(micros),
        name=name,
    )(place, *[in_hbm(item) for item, _ in ins])


def project_kernel(place, left_ref, *refs):
    refs[-1][...] = times(left_ref, place, refs[:-1]).astype(BF16)


def project(place, left, weight, first, count, name):
    rows, depth = left[1].block_shape
    chunk = 512
    steps = count * 1024 // chunk
    base = first * 1024 // chunk
    return run(
        project_kernel,
        name,
        place,
        (steps,),
        [left]
        + list(zip(weight, part_specs(weight, chunk, lambda j, s: base + j))),
        [((rows, count * 1024), BF16, pl.BlockSpec((rows, chunk), lambda j, s: (0, j)))],
        2.5 * count,
    )[0]


def mix_kernel(parts, both, place, mixed_ref, resid_ref, norm_ref, *refs):
    out_parts = refs[:parts]
    query_parts = refs[parts : 2 * parts] if both else ()
    outs = refs[2 * parts :] if both else refs[parts:]
    summed_ref, normed_ref, low_ref = outs[:3]
    step = pl.program_id(0)
    rows, width = summed_ref.shape
    half = width // 2

    @pl.when(step < 2)
    def _():
        columns = pl.ds(offset(step, half), half)
        summed_ref[:, columns] = resid_ref[:, columns].astype(F32) + times(
            mixed_ref, place, out_parts
        )

    @pl.when(step == 1)
    def _():
        for strip in strips(rows):
            normed, _ = norm_parts(summed_ref[strip, :])
            value = normed * norm_ref[0:1, :] + norm_ref[1:2, :]
            normed_ref[strip, :] = value
            low_ref[strip, :] = value.astype(BF16)

    if both:

        @pl.when(step >= 2)
        def _():
            outs[3][...] = times(low_ref, place, query_parts).astype(BF16)


def mix(place, mixed, resid, norm, w_out, at_out, w_query, at_query, name):
    rows, width = mixed.shape
    half = width // 2
    both = w_query is not None
    ins = [(mixed, fixed(mixed.shape)), resid, (norm, fixed(norm.shape))]
    ins += zip(
        w_out, part_specs(w_out, half, lambda j, s: at_out * 2 + jnp.minimum(j, 1))
    )
    outs = [
        ((rows, width), F32, fixed((rows, width)), True),
        ((rows, width), F32, fixed((rows, width)), True),
        ((rows, width), BF16, fixed((rows, width)), True),
    ]
    if both:
        ins += zip(
            w_query,
            part_specs(w_query, half, lambda j, s: at_query * 2 + jnp.maximum(j - 2, 0)),
        )
        outs += [
            (
                (rows, width),
                BF16,
                pl.BlockSpec((rows, half), lambda j, s: (0, jnp.maximum(j - 2, 0))),
            )
        ]
    return run(
        functools.partial(mix_kernel, len(w_out), both),
        name,
        place,
        (4 if both else 2,),
        ins,
        outs,
        6.3 if both else 4,
    )


def up_parts(place, refs, packed):
    if not packed:
        return [(0, refs[0][...])]
    unpacked = []
    for slot, part in row_parts(place, refs):
        rows = part.shape[0] // 2
        unpacked.append((slot, jnp.concatenate([part[:rows], part[rows:]], axis=1)))
    return unpacked


def chunk_of(refs, step, counts, use):
    low = 0
    for ref, count in zip(refs, counts):

        @pl.when((step >= low) & (step < low + count))
        def _(ref=ref):
            use(ref)

        low += count


def feed_specs(w_in, w_out, counts, first, chunk, width):
    in_specs = part_specs(w_in, chunk, lambda j, s: s[8 + first + j])
    shift = first if len(w_in) == 1 else 0
    out_specs, start = [], 0
    for count in counts:
        out_specs.append(
            pl.BlockSpec(
                (chunk, width),
                lambda j, s, start=start, count=count: (
                    shift + jnp.clip(j - start, 0, count - 1),
                    0,
                ),
            )
        )
        start += count
    return in_specs, out_specs


def feed_first_kernel(
    sizes, counts, packed, place, low_ref, second_ref, *refs
):
    n_in, n_out, n_down, n_up = sizes
    in_refs, refs = refs[:n_in], refs[n_in:]
    out_refs, refs = refs[:n_out], refs[n_out:]
    down_refs, refs = refs[:n_down], refs[n_down:]
    up_refs, refs = refs[:n_up], refs[n_up:]
    total_ref, slope_ref, hidden_ref, aslope_ref = refs
    step = pl.program_id(0)

    @pl.when(step == 0)
    def _():
        hidden, slope = gelu_pair(times(low_ref, place, down_refs))
        hidden_ref[...] = hidden.astype(BF16)
        aslope_ref[...] = slope.astype(BF16)
        total = None
        for slot, part in up_parts(place, up_refs, packed):
            count = part.shape[0]
            term = dot(hidden_ref[:, pl.ds(offset(slot, count), count)], part)
            total = term if total is None else total + term
        total_ref[...] = second_ref[...] + 4.0 * total

    feed_chunk(place, low_ref, in_refs, out_refs, counts, total_ref, slope_ref)


def feed_chunk(place, low_ref, in_refs, out_refs, counts, total_ref, slope_ref):
    hidden, slope = gelu_pair(times(low_ref, place, in_refs))
    slope_ref[...] = slope.astype(BF16)
    hidden = hidden.astype(BF16)

    def use(ref):
        total_ref[...] += dot(hidden, ref[...])

    chunk_of(out_refs, pl.program_id(0), counts, use)


def feed_second_kernel(
    sizes, counts, steps, place, low_ref, first_ref, grad_ref, norm_ref, *refs
):
    n_in, n_out = sizes
    in_refs, refs = refs[:n_in], refs[n_in:]
    out_refs, refs = refs[:n_out], refs[n_out:]
    final_ref, d_ref, dlow_ref, dnorm_ref, slope_ref, total_ref = refs
    step = pl.program_id(0)
    rows, width = total_ref.shape

    @pl.when(step == 0)
    def _():
        total_ref[...] = first_ref[...]

    feed_chunk(place, low_ref, in_refs, out_refs, counts, total_ref, slope_ref)

    @pl.when(step == steps - 1)
    def _():
        gain, shift = norm_ref[0:1, :], norm_ref[1:2, :]
        dgain = jnp.zeros((1, width), F32)
        dshift = jnp.zeros((1, width), F32)
        for strip in strips(rows):
            normed, rstd = norm_parts(total_ref[strip, :])
            final_ref[strip, :] = (normed * gain + shift).astype(BF16)
            grad = grad_ref[strip, :].astype(F32)
            dgain += jnp.sum(grad * normed, axis=0, keepdims=True)
            dshift += jnp.sum(grad, axis=0, keepdims=True)
            back = norm_backward(normed, rstd, gain, grad)
            d_ref[strip, :] = back
            dlow_ref[strip, :] = back.astype(BF16)
        dnorm_ref[0:1, :] = dgain
        dnorm_ref[1:2, :] = dshift


CHUNK = 512


def feed_first(place, low, second, w_in, w_out, counts, w_down, at_down, w_up, at_up):
    rows, width = low.shape
    adapter = 512
    packed = len(w_up) > 1
    steps = sum(counts)
    in_specs, out_specs = feed_specs(w_in, w_out, counts, 0, CHUNK, width)
    up_columns = 512 if packed else width
    full = fixed((rows, width))
    ins = [(low, full), (second, full)]
    ins += zip(w_in, in_specs)
    ins += zip(w_out, out_specs)
    ins += zip(w_down, part_specs(w_down, adapter, lambda j, s: at_down))
    ins += zip(w_up, part_specs(w_up, up_columns, lambda j, s: at_up))
    return run(
        functools.partial(
            feed_first_kernel, (len(w_in), len(w_out), len(w_down), len(w_up)), counts, packed
        ),
        "feed_first",
        place,
        (steps,),
        ins,
        [
            ((rows, width), F32, full),
            ((rows, steps * CHUNK), BF16, pl.BlockSpec((rows, CHUNK), lambda j, s: (0, j)), True),
            ((rows, adapter), BF16, fixed((rows, adapter)), True),
            ((rows, adapter), BF16, fixed((rows, adapter)), True),
        ],
        13,
    )


def feed_second(place, low, first, grad, norm, w_in, w_out, counts, start):
    rows, width = low.shape
    steps = sum(counts)
    in_specs, out_specs = feed_specs(w_in, w_out, counts, start, CHUNK, width)
    full = fixed((rows, width))
    ins = [(low, full), (first, full), (grad, full), (norm, fixed(norm.shape))]
    ins += zip(w_in, in_specs)
    ins += zip(w_out, out_specs)
    return run(
        functools.partial(feed_second_kernel, (len(w_in), len(w_out)), counts, steps),
        "feed_second",
        place,
        (steps,),
        ins,
        [
            ((rows, width), BF16, full, True),
            ((rows, width), F32, full),
            ((rows, width), BF16, full),
            ((2, width), F32, fixed((2, width)), True),
            ((rows, steps * CHUNK), BF16, pl.BlockSpec((rows, CHUNK), lambda j, s: (0, j)), True),
        ],
        13.5,
        scratch=[pltpu.VMEM((rows, width), F32)],
    )


def feed_backward_kernel(
    sizes,
    counts,
    packed,
    steps,
    place,
    dlow_ref,
    d_ref,
    resid_ref,
    norm_ref,
    slope_ref,
    later_ref,
    aslope_ref,
    *refs,
):
    n_in, n_out, n_down, n_up, n_mix = sizes
    in_refs, refs = refs[:n_in], refs[n_in:]
    out_refs, refs = refs[:n_out], refs[n_out:]
    down_refs, refs = refs[:n_down], refs[n_down:]
    up_refs, refs = refs[:n_up], refs[n_up:]
    mix_refs, refs = refs[:n_mix], refs[n_mix:]
    dtwo_ref, dtwo_low_ref, dnorm_ref, dadapter_ref, dmixed_ref, total_ref, dhidden_ref = refs
    step = pl.program_id(0)
    rows, width = total_ref.shape

    def add(columns, value):
        total_ref[:, columns] += value

    @pl.when(step == 0)
    def _():
        total_ref[...] = d_ref[...]
        for slot, part in up_parts(place, up_refs, packed):
            count = part.shape[0]
            columns = pl.ds(offset(slot, count), count)
            back = 4.0 * dot_nt(dlow_ref[...], part)
            dadapter_ref[:, columns] = (aslope_ref[:, columns].astype(F32) * back).astype(BF16)
        times_up(dadapter_ref[...], place, down_refs, add)

    def use(ref):
        back = dot_nt(dlow_ref[...], ref[...])
        chosen = jnp.where(step < steps // 2, slope_ref[...], later_ref[...])
        dhidden_ref[...] = (chosen.astype(F32) * back).astype(BF16)

    chunk_of(out_refs, step, counts, use)
    times_up(dhidden_ref[...], place, in_refs, add)

    @pl.when(step == steps - 1)
    def _():
        finish_norm(total_ref, resid_ref, norm_ref, dtwo_ref, dtwo_low_ref, dnorm_ref)

        def keep(columns, value):
            dmixed_ref[:, columns] = value.astype(BF16)

        times_up(dtwo_low_ref[...], place, mix_refs, keep)


def finish_norm(grad_ref, resid_ref, norm_ref, d_ref, dlow_ref, dnorm_ref):
    rows, width = grad_ref.shape
    gain = norm_ref[0:1, :]
    dgain = jnp.zeros((1, width), F32)
    dshift = jnp.zeros((1, width), F32)
    for strip in strips(rows):
        grad = grad_ref[strip, :]
        normed, rstd = norm_parts(resid_ref[strip, :])
        dgain += jnp.sum(grad * normed, axis=0, keepdims=True)
        dshift += jnp.sum(grad, axis=0, keepdims=True)
        back = norm_backward(normed, rstd, gain, grad)
        d_ref[strip, :] = back
        dlow_ref[strip, :] = back.astype(BF16)
    dnorm_ref[0:1, :] = dgain
    dnorm_ref[1:2, :] = dshift


def feed_backward(
    place,
    dlow,
    d_three,
    resid,
    norm,
    slope,
    later,
    aslope,
    w_in,
    w_out,
    counts,
    w_down,
    at_down,
    w_up,
    at_up,
    w_mix,
    at_mix,
):
    rows, width = dlow.shape
    hidden = w_in[0].shape[1]
    adapter = 512
    packed = len(w_up) > 1
    chunk = CHUNK
    steps = hidden // chunk
    in_specs, out_specs = feed_specs(w_in, w_out, counts, 0, chunk, width)
    middle = steps // 2
    up_columns = 512 if packed else width
    full = fixed((rows, width))
    ins = [
        (dlow, full),
        (d_three, full),
        (resid, full),
        (norm, fixed(norm.shape)),
        (slope, pl.BlockSpec((rows, chunk), lambda j, s: (0, jnp.minimum(j, middle - 1)))),
        (later, pl.BlockSpec((rows, chunk), lambda j, s: (0, jnp.maximum(j - middle, 0)))),
        (aslope, fixed((rows, adapter))),
    ]
    ins += zip(w_in, in_specs)
    ins += zip(w_out, out_specs)
    ins += zip(w_down, part_specs(w_down, adapter, lambda j, s: at_down))
    ins += zip(w_up, part_specs(w_up, up_columns, lambda j, s: at_up))
    ins += zip(w_mix, part_specs(w_mix, width, lambda j, s: at_mix))
    return run(
        functools.partial(
            feed_backward_kernel,
            (len(w_in), len(w_out), len(w_down), len(w_up), len(w_mix)),
            counts,
            packed,
            steps,
        ),
        "feed_backward",
        place,
        (steps,),
        ins,
        [
            ((rows, width), F32, full, True),
            ((rows, width), BF16, full),
            ((2, width), F32, fixed((2, width)), True),
            ((rows, adapter), BF16, fixed((rows, adapter))),
            ((rows, width), BF16, full),
        ],
        29,
        scratch=[pltpu.VMEM((rows, width), F32), pltpu.VMEM((rows, chunk), BF16)],
    )


def norm_step_kernel(parts, place, dquery_ref, d_ref, resid_ref, norm_ref, *refs):
    query_refs, refs = refs[:parts], refs[parts:]
    out_refs, refs = refs[:parts], refs[parts:]
    done_ref, done_low_ref, dnorm_ref, dmixed_ref, total_ref = refs
    step = pl.program_id(0)

    @pl.when(step == 0)
    def _():
        def add(columns, value):
            total_ref[:, columns] = d_ref[:, columns] + value

        times_up(dquery_ref[...], place, query_refs, add)
        finish_norm(total_ref, resid_ref, norm_ref, done_ref, done_low_ref, dnorm_ref)

    @pl.when(step == 1)
    def _():
        def keep(columns, value):
            dmixed_ref[:, columns] = value.astype(BF16)

        times_up(done_low_ref[...], place, out_refs, keep)


def norm_step(place, dquery, d_two, resid, norm, w_query, at_query, w_out, at_out):
    rows, width = dquery.shape
    full = fixed((rows, width))
    ins = [(dquery, full), (d_two, full), (resid, full), (norm, fixed(norm.shape))]
    ins += zip(w_query, part_specs(w_query, width, lambda j, s: at_query))
    ins += zip(w_out, part_specs(w_out, width, lambda j, s: at_out))
    return run(
        functools.partial(norm_step_kernel, len(w_query)),
        "norm_step",
        place,
        (2,),
        ins,
        [
            ((rows, width), F32, full, True),
            ((rows, width), BF16, full),
            ((2, width), F32, fixed((2, width)), True),
            ((rows, width), BF16, full),
        ],
        6.6,
        scratch=[pltpu.VMEM((rows, width), F32)],
    )


def inputs_back_kernel(lefts, parts, extra, place, *refs):
    left_refs, refs = refs[:lefts], refs[lefts:]
    part_refs, refs = refs[:parts], refs[parts:]
    if extra:
        extra_ref, refs = refs[0], refs[1:]
    out_ref, total_ref = refs
    step = pl.program_id(0)
    width = total_ref.shape[1]

    @pl.when(step == 0)
    def _():
        if extra == "base":
            total_ref[...] = extra_ref[...]
        else:
            total_ref[...] = jnp.zeros_like(total_ref)
        if extra == "beside":
            out_ref[:, :width] = extra_ref[...]

    def add(columns, value):
        total_ref[:, columns] += value

    for which in range(lefts):

        @pl.when(step == which)
        def _(which=which):
            left = left_refs[which][...]
            times_up(left.reshape(left.shape[-2:]), place, part_refs, add)

    @pl.when(step == lefts - 1)
    def _():
        out_ref[:, out_ref.shape[1] - width :] = total_ref[...].astype(BF16)


def inputs_back(place, lefts, weight, blocks, extra, item, name):
    depth = lefts[0][1].block_shape[-1]
    rows = lefts[0][1].block_shape[-2]
    width = 1024
    first = blocks[0]
    strides = {blocks[k + 1] - blocks[k] for k in range(len(blocks) - 1)}

    def at(j, s):
        index = first
        for k in range(1, len(blocks)):
            index = jnp.where(j == k, blocks[k], index)
        return first + j if strides == {1} else index

    ins = list(lefts)
    ins += zip(weight, part_specs(weight, depth, at))
    if extra:
        ins += [(item, fixed((rows, width)))]
    size = 2 * width if extra == "beside" else width
    return run(
        functools.partial(inputs_back_kernel, len(lefts), len(weight), extra),
        name,
        place,
        (len(lefts),),
        ins,
        [((rows, size), BF16, fixed((rows, size)))],
        3 * len(lefts) * depth / width,
        scratch=[pltpu.VMEM((rows, width), F32)],
    )[0]


def laid_out_kernel(slots, item_ref, *refs):
    out_ref = refs[-1]
    out_ref[slots[0]] = item_ref[0]
    for index, ref in enumerate(refs[:-1], 1):
        out_ref[slots[index]] = ref[...]


def laid_out(slots, item, parts):
    part = parts[0].shape
    return run(
        laid_out_kernel,
        "laid_out",
        slots,
        (1,),
        [(item, pl.BlockSpec((1,) + part, lambda j, s: (s[0], 0, 0)))]
        + [(piece, fixed(part)) for piece in parts],
        [(item.shape, item.dtype, fixed(item.shape))],
        1.5,
    )[0]


def swap_pairs(size, bit):
    return [(index, index ^ bit) for index in range(size)]


def by_core(even, odd):
    return [
        (d * 8 + s, (d ^ (odd if s % 2 else even)) * 8 + s) for d in range(4) for s in range(8)
    ]


def after(item, *others):
    return lax.optimization_barrier((item,) + others)[0]


def gather_first(own):
    return (own, lax.ppermute(own, ("dp", "seq"), by_core(1, 2)))


def gather_swap(parts, *others):
    return parts + (lax.ppermute(after(parts[1], *others), "seq", swap_pairs(8, 1)),)


def gather_near(parts, core, *others):
    one = parts[1]
    half = one.shape[0] // 2
    half_one = lax.dynamic_slice_in_dim(after(one, *others), core * half, half, 0)
    return parts + (lax.ppermute(half_one, ("dp", "seq"), by_core(2, 1)),)


def gather_far(parts, *others):
    return parts + (lax.ppermute(after(parts[3], *others), "seq", swap_pairs(8, 1)),)


def gather_dp(item):
    return (lax.all_gather(item, "dp", axis=0, tiled=True),)


def row_blocks(value, size):
    return [value[start : start + size] for start in range(0, value.shape[0], size)]


def wgrad_kernel(fresh, split, scales, extra, place, *refs):
    count = len(fresh)
    left_refs, right_refs = refs[:count], refs[count : 2 * count]
    outs, up_ref = refs[2 * count + extra : -1], refs[-1]
    step = pl.program_id(0)
    wide = outs[0].shape[1]
    if extra:

        @pl.when(step == count)
        def _():
            rows = jnp.concatenate([ref[...] for ref in refs[2 * count : 2 * count + extra]])
            filler = jnp.zeros((128 - rows.shape[0], rows.shape[1]), F32)
            columns = jnp.concatenate([rows, filler], axis=0).T.astype(BF16)
            blocks = row_blocks(columns, 32)
            even = jnp.concatenate(blocks[0::2], axis=0)
            odd = jnp.concatenate(blocks[1::2], axis=0)
            outs[0][:, :128] = jnp.where(place[4] == 0, odd, even)
            outs[1][:, :128] = jnp.where(place[4] == 0, even, odd)
            for out in outs:
                out[:, 128:256] = jnp.zeros(even.shape, BF16)

    for which in range(count):

        @pl.when(step == which)
        def _(which=which):
            right = right_refs[which][...]
            right = right.reshape(right.shape[-2:])
            tall = left_refs[which].shape[-1]
            if fresh[which]:
                left = left_refs[which][...]
                up_ref[:tall, :] = left.reshape(left.shape[-2:]).T
            value = dot(up_ref[:tall, :], right)
            value = (value * scales[which] if scales[which] != 1.0 else value).astype(BF16)
            own = tall // 32
            blocks = row_blocks(value, own)
            if split:
                even = jnp.concatenate(blocks[0::2], axis=0)
                odd = jnp.concatenate(blocks[1::2], axis=0)
                outs[0][...] = jnp.where(place[4] == 0, odd, even)
                outs[1][...] = jnp.where(place[4] == 0, even, odd)
                return
            folds = right.shape[1] // wide
            for index, item in enumerate(blocks):
                at = (index % 8 * 4 + index // 8) * own * folds
                for fold in range(folds):
                    low = at + fold * own
                    outs[0][low : low + own, :] = item[:, fold * wide : (fold + 1) * wide]


def wgrad(place, lefts, rights, wide, split, scales, name, extra=()):
    fresh = []
    for index, (item, spec) in enumerate(lefts):
        before = lefts[index - 1] if index else (None, None)
        fresh.append(item is not before[0] or spec is not before[1])
    rows, tall = lefts[0][1].block_shape[-2:]
    high = tall // 2 if split else tall
    spec = pl.BlockSpec((high, wide), lambda j, s: (0, j))
    more = 1 if extra else 0
    return run(
        functools.partial(wgrad_kernel, tuple(fresh), split, scales, len(extra)),
        name,
        place,
        (len(lefts) + more,),
        list(lefts) + list(rights) + [(item, fixed(item.shape)) for item in extra],
        [((high, wide * len(lefts) + 256 * more), BF16, spec, True)] * (2 if split else 1),
        1.6 * len(lefts) * wide / 1024,
        scratch=[pltpu.VMEM((tall, rows), BF16)],
    )


def take(item, index, axis):
    return lax.dynamic_index_in_dim(item, index, axis, keepdims=False)


def add(kept, received, kind=BF16):
    return (kept.astype(F32) + received.astype(F32)).astype(kind)


def sum_over(partial, name):
    return lax.psum_scatter(partial, name, scatter_dimension=0, tiled=True)


class Scatter:
    def __init__(self, send, keep):
        here, there = lax.axis_index("dp"), lax.axis_index("seq")
        self.x, self.y = here % 2, here // 2
        self.low, self.high = (there // 2) % 2, there // 4
        self.send, self.keep = send, keep
        self.width = keep.shape[1]

    def core(self):
        received = lax.ppermute(self.send, "seq", swap_pairs(8, 1))
        item = add(self.keep, received).reshape(2, 2, 128, self.width)
        self.one, self.two = item[..., : self.width // 2], item[..., self.width // 2 :]
        return self.one

    def plane_one(self):
        x, y = self.x, self.y
        from_x = lax.ppermute(take(self.one, 1 - x, 1), "dp", swap_pairs(4, 1))
        from_y = lax.ppermute(take(self.two, 1 - y, 0), "dp", swap_pairs(4, 2))
        self.one = add(take(self.one, x, 1), from_x)
        self.two = add(take(self.two, y, 0), from_y)
        return self.one

    def plane_two(self):
        x, y = self.x, self.y
        from_y = lax.ppermute(take(self.one, 1 - y, 0), "dp", swap_pairs(4, 2))
        from_x = lax.ppermute(take(self.two, 1 - x, 0), "dp", swap_pairs(4, 1))
        one = add(take(self.one, y, 0), from_y)
        two = add(take(self.two, x, 0), from_x)
        self.item = jnp.concatenate([one, two], axis=1)
        return self.item

    def z_one(self):
        self.item = self.item.reshape(2, 2, 32, self.width)
        received = lax.ppermute(take(self.item, 1 - self.low, 1), "seq", swap_pairs(8, 2))
        self.item = add(take(self.item, self.low, 1), received)
        return self.item

    def z_two(self):
        received = lax.ppermute(take(self.item, 1 - self.high, 0), "seq", swap_pairs(8, 4))
        self.item = add(take(self.item, self.high, 0), received, F32)
        return self.item


def sum_all(partial):
    return lax.psum_scatter(
        partial.astype(BF16), ("dp", "seq"), scatter_dimension=0, tiled=True
    ).astype(F32)


def body(
    target,
    source,
    target_len,
    source_len,
    self_query,
    self_key,
    self_value,
    self_output,
    cross_query,
    cross_key,
    cross_value,
    cross_output,
    feed_in,
    feed_out,
    adapter_down,
    adapter_up,
    self_gain,
    self_shift,
    cross_gain,
    cross_shift,
    final_gain,
    final_shift,
    cotangent,
):
    block, seqs, width = target.shape
    dp, seq = lax.axis_size("dp"), lax.axis_size("seq")
    group = seq // seqs
    rows = seqs * block
    here, there = lax.axis_index("dp"), lax.axis_index("seq")
    inner, which = there % group, there // group
    core = there % 2
    halving = dp == 4 and seq == 8
    apart = [[start + group * step for step in range(seqs)] for start in range(group)]

    def to_sequence(item):
        return lax.all_to_all(
            item.swapaxes(0, 1), "seq", 0, 0, axis_index_groups=apart, tiled=True
        ).reshape(rows, item.shape[-1])

    slots = jnp.stack([which ^ bit for bit in range(seqs)]).astype(jnp.int32)

    def send_back(item):
        item = item.reshape(seqs, block, item.shape[-1])
        parts = [item]
        for bit in range(1, seqs):
            pairs = [(index, (index // group ^ bit) * group + index % group) for index in range(seq)]
            parts.append(lax.ppermute(take(item, which ^ bit, 0), "seq", pairs))
        return parts

    def set_down(parts, *others):
        item, *parts = lax.optimization_barrier((*parts, *others))[: len(parts)]
        return laid_out(slots, item, parts).swapaxes(0, 1)

    def near(shift):
        return [
            (k * group + c, k * group + (c + shift) % group)
            for k in range(seqs)
            for c in range(group)
        ]

    def spread(item):
        return [item] + [lax.ppermute(item, "seq", near(-s)) for s in range(1, group)]

    def collect(own, others):
        for shift, other in enumerate(others, 1):
            own = own + lax.ppermute(other, "seq", near(shift)).astype(F32)
        return own.astype(BF16)

    own_inputs, own_memory = to_sequence(target), to_sequence(source)
    inputs, memory = view(own_inputs, width, 0), view(own_memory, width, 0)
    grad_out = to_sequence(cotangent)
    vectors = jnp.stack([self_gain, self_shift, cross_gain, cross_shift, final_gain, final_shift])
    if halving:
        one = jnp.where(core == 0, here ^ 1, here ^ 2)
        two = jnp.where(core == 0, here ^ 2, here ^ 1)
        diagonal = here ^ 3
        chunks = [item * 2 + part for item in (here, one, two) for part in (0, 1)]
        chunks += [diagonal * 2 + core, diagonal * 2 + 1 - core]
        place = jnp.stack([here, one, two, diagonal, core, core, core, core] + chunks)
        first_group = jnp.concatenate(
            [self_query, self_key, self_value, cross_key, cross_value], axis=1
        )
        half = width // 2
        up_packed = jnp.concatenate([adapter_up[:, :half], adapter_up[:, half:]], axis=0)
        second_group = jnp.concatenate(
            [self_output, cross_query, cross_output, adapter_down, up_packed], axis=1
        )
        vector_parts = [vectors] + [
            lax.ppermute(vectors, "dp", swap_pairs(4, bit)) for bit in (1, 2, 3)
        ]
        w_self = gather_swap(gather_first(first_group))
        w_self = gather_far(
            gather_near(w_self, core, own_inputs, second_group, *vector_parts)
        )
        w_mid = gather_swap(gather_first(after(second_group, w_self[3])))
        w_in = gather_first(after(feed_in, w_mid[1]))
        at_q, at_kv, at_ckv = (w_self, 0), (w_self, 1), (w_self, 3)
        parts = jnp.stack(vector_parts)
        vectors = jnp.concatenate([take(parts, here ^ slot, 0) for slot in range(4)], axis=1)
        counts_first, counts_second = (2, 2), (2, 1, 1)
    else:
        steps = feed_in.shape[1] // CHUNK
        place = jnp.stack([jnp.int32(0)] * 8 + [jnp.int32(j) for j in range(steps)])
        at_q = (gather_dp(self_query), 0)
        at_kv = (gather_dp(jnp.concatenate([self_key, self_value], axis=1)), 0)
        at_o, at_cq = (gather_dp(self_output), 0), (gather_dp(cross_query), 0)
        at_ckv = (gather_dp(jnp.concatenate([cross_key, cross_value], axis=1)), 0)
        at_co = (gather_dp(cross_output), 0)
        w_in, w_out = gather_dp(feed_in), gather_dp(feed_out)
        at_down, at_up = (gather_dp(adapter_down), 0), (gather_dp(adapter_up), 0)
        vectors = lax.all_gather(vectors, "dp", axis=1, tiled=True)
        out_first = out_second = w_out
        counts_first, counts_second = (steps // 2,), (steps - steps // 2,)
    place = place.astype(jnp.int32)
    vectors = vectors.astype(F32)
    norm_one, norm_two, norm_three = vectors[0:2], vectors[2:4], vectors[4:6]

    local = jnp.arange(rows, dtype=jnp.int32)

    def positions(place_in_group):
        return (local // block * group + place_in_group) * block + local % block

    target_limit = take(target_len, which, 0)
    source_limit = take(source_len, which, 0)
    key_pos = jnp.stack([positions((inner + shift) % group) for shift in range(group)])
    self_keys = jnp.where(key_pos < target_limit, key_pos, NEVER)[..., None]
    cross_keys = jnp.where(key_pos < source_limit, key_pos, NEVER)[..., None]
    self_rows = positions(inner)[None]
    cross_rows = jnp.full((1, rows), ALWAYS, jnp.int32)

    kv_own = project(place, inputs, *at_kv, 2, "self_kv")
    kv_all = spread(kv_own)
    queries = project(place, inputs, *at_q, 1, "self_q")
    if halving:
        w_mid = gather_near(w_mid, core, queries)
        queries = after(queries, w_mid[1])
    mixed, totals = attend_forward(queries, kv_all, self_keys, self_rows, block, True)
    ckv_own = project(
        place, (after(own_memory, mixed), memory[1]), *at_ckv, 2, "cross_kv"
    )
    ckv_all = spread(ckv_own)
    mixed = after(mixed, ckv_own)
    if halving:
        w_mid = gather_far(w_mid, mixed)
        w_out = gather_first(after(feed_out, mixed))
        at_o, at_cq, at_co = (w_mid, 0), (w_mid, 1), (w_mid, 2)
        at_down, at_up = (w_mid, 6), (w_mid, 7)
    resid_one, first, first_low, cross_q = mix(
        place, mixed, inputs, norm_one, *at_o, *at_cq, "mix_self"
    )
    if halving:
        w_in = gather_near(gather_swap(w_in, cross_q), core, cross_q)
        cross_q = after(cross_q, w_in[1])
    cross_mixed, cross_totals = attend_forward(
        cross_q, ckv_all, cross_keys, cross_rows, block, False
    )
    if halving:
        w_in = gather_far(w_in, cross_mixed)
        w_out = gather_far(gather_near(gather_swap(w_out, cross_mixed), core, cross_mixed))
        out_first, out_second = w_out[:2], w_out[2:]
    cross_mixed = after(cross_mixed, grad_out)
    resid_two, second, second_low = mix(
        place, cross_mixed, view(first, width, 0), norm_two, *at_co, None, None, "mix_cross"
    )
    partial, slope, hidden, adapter_slope = feed_first(
        place, second_low, second, w_in, out_first, counts_first, *at_down, *at_up
    )
    final, d_three, d_branch, d_norm_three, later = feed_second(
        place,
        second_low,
        partial,
        grad_out,
        norm_three,
        w_in,
        out_second,
        counts_second,
        sum(counts_first),
    )
    output = send_back(final)

    d_two, d_two_low, d_norm_two, d_adapter, d_cross = feed_backward(
        place,
        d_branch,
        d_three,
        resid_two,
        norm_two,
        slope,
        later,
        adapter_slope,
        w_in,
        w_out,
        counts_first + counts_second if halving else (steps,),
        *at_down,
        *at_up,
        *at_co,
    )

    d_two_low = after(d_two_low, *output[1:])

    def whole(item, layer=0):
        return view(item, item.shape[-1], layer)

    pairs = width // PAIR
    if halving:
        half = width // 2
        left = whole(cross_mixed)
        early = wgrad(
            place,
            [left, left, whole(second_low), whole(hidden)],
            [view(d_two_low, half, 0), view(d_two_low, half, 1), whole(d_adapter), whole(d_branch)],
            half,
            False,
            (1.0, 1.0, 1.0, 4.0),
            "wgrad_early",
        )[0]
        d_cross = after(d_cross, early)
        early = sum_over(early, "seq")
    d_cq, *d_ckv = attend_backward(
        cross_q,
        ckv_all,
        cross_mixed,
        d_cross,
        cross_totals,
        cross_keys,
        cross_rows,
        block,
        False,
        (0, pairs),
    )
    output = set_down(output, d_cq)
    d_one, d_one_low, d_norm_one, d_mixed = norm_step(
        place, d_cq, d_two, resid_one, norm_one, *at_cq, *at_o
    )
    d_ckv = collect(after(d_ckv[0], d_one_low), d_ckv[1:])
    grad_source = inputs_back(
        place,
        [whole(d_ckv, 0), whole(d_ckv, 1)],
        at_ckv[0],
        [at_ckv[1], at_ckv[1] + 1],
        None,
        None,
        "source_back",
    )
    d_ckv = after(d_ckv, grad_source)
    grad_source = send_back(grad_source)
    if halving:
        d_one_low = after(d_one_low, early)
        early = sum_over(early, "dp").astype(F32)
        inner_sums = Scatter(
            *wgrad(
                place,
                [memory, memory, whole(mixed), whole(first_low)],
                [whole(d_ckv, 0), whole(d_ckv, 1), whole(d_one_low), whole(d_cq)],
                width,
                True,
                (1.0,) * 4,
                "wgrad_inner",
                [d_norm_one, d_norm_two, d_norm_three],
            )
        )
    if halving:
        d_mixed = after(d_mixed, inner_sums.core())
    else:
        d_mixed = after(d_mixed, grad_source[0])

    begun = ()
    split = pairs * 3 // 4
    for span in ((0, split), (split, pairs - split)):
        begun = attend_backward(
            queries,
            kv_all,
            mixed,
            d_mixed,
            totals,
            self_keys,
            self_rows,
            block,
            True,
            span,
            begun,
        )
        if halving and span[0] == 0:
            d_mixed = after(d_mixed, begun[0], *grad_source[1:3])
    d_q, *d_kv = begun
    d_kv = collect(d_kv[0], d_kv[1:])
    at_self = at_q if halving else ((jnp.concatenate([at_q[0][0], at_kv[0][0]], axis=1),), 0)
    grad_target = inputs_back(
        place,
        [whole(d_q), whole(d_kv, 0), whole(d_kv, 1)],
        at_self[0],
        [at_self[1] + index for index in range(3)],
        "base",
        d_one,
        "target_back",
    )
    d_q = after(d_q, grad_target)
    grad_target = send_back(grad_target)
    if not halving:
        grad_source = set_down(grad_source)
        grad_target = set_down(grad_target)
    if halving:
        d_q = after(d_q, inner_sums.plane_one())
        late = Scatter(
            *wgrad(
                place,
                [inputs] * 3,
                [whole(d_q), whole(d_kv, 0), whole(d_kv, 1)],
                width,
                True,
                (1.0,) * 3,
                "wgrad_self",
            )
        )
        grad_source = set_down(grad_source, late.send)
        late.keep = after(late.keep, inner_sums.plane_two(), grad_source, *grad_target[1:])
        late.core()
        late.plane_one()
        late.one, late.two, *_ = lax.optimization_barrier(
            (late.one, late.two, inner_sums.z_one(), *grad_target)
        )
        grad_target = set_down(grad_target, late.one)
        late.plane_two()
        late.item = after(late.item, grad_target, inner_sums.z_two())
        late.z_one()
        late.z_two()
        grad_co, grad_down = early[:, :width], early[:, width : width + half]
        lifted = early[:, width + half :]
        folded = lifted.shape[0] // 2
        grad_up = jnp.concatenate([lifted[:folded], lifted[folded:]], axis=1)
        norm_sums = inner_sums.item[:, 4 * width : 4 * width + 6].T
        grad_ck, grad_cv, grad_o, grad_cq = [
            inner_sums.item[:, index * width : (index + 1) * width] for index in range(4)
        ]
        grad_q, grad_k, grad_v = [
            late.item[:, index * width : (index + 1) * width] for index in range(3)
        ]
    else:
        norm_sums = jnp.concatenate([d_norm_one, d_norm_two, d_norm_three], axis=0)
        norm_sums = lax.psum_scatter(norm_sums, ("dp", "seq"), scatter_dimension=1, tiled=True)
        grad_down = sum_all(dot_tn(second_low, d_adapter))
        grad_up = sum_all(4.0 * dot_tn(hidden, d_branch))
        grad_co = sum_all(dot_tn(cross_mixed, d_two_low))
        grad_o = sum_all(dot_tn(mixed, d_one_low))
        grad_cq = sum_all(dot_tn(first_low, d_cq))
        grad_ck = sum_all(dot_tn(own_memory, d_ckv[0]))
        grad_cv = sum_all(dot_tn(own_memory, d_ckv[1]))
        grad_q = sum_all(dot_tn(own_inputs, d_q))
        grad_k = sum_all(dot_tn(own_inputs, d_kv[0]))
        grad_v = sum_all(dot_tn(own_inputs, d_kv[1]))
    return (
        output,
        grad_target,
        grad_source,
        grad_q,
        grad_k,
        grad_v,
        grad_o,
        grad_cq,
        grad_ck,
        grad_cv,
        grad_co,
        grad_down,
        grad_up,
        *[norm_sums[index] for index in range(6)],
    )


def solution(mesh):
    tokens = P("seq", "dp", None)
    rows = P("dp", None)
    vector = P("dp")
    both = P(("dp", "seq"), None)
    return jax.shard_map(
        body,
        mesh=mesh,
        in_specs=(tokens, tokens, vector, vector) + (rows,) * 12 + (vector,) * 6 + (tokens,),
        out_specs=(tokens,) * 3 + (both,) * 10 + (P(("dp", "seq")),) * 6,
        check_vma=False,
    )
```

```python
import functools

import jax
import jax.numpy as jnp
from jax import lax
from jax.experimental import pallas as pl
from jax.experimental.pallas import tpu as pltpu
from jax.sharding import PartitionSpec as P

HEAD = 64
PAIR = 2 * HEAD
SCALE = HEAD ** (-0.5)
MASKED_SCORE = -1e30
NEVER = 2**30
ALWAYS = 2**29
F32 = jnp.float32
BF16 = jnp.bfloat16
STRIP = 128
ROOT_HALF = 0.7071067811865476
PDF_SCALE = 0.3989422804014327


def dot(left, right):
    return jnp.dot(left, right, preferred_element_type=F32)


def dot_tn(left, right):
    return lax.dot_general(left, right, (((0,), (0,)), ((), ())), preferred_element_type=F32)


def dot_nt(left, right):
    return lax.dot_general(left, right, (((1,), (1,)), ((), ())), preferred_element_type=F32)


def gelu_pair(inputs):
    below_it = 0.5 * (1.0 + lax.erf(inputs * ROOT_HALF))
    density = PDF_SCALE * jnp.exp(-0.5 * inputs * inputs)
    return inputs * below_it, below_it + inputs * density


def norm_parts(inputs):
    centre = jnp.mean(inputs, axis=-1, keepdims=True)
    centred = inputs - centre
    spread = jnp.mean(centred * centred, axis=-1, keepdims=True)
    rstd = lax.rsqrt(spread + 1e-05)
    return centred * rstd, rstd


def norm_backward(normed, rstd, gain, grad):
    inner = grad * gain
    mean_one = jnp.mean(inner, axis=-1, keepdims=True)
    mean_two = jnp.mean(inner * normed, axis=-1, keepdims=True)
    return rstd * (inner - mean_one - normed * mean_two)


def strips(rows):
    return [slice(start, start + STRIP) for start in range(0, rows, STRIP)]


MIB = 1024 * 1024


def bytes_of(shape, kind):
    size = jnp.dtype(kind).itemsize
    for extent in shape:
        size *= extent
    return size


def in_hbm(item):
    if item.size * item.dtype.itemsize < 256 * 1024:
        return item
    return pltpu.with_memory_space_constraint(item, pltpu.HBM)


def params(blocks, scratch=0, spare=10):
    limit = 2 * sum(bytes_of(shape, kind) for shape, kind in blocks) + scratch + spare * MIB
    return pltpu.CompilerParams(vmem_limit_bytes=min(limit, 60 * MIB))


def cost(micros):
    return pl.CostEstimate(
        flops=int(micros * 1.15e9), bytes_accessed=int(micros * 3.6e6), transcendentals=0
    )


def tile_of(rows):
    return 128 if rows % 128 == 0 else rows


def key_rows(tile_end, rows, block, causal):
    if not causal:
        return rows
    return min(rows, ((tile_end - 1) // block + 1) * block)


def beside(top):
    row = lax.broadcasted_iota(jnp.int32, top.shape, 0)
    zero = jnp.zeros_like(top)
    return jnp.concatenate(
        [jnp.where(row < HEAD, top, zero), jnp.where(row < HEAD, zero, top)], axis=1
    )


def below(side):
    lane = lax.broadcasted_iota(jnp.int32, side.shape, 1)
    zero = jnp.zeros_like(side)
    return jnp.concatenate(
        [jnp.where(lane < HEAD, side, zero), jnp.where(lane < HEAD, zero, side)], axis=0
    )


def heads_back(wide, tile):
    return jnp.concatenate([wide[:HEAD, :tile], wide[HEAD:, tile:]], axis=0).T


def forward_kernel(pieces, block, causal, *refs):
    query_ref, key_pos_ref, query_pos_ref = refs[:3]
    key_refs = refs[3 : 3 + pieces]
    value_refs = refs[3 + pieces : 3 + 2 * pieces]
    out_ref, total_ref = refs[3 + 2 * pieces :]
    rows = query_ref.shape[0]
    tile = tile_of(rows)
    scaled = query_ref[...].astype(F32) * SCALE
    query_up = scaled.T.astype(BF16)
    values_up = [ref[...].astype(F32).T.astype(BF16) for ref in value_refs]
    for start in range(0, rows, tile):
        keys = key_rows(start + tile, rows, block, causal)
        wide = beside(query_up[:, start : start + tile])
        query_pos = query_pos_ref[:, start : start + tile]
        limit = jnp.concatenate([query_pos, query_pos], axis=1)
        scores = []
        for piece in range(pieces):
            score = dot(key_refs[piece][:keys, :], wide)
            allowed = key_pos_ref[piece, :keys, :] <= limit
            scores.append(jnp.where(allowed, score, MASKED_SCORE))
        highest = functools.reduce(
            jnp.maximum, [jnp.max(score, axis=0, keepdims=True) for score in scores]
        )
        summed = jnp.zeros_like(highest)
        mixed = jnp.zeros((PAIR, 2 * tile), F32)
        for piece in range(pieces):
            raised = jnp.exp(scores[piece] - highest)
            summed = summed + jnp.sum(raised, axis=0, keepdims=True)
            mixed = mixed + dot(values_up[piece][:, :keys], raised.astype(BF16))
        mixed = mixed / summed
        out_ref[start : start + tile, :] = heads_back(mixed, tile).astype(BF16)
        total = highest + jnp.log(summed)
        total_ref[0, 0:1, start : start + tile] = total[:, :tile]
        total_ref[0, 1:2, start : start + tile] = total[:, tile:]


def attend_forward(queries, keys_values, key_pos, query_pos, block, causal):
    rows, width = queries.shape
    pieces = len(keys_values)
    pairs = width // PAIR
    column = pl.BlockSpec((rows, PAIR), lambda p: (0, p))
    second = pl.BlockSpec((rows, PAIR), lambda p: (0, p + pairs))
    whole_pos = pl.BlockSpec((pieces, rows, 1), lambda p: (0, 0, 0))
    row_pos = pl.BlockSpec((1, rows), lambda p: (0, 0))
    return pl.pallas_call(
        functools.partial(forward_kernel, pieces, block, causal),
        grid=(pairs,),
        in_specs=[column, whole_pos, row_pos] + [column] * pieces + [second] * pieces,
        out_specs=[column, pl.BlockSpec((1, 2, rows), lambda p: (p, 0, 0))],
        out_shape=[
            jax.ShapeDtypeStruct((rows, width), BF16),
            jax.ShapeDtypeStruct((pairs, 2, rows), F32),
        ],
        compiler_params=params(
            [((rows, PAIR), BF16)] * (2 + 2 * pieces) + [((pieces, rows, 128), F32)],
            spare=10 + 4 * (pieces > 2),
        ),
        cost_estimate=cost(18 if causal else 22),
        name="attend_forward",
    )(queries, key_pos, query_pos, *keys_values, *keys_values)


def backward_kernel(pieces, block, causal, begun, *refs):
    refs = refs[: 6 + 2 * pieces] + refs[6 + 2 * pieces + begun :]
    query_ref, out_ref, grad_ref, total_ref, key_pos_ref, query_pos_ref = refs[:6]
    key_refs = refs[6 : 6 + pieces]
    value_refs = refs[6 + pieces : 6 + 2 * pieces]
    dquery_ref, down_ref = refs[6 + 2 * pieces : 8 + 2 * pieces]
    dother_refs = refs[8 + 2 * pieces : 7 + 3 * pieces]
    dkey_ref, dvalue_ref = refs[7 + 3 * pieces :]
    rows = query_ref.shape[0]
    tile = tile_of(rows)
    scaled = query_ref[...].astype(F32) * SCALE
    query_up = scaled.T
    scaled = scaled.astype(BF16)
    grad_up = grad_ref[...].astype(F32).T
    out_up = out_ref[...].astype(F32).T
    keys_up = [ref[...].astype(F32).T.astype(BF16) for ref in key_refs]
    product_up = grad_up * out_up
    query_up = query_up.astype(BF16)
    grad_up = grad_up.astype(BF16)
    dkey_ref[...] = jnp.zeros_like(dkey_ref)
    dvalue_ref[...] = jnp.zeros_like(dvalue_ref)
    for start in range(0, rows, tile):
        stop = start + tile
        keys = key_rows(stop, rows, block, causal)
        query_wide = beside(query_up[:, start:stop])
        grad_wide = beside(grad_up[:, start:stop])
        query_tall = below(scaled[start:stop, :])
        grad_tall = below(grad_ref[start:stop, :])
        product = product_up[:, start:stop]
        centre = jnp.concatenate(
            [
                jnp.sum(product[:HEAD], axis=0, keepdims=True),
                jnp.sum(product[HEAD:], axis=0, keepdims=True),
            ],
            axis=1,
        )
        total = jnp.concatenate(
            [total_ref[0, 0:1, start:stop], total_ref[0, 1:2, start:stop]], axis=1
        )
        query_pos = query_pos_ref[:, start:stop]
        limit = jnp.concatenate([query_pos, query_pos], axis=1)
        dquery = jnp.zeros((PAIR, 2 * tile), F32)
        for piece in range(pieces):
            score = dot(key_refs[piece][:keys, :], query_wide)
            allowed = key_pos_ref[piece, :keys, :] <= limit
            probs = jnp.exp(jnp.where(allowed, score, MASKED_SCORE) - total)
            dprob = dot(value_refs[piece][:keys, :], grad_wide)
            dscore = (probs * (dprob - centre)).astype(BF16)
            dvalue_ref[piece, :keys, :] += dot(probs.astype(BF16), grad_tall)
            dkey_ref[piece, :keys, :] += dot(dscore, query_tall)
            dquery = dquery + dot(keys_up[piece][:, :keys], dscore)
        dquery_ref[start:stop, :] = (heads_back(dquery, tile) * SCALE).astype(BF16)
    down_ref[0] = dkey_ref[0]
    down_ref[1] = dvalue_ref[0]
    for piece in range(1, pieces):
        dother_refs[piece - 1][0] = dkey_ref[piece].astype(BF16)
        dother_refs[piece - 1][1] = dvalue_ref[piece].astype(BF16)


def attend_backward(
    queries, keys_values, outputs, grads, totals, key_pos, query_pos, block, causal, span, begun=()
):
    first, pairs = span
    rows, width = queries.shape
    pieces = len(keys_values)
    shift = width // PAIR
    column = pl.BlockSpec((rows, PAIR), lambda p: (0, p + first))
    second = pl.BlockSpec((rows, PAIR), lambda p: (0, p + first + shift))
    whole_pos = pl.BlockSpec((pieces, rows, 1), lambda p: (0, 0, 0))
    row_pos = pl.BlockSpec((1, rows), lambda p: (0, 0))
    both = pl.BlockSpec((2, rows, PAIR), lambda p: (0, 0, p + first))
    held = 6 + 2 * pieces
    return pl.pallas_call(
        functools.partial(backward_kernel, pieces, block, causal, len(begun)),
        grid=(pairs,),
        in_specs=[
            column,
            column,
            column,
            pl.BlockSpec((1, 2, rows), lambda p: (p + first, 0, 0)),
            whole_pos,
            row_pos,
        ]
        + [column] * pieces
        + [second] * pieces
        + [pl.BlockSpec(memory_space=pl.ANY)] * len(begun),
        out_specs=[column, both] + [both] * (pieces - 1),
        out_shape=[
            pltpu.HBM((rows, width), BF16),
            pltpu.HBM((2, rows, width), F32),
        ]
        + [pltpu.HBM((2, rows, width), BF16)] * (pieces - 1),
        input_output_aliases={held + index: index for index in range(len(begun))},
        scratch_shapes=[pltpu.VMEM((pieces, rows, PAIR), F32)] * 2,
        compiler_params=params(
            [((rows, PAIR), BF16)] * (6 + 4 * pieces) + [((pieces, rows, 128), F32)] * 2,
            spare=10 + 4 * (pieces > 2),
        ),
        cost_estimate=cost((24 if causal else 28) * pairs * PAIR / width),
        name="attend_backward",
    )(queries, outputs, grads, totals, key_pos, query_pos, *keys_values, *keys_values, *begun)


def offset(slot, size):
    return pl.multiple_of(slot * size, size)


def row_parts(place, refs):
    if len(refs) == 1:
        return [(0, refs[0][...])]
    own, one, two, near, far = [ref[...] for ref in refs]
    near_first = jnp.concatenate([near, far], axis=0)
    far_first = jnp.concatenate([far, near], axis=0)
    diagonal = jnp.where(place[4] == 0, near_first, far_first)
    return [(place[0], own), (place[1], one), (place[2], two), (place[3], diagonal)]


def times(left_ref, place, refs):
    total = None
    for slot, part in row_parts(place, refs):
        rows = part.shape[0]
        term = dot(left_ref[:, pl.ds(offset(slot, rows), rows)], part)
        total = term if total is None else total + term
    return total


def times_up(left, place, refs, store):
    for slot, part in row_parts(place, refs):
        rows = part.shape[0]
        store(pl.ds(offset(slot, rows), rows), dot_nt(left, part))


def part_specs(arrays, columns, index):
    return [pl.BlockSpec((item.shape[0], columns), lambda *at: (0, index(*at))) for item in arrays]


def fixed(shape):
    zeros = (0,) * len(shape)
    return pl.BlockSpec(shape, lambda *at: zeros)


def view(item, columns, index):
    if item.ndim == 2:
        return (item, pl.BlockSpec((item.shape[0], columns), lambda *at: (0, index)))
    return (item, pl.BlockSpec((1, item.shape[1], columns), lambda *at: (index, 0, 0)))


def run(kernel, name, place, grid, ins, outs, micros, scratch=(), spare=10):
    kept = [bool(out[3:]) for out in outs]
    outs = [out[:3] for out in outs]
    blocks = [(spec.block_shape, item.dtype) for item, spec in ins]
    blocks += [(spec.block_shape, kind) for _, kind, spec in outs]
    held = sum(bytes_of(item.shape, item.dtype) for item in scratch)
    return pl.pallas_call(
        kernel,
        grid_spec=pltpu.PrefetchScalarGridSpec(
            num_scalar_prefetch=1,
            grid=grid,
            in_specs=[spec for _, spec in ins],
            out_specs=[spec for _, _, spec in outs],
            scratch_shapes=list(scratch),
        ),
        out_shape=[
            pltpu.HBM(shape, kind) if keep else jax.ShapeDtypeStruct(shape, kind)
            for keep, (shape, kind, _) in zip(kept, outs)
        ],
        compiler_params=params(blocks, held, spare),
        cost_estimate=cost(micros),
        name=name,
    )(place, *[in_hbm(item) for item, _ in ins])


def project_kernel(place, left_ref, *refs):
    refs[-1][...] = times(left_ref, place, refs[:-1]).astype(BF16)


def project(place, left, weight, first, count, name):
    rows, depth = left[1].block_shape
    chunk = 512
    steps = count * 1024 // chunk
    base = first * 1024 // chunk
    return run(
        project_kernel,
        name,
        place,
        (steps,),
        [left]
        + list(zip(weight, part_specs(weight, chunk, lambda j, s: base + j))),
        [((rows, count * 1024), BF16, pl.BlockSpec((rows, chunk), lambda j, s: (0, j)))],
        2.5 * count,
    )[0]


def mix_kernel(parts, both, place, mixed_ref, resid_ref, norm_ref, *refs):
    out_parts = refs[:parts]
    query_parts = refs[parts : 2 * parts] if both else ()
    outs = refs[2 * parts :] if both else refs[parts:]
    summed_ref, normed_ref, low_ref = outs[:3]
    step = pl.program_id(0)
    rows, width = summed_ref.shape
    half = width // 2

    @pl.when(step < 2)
    def _():
        columns = pl.ds(offset(step, half), half)
        summed_ref[:, columns] = resid_ref[:, columns].astype(F32) + times(
            mixed_ref, place, out_parts
        )

    @pl.when(step == 1)
    def _():
        for strip in strips(rows):
            normed, _ = norm_parts(summed_ref[strip, :])
            value = normed * norm_ref[0:1, :] + norm_ref[1:2, :]
            normed_ref[strip, :] = value
            low_ref[strip, :] = value.astype(BF16)

    if both:

        @pl.when(step >= 2)
        def _():
            outs[3][...] = times(low_ref, place, query_parts).astype(BF16)


def mix(place, mixed, resid, norm, w_out, at_out, w_query, at_query, name):
    rows, width = mixed.shape
    half = width // 2
    both = w_query is not None
    ins = [(mixed, fixed(mixed.shape)), resid, (norm, fixed(norm.shape))]
    ins += zip(
        w_out, part_specs(w_out, half, lambda j, s: at_out * 2 + jnp.minimum(j, 1))
    )
    outs = [
        ((rows, width), F32, fixed((rows, width)), True),
        ((rows, width), F32, fixed((rows, width)), True),
        ((rows, width), BF16, fixed((rows, width)), True),
    ]
    if both:
        ins += zip(
            w_query,
            part_specs(w_query, half, lambda j, s: at_query * 2 + jnp.maximum(j - 2, 0)),
        )
        outs += [
            (
                (rows, width),
                BF16,
                pl.BlockSpec((rows, half), lambda j, s: (0, jnp.maximum(j - 2, 0))),
            )
        ]
    return run(
        functools.partial(mix_kernel, len(w_out), both),
        name,
        place,
        (4 if both else 2,),
        ins,
        outs,
        6.3 if both else 4,
    )


def up_parts(place, refs, packed):
    if not packed:
        return [(0, refs[0][...])]
    unpacked = []
    for slot, part in row_parts(place, refs):
        rows = part.shape[0] // 2
        unpacked.append((slot, jnp.concatenate([part[:rows], part[rows:]], axis=1)))
    return unpacked


def chunk_of(refs, step, counts, use):
    low = 0
    for ref, count in zip(refs, counts):

        @pl.when((step >= low) & (step < low + count))
        def _(ref=ref):
            use(ref)

        low += count


def feed_specs(w_in, w_out, counts, first, chunk, width):
    in_specs = part_specs(w_in, chunk, lambda j, s: s[8 + first + j])
    shift = first if len(w_in) == 1 else 0
    out_specs, start = [], 0
    for count in counts:
        out_specs.append(
            pl.BlockSpec(
                (chunk, width),
                lambda j, s, start=start, count=count: (
                    shift + jnp.clip(j - start, 0, count - 1),
                    0,
                ),
            )
        )
        start += count
    return in_specs, out_specs


def feed_first_kernel(
    sizes, counts, packed, place, low_ref, second_ref, *refs
):
    n_in, n_out, n_down, n_up = sizes
    in_refs, refs = refs[:n_in], refs[n_in:]
    out_refs, refs = refs[:n_out], refs[n_out:]
    down_refs, refs = refs[:n_down], refs[n_down:]
    up_refs, refs = refs[:n_up], refs[n_up:]
    total_ref, slope_ref, hidden_ref, aslope_ref = refs
    step = pl.program_id(0)

    @pl.when(step == 0)
    def _():
        hidden, slope = gelu_pair(times(low_ref, place, down_refs))
        hidden_ref[...] = hidden.astype(BF16)
        aslope_ref[...] = slope.astype(BF16)
        total = None
        for slot, part in up_parts(place, up_refs, packed):
            count = part.shape[0]
            term = dot(hidden_ref[:, pl.ds(offset(slot, count), count)], part)
            total = term if total is None else total + term
        total_ref[...] = second_ref[...] + 4.0 * total

    feed_chunk(place, low_ref, in_refs, out_refs, counts, total_ref, slope_ref)


def feed_chunk(place, low_ref, in_refs, out_refs, counts, total_ref, slope_ref):
    hidden, slope = gelu_pair(times(low_ref, place, in_refs))
    slope_ref[...] = slope.astype(BF16)
    hidden = hidden.astype(BF16)

    def use(ref):
        total_ref[...] += dot(hidden, ref[...])

    chunk_of(out_refs, pl.program_id(0), counts, use)


def feed_second_kernel(
    sizes, counts, steps, place, low_ref, first_ref, grad_ref, norm_ref, *refs
):
    n_in, n_out = sizes
    in_refs, refs = refs[:n_in], refs[n_in:]
    out_refs, refs = refs[:n_out], refs[n_out:]
    final_ref, d_ref, dlow_ref, dnorm_ref, slope_ref, total_ref = refs
    step = pl.program_id(0)
    rows, width = total_ref.shape

    @pl.when(step == 0)
    def _():
        total_ref[...] = first_ref[...]

    feed_chunk(place, low_ref, in_refs, out_refs, counts, total_ref, slope_ref)

    @pl.when(step == steps - 1)
    def _():
        gain, shift = norm_ref[0:1, :], norm_ref[1:2, :]
        dgain = jnp.zeros((1, width), F32)
        dshift = jnp.zeros((1, width), F32)
        for strip in strips(rows):
            normed, rstd = norm_parts(total_ref[strip, :])
            final_ref[strip, :] = (normed * gain + shift).astype(BF16)
            grad = grad_ref[strip, :].astype(F32)
            dgain += jnp.sum(grad * normed, axis=0, keepdims=True)
            dshift += jnp.sum(grad, axis=0, keepdims=True)
            back = norm_backward(normed, rstd, gain, grad)
            d_ref[strip, :] = back
            dlow_ref[strip, :] = back.astype(BF16)
        dnorm_ref[0:1, :] = dgain
        dnorm_ref[1:2, :] = dshift


CHUNK = 512


def feed_first(place, low, second, w_in, w_out, counts, w_down, at_down, w_up, at_up):
    rows, width = low.shape
    adapter = 512
    packed = len(w_up) > 1
    steps = sum(counts)
    in_specs, out_specs = feed_specs(w_in, w_out, counts, 0, CHUNK, width)
    up_columns = 512 if packed else width
    full = fixed((rows, width))
    ins = [(low, full), (second, full)]
    ins += zip(w_in, in_specs)
    ins += zip(w_out, out_specs)
    ins += zip(w_down, part_specs(w_down, adapter, lambda j, s: at_down))
    ins += zip(w_up, part_specs(w_up, up_columns, lambda j, s: at_up))
    return run(
        functools.partial(
            feed_first_kernel, (len(w_in), len(w_out), len(w_down), len(w_up)), counts, packed
        ),
        "feed_first",
        place,
        (steps,),
        ins,
        [
            ((rows, width), F32, full),
            ((rows, steps * CHUNK), BF16, pl.BlockSpec((rows, CHUNK), lambda j, s: (0, j)), True),
            ((rows, adapter), BF16, fixed((rows, adapter)), True),
            ((rows, adapter), BF16, fixed((rows, adapter)), True),
        ],
        13,
    )


def feed_second(place, low, first, grad, norm, w_in, w_out, counts, start):
    rows, width = low.shape
    steps = sum(counts)
    in_specs, out_specs = feed_specs(w_in, w_out, counts, start, CHUNK, width)
    full = fixed((rows, width))
    ins = [(low, full), (first, full), (grad, full), (norm, fixed(norm.shape))]
    ins += zip(w_in, in_specs)
    ins += zip(w_out, out_specs)
    return run(
        functools.partial(feed_second_kernel, (len(w_in), len(w_out)), counts, steps),
        "feed_second",
        place,
        (steps,),
        ins,
        [
            ((rows, width), BF16, full, True),
            ((rows, width), F32, full),
            ((rows, width), BF16, full),
            ((2, width), F32, fixed((2, width)), True),
            ((rows, steps * CHUNK), BF16, pl.BlockSpec((rows, CHUNK), lambda j, s: (0, j)), True),
        ],
        13.5,
        scratch=[pltpu.VMEM((rows, width), F32)],
    )


def feed_backward_kernel(
    sizes,
    counts,
    packed,
    steps,
    place,
    dlow_ref,
    d_ref,
    resid_ref,
    norm_ref,
    slope_ref,
    later_ref,
    aslope_ref,
    *refs,
):
    n_in, n_out, n_down, n_up, n_mix = sizes
    in_refs, refs = refs[:n_in], refs[n_in:]
    out_refs, refs = refs[:n_out], refs[n_out:]
    down_refs, refs = refs[:n_down], refs[n_down:]
    up_refs, refs = refs[:n_up], refs[n_up:]
    mix_refs, refs = refs[:n_mix], refs[n_mix:]
    dtwo_ref, dtwo_low_ref, dnorm_ref, dadapter_ref, dmixed_ref, total_ref, dhidden_ref = refs
    step = pl.program_id(0)
    rows, width = total_ref.shape

    def add(columns, value):
        total_ref[:, columns] += value

    @pl.when(step == 0)
    def _():
        total_ref[...] = d_ref[...]
        for slot, part in up_parts(place, up_refs, packed):
            count = part.shape[0]
            columns = pl.ds(offset(slot, count), count)
            back = 4.0 * dot_nt(dlow_ref[...], part)
            dadapter_ref[:, columns] = (aslope_ref[:, columns].astype(F32) * back).astype(BF16)
        times_up(dadapter_ref[...], place, down_refs, add)

    def use(ref):
        back = dot_nt(dlow_ref[...], ref[...])
        chosen = jnp.where(step < steps // 2, slope_ref[...], later_ref[...])
        dhidden_ref[...] = (chosen.astype(F32) * back).astype(BF16)

    chunk_of(out_refs, step, counts, use)
    times_up(dhidden_ref[...], place, in_refs, add)

    @pl.when(step == steps - 1)
    def _():
        finish_norm(total_ref, resid_ref, norm_ref, dtwo_ref, dtwo_low_ref, dnorm_ref)

        def keep(columns, value):
            dmixed_ref[:, columns] = value.astype(BF16)

        times_up(dtwo_low_ref[...], place, mix_refs, keep)


def finish_norm(grad_ref, resid_ref, norm_ref, d_ref, dlow_ref, dnorm_ref):
    rows, width = grad_ref.shape
    gain = norm_ref[0:1, :]
    dgain = jnp.zeros((1, width), F32)
    dshift = jnp.zeros((1, width), F32)
    for strip in strips(rows):
        grad = grad_ref[strip, :]
        normed, rstd = norm_parts(resid_ref[strip, :])
        dgain += jnp.sum(grad * normed, axis=0, keepdims=True)
        dshift += jnp.sum(grad, axis=0, keepdims=True)
        back = norm_backward(normed, rstd, gain, grad)
        d_ref[strip, :] = back
        dlow_ref[strip, :] = back.astype(BF16)
    dnorm_ref[0:1, :] = dgain
    dnorm_ref[1:2, :] = dshift


def feed_backward(
    place,
    dlow,
    d_three,
    resid,
    norm,
    slope,
    later,
    aslope,
    w_in,
    w_out,
    counts,
    w_down,
    at_down,
    w_up,
    at_up,
    w_mix,
    at_mix,
):
    rows, width = dlow.shape
    hidden = w_in[0].shape[1]
    adapter = 512
    packed = len(w_up) > 1
    chunk = CHUNK
    steps = hidden // chunk
    in_specs, out_specs = feed_specs(w_in, w_out, counts, 0, chunk, width)
    middle = steps // 2
    up_columns = 512 if packed else width
    full = fixed((rows, width))
    ins = [
        (dlow, full),
        (d_three, full),
        (resid, full),
        (norm, fixed(norm.shape)),
        (slope, pl.BlockSpec((rows, chunk), lambda j, s: (0, jnp.minimum(j, middle - 1)))),
        (later, pl.BlockSpec((rows, chunk), lambda j, s: (0, jnp.maximum(j - middle, 0)))),
        (aslope, fixed((rows, adapter))),
    ]
    ins += zip(w_in, in_specs)
    ins += zip(w_out, out_specs)
    ins += zip(w_down, part_specs(w_down, adapter, lambda j, s: at_down))
    ins += zip(w_up, part_specs(w_up, up_columns, lambda j, s: at_up))
    ins += zip(w_mix, part_specs(w_mix, width, lambda j, s: at_mix))
    return run(
        functools.partial(
            feed_backward_kernel,
            (len(w_in), len(w_out), len(w_down), len(w_up), len(w_mix)),
            counts,
            packed,
            steps,
        ),
        "feed_backward",
        place,
        (steps,),
        ins,
        [
            ((rows, width), F32, full, True),
            ((rows, width), BF16, full),
            ((2, width), F32, fixed((2, width)), True),
            ((rows, adapter), BF16, fixed((rows, adapter))),
            ((rows, width), BF16, full),
        ],
        29,
        scratch=[pltpu.VMEM((rows, width), F32), pltpu.VMEM((rows, chunk), BF16)],
    )


def norm_step_kernel(parts, place, dquery_ref, d_ref, resid_ref, norm_ref, *refs):
    query_refs, refs = refs[:parts], refs[parts:]
    out_refs, refs = refs[:parts], refs[parts:]
    done_ref, done_low_ref, dnorm_ref, dmixed_ref, total_ref = refs
    step = pl.program_id(0)

    @pl.when(step == 0)
    def _():
        def add(columns, value):
            total_ref[:, columns] = d_ref[:, columns] + value

        times_up(dquery_ref[...], place, query_refs, add)
        finish_norm(total_ref, resid_ref, norm_ref, done_ref, done_low_ref, dnorm_ref)

    @pl.when(step == 1)
    def _():
        def keep(columns, value):
            dmixed_ref[:, columns] = value.astype(BF16)

        times_up(done_low_ref[...], place, out_refs, keep)


def norm_step(place, dquery, d_two, resid, norm, w_query, at_query, w_out, at_out):
    rows, width = dquery.shape
    full = fixed((rows, width))
    ins = [(dquery, full), (d_two, full), (resid, full), (norm, fixed(norm.shape))]
    ins += zip(w_query, part_specs(w_query, width, lambda j, s: at_query))
    ins += zip(w_out, part_specs(w_out, width, lambda j, s: at_out))
    return run(
        functools.partial(norm_step_kernel, len(w_query)),
        "norm_step",
        place,
        (2,),
        ins,
        [
            ((rows, width), F32, full, True),
            ((rows, width), BF16, full),
            ((2, width), F32, fixed((2, width)), True),
            ((rows, width), BF16, full),
        ],
        6.6,
        scratch=[pltpu.VMEM((rows, width), F32)],
    )


def inputs_back_kernel(lefts, parts, extra, place, *refs):
    left_refs, refs = refs[:lefts], refs[lefts:]
    part_refs, refs = refs[:parts], refs[parts:]
    if extra:
        extra_ref, refs = refs[0], refs[1:]
    out_ref, total_ref = refs
    step = pl.program_id(0)
    width = total_ref.shape[1]

    @pl.when(step == 0)
    def _():
        if extra == "base":
            total_ref[...] = extra_ref[...]
        else:
            total_ref[...] = jnp.zeros_like(total_ref)
        if extra == "beside":
            out_ref[:, :width] = extra_ref[...]

    def add(columns, value):
        total_ref[:, columns] += value

    for which in range(lefts):

        @pl.when(step == which)
        def _(which=which):
            left = left_refs[which][...]
            times_up(left.reshape(left.shape[-2:]), place, part_refs, add)

    @pl.when(step == lefts - 1)
    def _():
        out_ref[:, out_ref.shape[1] - width :] = total_ref[...].astype(BF16)


def inputs_back(place, lefts, weight, blocks, extra, item, name):
    depth = lefts[0][1].block_shape[-1]
    rows = lefts[0][1].block_shape[-2]
    width = 1024
    first = blocks[0]
    strides = {blocks[k + 1] - blocks[k] for k in range(len(blocks) - 1)}

    def at(j, s):
        index = first
        for k in range(1, len(blocks)):
            index = jnp.where(j == k, blocks[k], index)
        return first + j if strides == {1} else index

    ins = list(lefts)
    ins += zip(weight, part_specs(weight, depth, at))
    if extra:
        ins += [(item, fixed((rows, width)))]
    size = 2 * width if extra == "beside" else width
    return run(
        functools.partial(inputs_back_kernel, len(lefts), len(weight), extra),
        name,
        place,
        (len(lefts),),
        ins,
        [((rows, size), BF16, fixed((rows, size)))],
        3 * len(lefts) * depth / width,
        scratch=[pltpu.VMEM((rows, width), F32)],
    )[0]


def laid_out_kernel(slots, item_ref, *refs):
    out_ref = refs[-1]
    out_ref[slots[0]] = item_ref[0]
    for index, ref in enumerate(refs[:-1], 1):
        out_ref[slots[index]] = ref[...]


def laid_out(slots, item, parts):
    part = parts[0].shape
    return run(
        laid_out_kernel,
        "laid_out",
        slots,
        (1,),
        [(item, pl.BlockSpec((1,) + part, lambda j, s: (s[0], 0, 0)))]
        + [(piece, fixed(part)) for piece in parts],
        [(item.shape, item.dtype, fixed(item.shape))],
        1.5,
    )[0]


def swap_pairs(size, bit):
    return [(index, index ^ bit) for index in range(size)]


def by_core(even, odd):
    return [
        (d * 8 + s, (d ^ (odd if s % 2 else even)) * 8 + s) for d in range(4) for s in range(8)
    ]


def after(item, *others):
    return lax.optimization_barrier((item,) + others)[0]


def gather_first(own):
    return (own, lax.ppermute(own, ("dp", "seq"), by_core(1, 2)))


def gather_swap(parts, *others):
    return parts + (lax.ppermute(after(parts[1], *others), "seq", swap_pairs(8, 1)),)


def gather_near(parts, core, *others):
    one = parts[1]
    half = one.shape[0] // 2
    half_one = lax.dynamic_slice_in_dim(after(one, *others), core * half, half, 0)
    return parts + (lax.ppermute(half_one, ("dp", "seq"), by_core(2, 1)),)


def gather_far(parts, *others):
    return parts + (lax.ppermute(after(parts[3], *others), "seq", swap_pairs(8, 1)),)


def gather_dp(item):
    return (lax.all_gather(item, "dp", axis=0, tiled=True),)


def row_blocks(value, size):
    return [value[start : start + size] for start in range(0, value.shape[0], size)]


def wgrad_kernel(fresh, split, scales, extra, place, *refs):
    count = len(fresh)
    left_refs, right_refs = refs[:count], refs[count : 2 * count]
    outs, up_ref = refs[2 * count + extra : -1], refs[-1]
    step = pl.program_id(0)
    wide = outs[0].shape[1]
    if extra:

        @pl.when(step == count)
        def _():
            rows = jnp.concatenate([ref[...] for ref in refs[2 * count : 2 * count + extra]])
            filler = jnp.zeros((128 - rows.shape[0], rows.shape[1]), F32)
            columns = jnp.concatenate([rows, filler], axis=0).T.astype(BF16)
            blocks = row_blocks(columns, 32)
            even = jnp.concatenate(blocks[0::2], axis=0)
            odd = jnp.concatenate(blocks[1::2], axis=0)
            outs[0][:, :128] = jnp.where(place[4] == 0, odd, even)
            outs[1][:, :128] = jnp.where(place[4] == 0, even, odd)
            for out in outs:
                out[:, 128:256] = jnp.zeros(even.shape, BF16)

    for which in range(count):

        @pl.when(step == which)
        def _(which=which):
            right = right_refs[which][...]
            right = right.reshape(right.shape[-2:])
            tall = left_refs[which].shape[-1]
            if fresh[which]:
                left = left_refs[which][...]
                up_ref[:tall, :] = left.reshape(left.shape[-2:]).T
            value = dot(up_ref[:tall, :], right)
            value = (value * scales[which] if scales[which] != 1.0 else value).astype(BF16)
            own = tall // 32
            blocks = row_blocks(value, own)
            if split:
                even = jnp.concatenate(blocks[0::2], axis=0)
                odd = jnp.concatenate(blocks[1::2], axis=0)
                outs[0][...] = jnp.where(place[4] == 0, odd, even)
                outs[1][...] = jnp.where(place[4] == 0, even, odd)
                return
            folds = right.shape[1] // wide
            for index, item in enumerate(blocks):
                at = (index % 8 * 4 + index // 8) * own * folds
                for fold in range(folds):
                    low = at + fold * own
                    outs[0][low : low + own, :] = item[:, fold * wide : (fold + 1) * wide]


def wgrad(place, lefts, rights, wide, split, scales, name, extra=()):
    fresh = []
    for index, (item, spec) in enumerate(lefts):
        before = lefts[index - 1] if index else (None, None)
        fresh.append(item is not before[0] or spec is not before[1])
    rows, tall = lefts[0][1].block_shape[-2:]
    high = tall // 2 if split else tall
    spec = pl.BlockSpec((high, wide), lambda j, s: (0, j))
    more = 1 if extra else 0
    return run(
        functools.partial(wgrad_kernel, tuple(fresh), split, scales, len(extra)),
        name,
        place,
        (len(lefts) + more,),
        list(lefts) + list(rights) + [(item, fixed(item.shape)) for item in extra],
        [((high, wide * len(lefts) + 256 * more), BF16, spec, True)] * (2 if split else 1),
        1.6 * len(lefts) * wide / 1024,
        scratch=[pltpu.VMEM((tall, rows), BF16)],
    )


def take(item, index, axis):
    return lax.dynamic_index_in_dim(item, index, axis, keepdims=False)


def add(kept, received, kind=BF16):
    return (kept.astype(F32) + received.astype(F32)).astype(kind)


def sum_over(partial, name):
    return lax.psum_scatter(partial, name, scatter_dimension=0, tiled=True)


class Scatter:
    def __init__(self, send, keep):
        here, there = lax.axis_index("dp"), lax.axis_index("seq")
        self.x, self.y = here % 2, here // 2
        self.low, self.high = (there // 2) % 2, there // 4
        self.send, self.keep = send, keep
        self.width = keep.shape[1]

    def core(self):
        received = lax.ppermute(self.send, "seq", swap_pairs(8, 1))
        item = add(self.keep, received).reshape(2, 2, 128, self.width)
        self.one, self.two = item[..., : self.width // 2], item[..., self.width // 2 :]
        return self.one

    def plane_one(self):
        x, y = self.x, self.y
        from_x = lax.ppermute(take(self.one, 1 - x, 1), "dp", swap_pairs(4, 1))
        from_y = lax.ppermute(take(self.two, 1 - y, 0), "dp", swap_pairs(4, 2))
        self.one = add(take(self.one, x, 1), from_x)
        self.two = add(take(self.two, y, 0), from_y)
        return self.one, self.two

    def plane_two(self):
        x, y = self.x, self.y
        from_y = lax.ppermute(take(self.one, 1 - y, 0), "dp", swap_pairs(4, 2))
        from_x = lax.ppermute(take(self.two, 1 - x, 0), "dp", swap_pairs(4, 1))
        one = add(take(self.one, y, 0), from_y)
        two = add(take(self.two, x, 0), from_x)
        self.item = jnp.concatenate([one, two], axis=1)
        return self.item

    def z_one(self):
        self.item = self.item.reshape(2, 2, 32, self.width)
        received = lax.ppermute(take(self.item, 1 - self.low, 1), "seq", swap_pairs(8, 2))
        self.item = add(take(self.item, self.low, 1), received)
        return self.item

    def z_two(self):
        received = lax.ppermute(take(self.item, 1 - self.high, 0), "seq", swap_pairs(8, 4))
        self.item = add(take(self.item, self.high, 0), received, F32)
        return self.item


def sum_all(partial):
    return lax.psum_scatter(
        partial.astype(BF16), ("dp", "seq"), scatter_dimension=0, tiled=True
    ).astype(F32)


def body(
    target,
    source,
    target_len,
    source_len,
    self_query,
    self_key,
    self_value,
    self_output,
    cross_query,
    cross_key,
    cross_value,
    cross_output,
    feed_in,
    feed_out,
    adapter_down,
    adapter_up,
    self_gain,
    self_shift,
    cross_gain,
    cross_shift,
    final_gain,
    final_shift,
    cotangent,
):
    block, seqs, width = target.shape
    dp, seq = lax.axis_size("dp"), lax.axis_size("seq")
    group = seq // seqs
    rows = seqs * block
    here, there = lax.axis_index("dp"), lax.axis_index("seq")
    inner, which = there % group, there // group
    core = there % 2
    halving = dp == 4 and seq == 8
    apart = [[start + group * step for step in range(seqs)] for start in range(group)]

    def to_sequence(item):
        return lax.all_to_all(
            item.swapaxes(0, 1), "seq", 0, 0, axis_index_groups=apart, tiled=True
        ).reshape(rows, item.shape[-1])

    slots = jnp.stack([which ^ bit for bit in range(seqs)]).astype(jnp.int32)

    def send_back(item):
        item = item.reshape(seqs, block, item.shape[-1])
        parts = [item]
        for bit in range(1, seqs):
            pairs = [(index, (index // group ^ bit) * group + index % group) for index in range(seq)]
            parts.append(lax.ppermute(take(item, which ^ bit, 0), "seq", pairs))
        return parts

    def set_down(parts, *others):
        item, *parts = lax.optimization_barrier((*parts, *others))[: len(parts)]
        return laid_out(slots, item, parts).swapaxes(0, 1)

    def near(shift):
        return [
            (k * group + c, k * group + (c + shift) % group)
            for k in range(seqs)
            for c in range(group)
        ]

    def spread(item):
        return [item] + [lax.ppermute(item, "seq", near(-s)) for s in range(1, group)]

    def collect(own, others):
        for shift, other in enumerate(others, 1):
            own = own + lax.ppermute(other, "seq", near(shift)).astype(F32)
        return own.astype(BF16)

    own_inputs, own_memory = to_sequence(target), to_sequence(source)
    inputs, memory = view(own_inputs, width, 0), view(own_memory, width, 0)
    grad_out = to_sequence(cotangent)
    vectors = jnp.stack([self_gain, self_shift, cross_gain, cross_shift, final_gain, final_shift])
    if halving:
        one = jnp.where(core == 0, here ^ 1, here ^ 2)
        two = jnp.where(core == 0, here ^ 2, here ^ 1)
        diagonal = here ^ 3
        chunks = [item * 2 + part for item in (here, one, two) for part in (0, 1)]
        chunks += [diagonal * 2 + core, diagonal * 2 + 1 - core]
        place = jnp.stack([here, one, two, diagonal, core, core, core, core] + chunks)
        first_group = jnp.concatenate(
            [self_query, self_key, self_value, cross_key, cross_value], axis=1
        )
        half = width // 2
        up_packed = jnp.concatenate([adapter_up[:, :half], adapter_up[:, half:]], axis=0)
        second_group = jnp.concatenate(
            [self_output, cross_query, cross_output, adapter_down, up_packed], axis=1
        )
        vector_parts = [vectors] + [
            lax.ppermute(vectors, "dp", swap_pairs(4, bit)) for bit in (1, 2, 3)
        ]
        w_self = gather_swap(gather_first(first_group))
        w_self = gather_far(
            gather_near(w_self, core, own_inputs, second_group, *vector_parts)
        )
        w_mid = gather_swap(gather_first(after(second_group, w_self[3])))
        w_in = gather_first(after(feed_in, w_mid[1]))
        at_q, at_kv, at_ckv = (w_self, 0), (w_self, 1), (w_self, 3)
        parts = jnp.stack(vector_parts)
        vectors = jnp.concatenate([take(parts, here ^ slot, 0) for slot in range(4)], axis=1)
        counts_first, counts_second = (2, 2), (2, 1, 1)
    else:
        steps = feed_in.shape[1] // CHUNK
        place = jnp.stack([jnp.int32(0)] * 8 + [jnp.int32(j) for j in range(steps)])
        at_q = (gather_dp(self_query), 0)
        at_kv = (gather_dp(jnp.concatenate([self_key, self_value], axis=1)), 0)
        at_o, at_cq = (gather_dp(self_output), 0), (gather_dp(cross_query), 0)
        at_ckv = (gather_dp(jnp.concatenate([cross_key, cross_value], axis=1)), 0)
        at_co = (gather_dp(cross_output), 0)
        w_in, w_out = gather_dp(feed_in), gather_dp(feed_out)
        at_down, at_up = (gather_dp(adapter_down), 0), (gather_dp(adapter_up), 0)
        vectors = lax.all_gather(vectors, "dp", axis=1, tiled=True)
        out_first = out_second = w_out
        counts_first, counts_second = (steps // 2,), (steps - steps // 2,)
    place = place.astype(jnp.int32)
    vectors = vectors.astype(F32)
    norm_one, norm_two, norm_three = vectors[0:2], vectors[2:4], vectors[4:6]

    local = jnp.arange(rows, dtype=jnp.int32)

    def positions(place_in_group):
        return (local // block * group + place_in_group) * block + local % block

    target_limit = take(target_len, which, 0)
    source_limit = take(source_len, which, 0)
    key_pos = jnp.stack([positions((inner + shift) % group) for shift in range(group)])
    self_keys = jnp.where(key_pos < target_limit, key_pos, NEVER)[..., None]
    cross_keys = jnp.where(key_pos < source_limit, key_pos, NEVER)[..., None]
    self_rows = positions(inner)[None]
    cross_rows = jnp.full((1, rows), ALWAYS, jnp.int32)

    kv_own = project(place, inputs, *at_kv, 2, "self_kv")
    kv_all = spread(kv_own)
    queries = project(place, inputs, *at_q, 1, "self_q")
    if halving:
        w_mid = gather_near(w_mid, core, queries)
        queries = after(queries, w_mid[1])
    mixed, totals = attend_forward(queries, kv_all, self_keys, self_rows, block, True)
    ckv_own = project(
        place, (after(own_memory, mixed), memory[1]), *at_ckv, 2, "cross_kv"
    )
    ckv_all = spread(ckv_own)
    mixed = after(mixed, ckv_own)
    if halving:
        w_mid = gather_far(w_mid, mixed)
        w_out = gather_first(after(feed_out, mixed))
        at_o, at_cq, at_co = (w_mid, 0), (w_mid, 1), (w_mid, 2)
        at_down, at_up = (w_mid, 6), (w_mid, 7)
    resid_one, first, first_low, cross_q = mix(
        place, mixed, inputs, norm_one, *at_o, *at_cq, "mix_self"
    )
    if halving:
        w_in = gather_near(gather_swap(w_in, cross_q), core, cross_q)
        cross_q = after(cross_q, w_in[1])
    cross_mixed, cross_totals = attend_forward(
        cross_q, ckv_all, cross_keys, cross_rows, block, False
    )
    if halving:
        w_in = gather_far(w_in, cross_mixed)
        w_out = gather_far(gather_near(gather_swap(w_out, cross_mixed), core, cross_mixed))
        out_first, out_second = w_out[:2], w_out[2:]
    cross_mixed = after(cross_mixed, grad_out)
    resid_two, second, second_low = mix(
        place, cross_mixed, view(first, width, 0), norm_two, *at_co, None, None, "mix_cross"
    )
    partial, slope, hidden, adapter_slope = feed_first(
        place, second_low, second, w_in, out_first, counts_first, *at_down, *at_up
    )
    final, d_three, d_branch, d_norm_three, later = feed_second(
        place,
        second_low,
        partial,
        grad_out,
        norm_three,
        w_in,
        out_second,
        counts_second,
        sum(counts_first),
    )
    output = send_back(final)

    d_two, d_two_low, d_norm_two, d_adapter, d_cross = feed_backward(
        place,
        d_branch,
        d_three,
        resid_two,
        norm_two,
        slope,
        later,
        adapter_slope,
        w_in,
        w_out,
        counts_first + counts_second if halving else (steps,),
        *at_down,
        *at_up,
        *at_co,
    )

    d_two_low = after(d_two_low, *output[1:])

    def whole(item, layer=0):
        return view(item, item.shape[-1], layer)

    pairs = width // PAIR
    if halving:
        half = width // 2
        left = whole(cross_mixed)
        early = wgrad(
            place,
            [left, left, whole(second_low), whole(hidden)],
            [view(d_two_low, half, 0), view(d_two_low, half, 1), whole(d_adapter), whole(d_branch)],
            half,
            False,
            (1.0, 1.0, 1.0, 4.0),
            "wgrad_early",
        )[0]
        d_cross = after(d_cross, early)
        early = sum_over(early, "seq")
    d_cq, *d_ckv = attend_backward(
        cross_q,
        ckv_all,
        cross_mixed,
        d_cross,
        cross_totals,
        cross_keys,
        cross_rows,
        block,
        False,
        (0, pairs),
    )
    output = set_down(output, d_cq)
    d_one, d_one_low, d_norm_one, d_mixed = norm_step(
        place, d_cq, d_two, resid_one, norm_one, *at_cq, *at_o
    )
    d_ckv = collect(after(d_ckv[0], d_one_low), d_ckv[1:])
    grad_source = inputs_back(
        place,
        [whole(d_ckv, 0), whole(d_ckv, 1)],
        at_ckv[0],
        [at_ckv[1], at_ckv[1] + 1],
        None,
        None,
        "source_back",
    )
    d_ckv = after(d_ckv, grad_source)
    grad_source = send_back(grad_source)
    if halving:
        d_one_low = after(d_one_low, early)
        early = sum_over(early, "dp").astype(F32)
        inner_sums = Scatter(
            *wgrad(
                place,
                [memory, memory, whole(mixed), whole(first_low)],
                [whole(d_ckv, 0), whole(d_ckv, 1), whole(d_one_low), whole(d_cq)],
                width,
                True,
                (1.0,) * 4,
                "wgrad_inner",
                [d_norm_one, d_norm_two, d_norm_three],
            )
        )
    if halving:
        d_mixed = after(d_mixed, inner_sums.core())
    else:
        d_mixed = after(d_mixed, grad_source[0])

    begun = ()
    split = pairs * 7 // 8
    for span in ((0, split), (split, pairs - split)):
        begun = attend_backward(
            queries,
            kv_all,
            mixed,
            d_mixed,
            totals,
            self_keys,
            self_rows,
            block,
            True,
            span,
            begun,
        )
        if halving and span[0] == 0:
            d_mixed = after(d_mixed, begun[0], inner_sums.plane_one(), *grad_source[1:3])
    d_q, *d_kv = begun
    d_kv = collect(d_kv[0], d_kv[1:])
    at_self = at_q if halving else ((jnp.concatenate([at_q[0][0], at_kv[0][0]], axis=1),), 0)
    grad_target = inputs_back(
        place,
        [whole(d_q), whole(d_kv, 0), whole(d_kv, 1)],
        at_self[0],
        [at_self[1] + index for index in range(3)],
        "base",
        d_one,
        "target_back",
    )
    d_q = after(d_q, grad_target)
    grad_target = send_back(grad_target)
    if not halving:
        grad_source = set_down(grad_source)
        grad_target = set_down(grad_target)
    if halving:
        inner_sums.one, inner_sums.two, _ = lax.optimization_barrier(
            (inner_sums.one, inner_sums.two, grad_target[0])
        )
        late = Scatter(
            *wgrad(
                place,
                [inputs] * 3,
                [whole(d_q), whole(d_kv, 0), whole(d_kv, 1)],
                width,
                True,
                (1.0,) * 3,
                "wgrad_self",
            )
        )
        grad_source = set_down(grad_source, late.send)
        late.keep = after(late.keep, inner_sums.plane_two(), grad_source, *grad_target[1:])
        late.core()
        late.plane_one()
        late.one, late.two, *_ = lax.optimization_barrier(
            (late.one, late.two, inner_sums.z_one(), *grad_target)
        )
        grad_target = set_down(grad_target, late.one)
        late.plane_two()
        late.item = after(late.item, grad_target, inner_sums.z_two())
        late.z_one()
        late.z_two()
        grad_co, grad_down = early[:, :width], early[:, width : width + half]
        lifted = early[:, width + half :]
        folded = lifted.shape[0] // 2
        grad_up = jnp.concatenate([lifted[:folded], lifted[folded:]], axis=1)
        norm_sums = inner_sums.item[:, 4 * width : 4 * width + 6].T
        grad_ck, grad_cv, grad_o, grad_cq = [
            inner_sums.item[:, index * width : (index + 1) * width] for index in range(4)
        ]
        grad_q, grad_k, grad_v = [
            late.item[:, index * width : (index + 1) * width] for index in range(3)
        ]
    else:
        norm_sums = jnp.concatenate([d_norm_one, d_norm_two, d_norm_three], axis=0)
        norm_sums = lax.psum_scatter(norm_sums, ("dp", "seq"), scatter_dimension=1, tiled=True)
        grad_down = sum_all(dot_tn(second_low, d_adapter))
        grad_up = sum_all(4.0 * dot_tn(hidden, d_branch))
        grad_co = sum_all(dot_tn(cross_mixed, d_two_low))
        grad_o = sum_all(dot_tn(mixed, d_one_low))
        grad_cq = sum_all(dot_tn(first_low, d_cq))
        grad_ck = sum_all(dot_tn(own_memory, d_ckv[0]))
        grad_cv = sum_all(dot_tn(own_memory, d_ckv[1]))
        grad_q = sum_all(dot_tn(own_inputs, d_q))
        grad_k = sum_all(dot_tn(own_inputs, d_kv[0]))
        grad_v = sum_all(dot_tn(own_inputs, d_kv[1]))
    return (
        output,
        grad_target,
        grad_source,
        grad_q,
        grad_k,
        grad_v,
        grad_o,
        grad_cq,
        grad_ck,
        grad_cv,
        grad_co,
        grad_down,
        grad_up,
        *[norm_sums[index] for index in range(6)],
    )


def solution(mesh):
    tokens = P("seq", "dp", None)
    rows = P("dp", None)
    vector = P("dp")
    both = P(("dp", "seq"), None)
    return jax.shard_map(
        body,
        mesh=mesh,
        in_specs=(tokens, tokens, vector, vector) + (rows,) * 12 + (vector,) * 6 + (tokens,),
        out_specs=(tokens,) * 3 + (both,) * 10 + (P(("dp", "seq")),) * 6,
        check_vma=False,
    )
```

```python
import functools

import jax
import jax.numpy as jnp
from jax import lax
from jax.experimental import pallas as pl
from jax.experimental.pallas import tpu as pltpu
from jax.sharding import PartitionSpec as P

HEAD = 64
PAIR = 2 * HEAD
SCALE = HEAD ** (-0.5)
MASKED_SCORE = -1e30
NEVER = 2**30
ALWAYS = 2**29
F32 = jnp.float32
BF16 = jnp.bfloat16
STRIP = 128
ROOT_HALF = 0.7071067811865476
PDF_SCALE = 0.3989422804014327


def dot(left, right):
    return jnp.dot(left, right, preferred_element_type=F32)


def dot_tn(left, right):
    return lax.dot_general(left, right, (((0,), (0,)), ((), ())), preferred_element_type=F32)


def dot_nt(left, right):
    return lax.dot_general(left, right, (((1,), (1,)), ((), ())), preferred_element_type=F32)


def gelu_pair(inputs):
    below_it = 0.5 * (1.0 + lax.erf(inputs * ROOT_HALF))
    density = PDF_SCALE * jnp.exp(-0.5 * inputs * inputs)
    return inputs * below_it, below_it + inputs * density


def norm_parts(inputs):
    centre = jnp.mean(inputs, axis=-1, keepdims=True)
    centred = inputs - centre
    spread = jnp.mean(centred * centred, axis=-1, keepdims=True)
    rstd = lax.rsqrt(spread + 1e-05)
    return centred * rstd, rstd


def norm_backward(normed, rstd, gain, grad):
    inner = grad * gain
    mean_one = jnp.mean(inner, axis=-1, keepdims=True)
    mean_two = jnp.mean(inner * normed, axis=-1, keepdims=True)
    return rstd * (inner - mean_one - normed * mean_two)


def strips(rows):
    return [slice(start, start + STRIP) for start in range(0, rows, STRIP)]


MIB = 1024 * 1024


def bytes_of(shape, kind):
    size = jnp.dtype(kind).itemsize
    for extent in shape:
        size *= extent
    return size


def in_hbm(item):
    if item.size * item.dtype.itemsize < 256 * 1024:
        return item
    return pltpu.with_memory_space_constraint(item, pltpu.HBM)


def params(blocks, scratch=0, spare=10):
    limit = 2 * sum(bytes_of(shape, kind) for shape, kind in blocks) + scratch + spare * MIB
    return pltpu.CompilerParams(vmem_limit_bytes=min(limit, 60 * MIB))


def cost(micros):
    return pl.CostEstimate(
        flops=int(micros * 1.15e9), bytes_accessed=int(micros * 3.6e6), transcendentals=0
    )


def tile_of(rows):
    return 128 if rows % 128 == 0 else rows


def key_rows(tile_end, rows, block, causal):
    if not causal:
        return rows
    return min(rows, ((tile_end - 1) // block + 1) * block)


def beside(top):
    row = lax.broadcasted_iota(jnp.int32, top.shape, 0)
    zero = jnp.zeros_like(top)
    return jnp.concatenate(
        [jnp.where(row < HEAD, top, zero), jnp.where(row < HEAD, zero, top)], axis=1
    )


def below(side):
    lane = lax.broadcasted_iota(jnp.int32, side.shape, 1)
    zero = jnp.zeros_like(side)
    return jnp.concatenate(
        [jnp.where(lane < HEAD, side, zero), jnp.where(lane < HEAD, zero, side)], axis=0
    )


def heads_back(wide, tile):
    return jnp.concatenate([wide[:HEAD, :tile], wide[HEAD:, tile:]], axis=0).T


def forward_kernel(pieces, block, causal, *refs):
    query_ref, key_pos_ref, query_pos_ref = refs[:3]
    key_refs = refs[3 : 3 + pieces]
    value_refs = refs[3 + pieces : 3 + 2 * pieces]
    out_ref, total_ref = refs[3 + 2 * pieces :]
    rows = query_ref.shape[0]
    tile = tile_of(rows)
    scaled = query_ref[...].astype(F32) * SCALE
    query_up = scaled.T.astype(BF16)
    values_up = [ref[...].astype(F32).T.astype(BF16) for ref in value_refs]
    for start in range(0, rows, tile):
        keys = key_rows(start + tile, rows, block, causal)
        wide = beside(query_up[:, start : start + tile])
        query_pos = query_pos_ref[:, start : start + tile]
        limit = jnp.concatenate([query_pos, query_pos], axis=1)
        scores = []
        for piece in range(pieces):
            score = dot(key_refs[piece][:keys, :], wide)
            allowed = key_pos_ref[piece, :keys, :] <= limit
            scores.append(jnp.where(allowed, score, MASKED_SCORE))
        highest = functools.reduce(
            jnp.maximum, [jnp.max(score, axis=0, keepdims=True) for score in scores]
        )
        summed = jnp.zeros_like(highest)
        mixed = jnp.zeros((PAIR, 2 * tile), F32)
        for piece in range(pieces):
            raised = jnp.exp(scores[piece] - highest)
            summed = summed + jnp.sum(raised, axis=0, keepdims=True)
            mixed = mixed + dot(values_up[piece][:, :keys], raised.astype(BF16))
        mixed = mixed / summed
        out_ref[start : start + tile, :] = heads_back(mixed, tile).astype(BF16)
        total = highest + jnp.log(summed)
        total_ref[0, 0:1, start : start + tile] = total[:, :tile]
        total_ref[0, 1:2, start : start + tile] = total[:, tile:]


def attend_forward(queries, keys_values, key_pos, query_pos, block, causal):
    rows, width = queries.shape
    pieces = len(keys_values)
    pairs = width // PAIR
    column = pl.BlockSpec((rows, PAIR), lambda p: (0, p))
    second = pl.BlockSpec((rows, PAIR), lambda p: (0, p + pairs))
    whole_pos = pl.BlockSpec((pieces, rows, 1), lambda p: (0, 0, 0))
    row_pos = pl.BlockSpec((1, rows), lambda p: (0, 0))
    return pl.pallas_call(
        functools.partial(forward_kernel, pieces, block, causal),
        grid=(pairs,),
        in_specs=[column, whole_pos, row_pos] + [column] * pieces + [second] * pieces,
        out_specs=[column, pl.BlockSpec((1, 2, rows), lambda p: (p, 0, 0))],
        out_shape=[
            jax.ShapeDtypeStruct((rows, width), BF16),
            jax.ShapeDtypeStruct((pairs, 2, rows), F32),
        ],
        compiler_params=params(
            [((rows, PAIR), BF16)] * (2 + 2 * pieces) + [((pieces, rows, 128), F32)],
            spare=10 + 4 * (pieces > 2),
        ),
        cost_estimate=cost(18 if causal else 22),
        name="attend_forward",
    )(queries, key_pos, query_pos, *keys_values, *keys_values)


def backward_kernel(pieces, block, causal, begun, *refs):
    refs = refs[: 6 + 2 * pieces] + refs[6 + 2 * pieces + begun :]
    query_ref, out_ref, grad_ref, total_ref, key_pos_ref, query_pos_ref = refs[:6]
    key_refs = refs[6 : 6 + pieces]
    value_refs = refs[6 + pieces : 6 + 2 * pieces]
    dquery_ref, down_ref = refs[6 + 2 * pieces : 8 + 2 * pieces]
    dother_refs = refs[8 + 2 * pieces : 7 + 3 * pieces]
    dkey_ref, dvalue_ref = refs[7 + 3 * pieces :]
    rows = query_ref.shape[0]
    tile = tile_of(rows)
    scaled = query_ref[...].astype(F32) * SCALE
    query_up = scaled.T
    scaled = scaled.astype(BF16)
    grad_up = grad_ref[...].astype(F32).T
    out_up = out_ref[...].astype(F32).T
    keys_up = [ref[...].astype(F32).T.astype(BF16) for ref in key_refs]
    product_up = grad_up * out_up
    query_up = query_up.astype(BF16)
    grad_up = grad_up.astype(BF16)
    dkey_ref[...] = jnp.zeros_like(dkey_ref)
    dvalue_ref[...] = jnp.zeros_like(dvalue_ref)
    for start in range(0, rows, tile):
        stop = start + tile
        keys = key_rows(stop, rows, block, causal)
        query_wide = beside(query_up[:, start:stop])
        grad_wide = beside(grad_up[:, start:stop])
        query_tall = below(scaled[start:stop, :])
        grad_tall = below(grad_ref[start:stop, :])
        product = product_up[:, start:stop]
        centre = jnp.concatenate(
            [
                jnp.sum(product[:HEAD], axis=0, keepdims=True),
                jnp.sum(product[HEAD:], axis=0, keepdims=True),
            ],
            axis=1,
        )
        total = jnp.concatenate(
            [total_ref[0, 0:1, start:stop], total_ref[0, 1:2, start:stop]], axis=1
        )
        query_pos = query_pos_ref[:, start:stop]
        limit = jnp.concatenate([query_pos, query_pos], axis=1)
        dquery = jnp.zeros((PAIR, 2 * tile), F32)
        for piece in range(pieces):
            score = dot(key_refs[piece][:keys, :], query_wide)
            allowed = key_pos_ref[piece, :keys, :] <= limit
            probs = jnp.exp(jnp.where(allowed, score, MASKED_SCORE) - total)
            dprob = dot(value_refs[piece][:keys, :], grad_wide)
            dscore = (probs * (dprob - centre)).astype(BF16)
            dvalue_ref[piece, :keys, :] += dot(probs.astype(BF16), grad_tall)
            dkey_ref[piece, :keys, :] += dot(dscore, query_tall)
            dquery = dquery + dot(keys_up[piece][:, :keys], dscore)
        dquery_ref[start:stop, :] = (heads_back(dquery, tile) * SCALE).astype(BF16)
    down_ref[0] = dkey_ref[0]
    down_ref[1] = dvalue_ref[0]
    for piece in range(1, pieces):
        dother_refs[piece - 1][0] = dkey_ref[piece].astype(BF16)
        dother_refs[piece - 1][1] = dvalue_ref[piece].astype(BF16)


def attend_backward(
    queries, keys_values, outputs, grads, totals, key_pos, query_pos, block, causal, span, begun=()
):
    first, pairs = span
    rows, width = queries.shape
    pieces = len(keys_values)
    shift = width // PAIR
    column = pl.BlockSpec((rows, PAIR), lambda p: (0, p + first))
    second = pl.BlockSpec((rows, PAIR), lambda p: (0, p + first + shift))
    whole_pos = pl.BlockSpec((pieces, rows, 1), lambda p: (0, 0, 0))
    row_pos = pl.BlockSpec((1, rows), lambda p: (0, 0))
    both = pl.BlockSpec((2, rows, PAIR), lambda p: (0, 0, p + first))
    held = 6 + 2 * pieces
    return pl.pallas_call(
        functools.partial(backward_kernel, pieces, block, causal, len(begun)),
        grid=(pairs,),
        in_specs=[
            column,
            column,
            column,
            pl.BlockSpec((1, 2, rows), lambda p: (p + first, 0, 0)),
            whole_pos,
            row_pos,
        ]
        + [column] * pieces
        + [second] * pieces
        + [pl.BlockSpec(memory_space=pl.ANY)] * len(begun),
        out_specs=[column, both] + [both] * (pieces - 1),
        out_shape=[
            pltpu.HBM((rows, width), BF16),
            pltpu.HBM((2, rows, width), F32),
        ]
        + [pltpu.HBM((2, rows, width), BF16)] * (pieces - 1),
        input_output_aliases={held + index: index for index in range(len(begun))},
        scratch_shapes=[pltpu.VMEM((pieces, rows, PAIR), F32)] * 2,
        compiler_params=params(
            [((rows, PAIR), BF16)] * (6 + 4 * pieces) + [((pieces, rows, 128), F32)] * 2,
            spare=10 + 4 * (pieces > 2),
        ),
        cost_estimate=cost((24 if causal else 28) * pairs * PAIR / width),
        name="attend_backward",
    )(queries, outputs, grads, totals, key_pos, query_pos, *keys_values, *keys_values, *begun)


def offset(slot, size):
    return pl.multiple_of(slot * size, size)


def row_parts(place, refs):
    if len(refs) == 1:
        return [(0, refs[0][...])]
    own, one, two, near, far = [ref[...] for ref in refs]
    near_first = jnp.concatenate([near, far], axis=0)
    far_first = jnp.concatenate([far, near], axis=0)
    diagonal = jnp.where(place[4] == 0, near_first, far_first)
    return [(place[0], own), (place[1], one), (place[2], two), (place[3], diagonal)]


def times(left_ref, place, refs):
    total = None
    for slot, part in row_parts(place, refs):
        rows = part.shape[0]
        term = dot(left_ref[:, pl.ds(offset(slot, rows), rows)], part)
        total = term if total is None else total + term
    return total


def times_up(left, place, refs, store):
    for slot, part in row_parts(place, refs):
        rows = part.shape[0]
        store(pl.ds(offset(slot, rows), rows), dot_nt(left, part))


def part_specs(arrays, columns, index):
    return [pl.BlockSpec((item.shape[0], columns), lambda *at: (0, index(*at))) for item in arrays]


def fixed(shape):
    zeros = (0,) * len(shape)
    return pl.BlockSpec(shape, lambda *at: zeros)


def view(item, columns, index):
    if item.ndim == 2:
        return (item, pl.BlockSpec((item.shape[0], columns), lambda *at: (0, index)))
    return (item, pl.BlockSpec((1, item.shape[1], columns), lambda *at: (index, 0, 0)))


def run(kernel, name, place, grid, ins, outs, micros, scratch=(), spare=10):
    kept = [bool(out[3:]) for out in outs]
    outs = [out[:3] for out in outs]
    blocks = [(spec.block_shape, item.dtype) for item, spec in ins]
    blocks += [(spec.block_shape, kind) for _, kind, spec in outs]
    held = sum(bytes_of(item.shape, item.dtype) for item in scratch)
    return pl.pallas_call(
        kernel,
        grid_spec=pltpu.PrefetchScalarGridSpec(
            num_scalar_prefetch=1,
            grid=grid,
            in_specs=[spec for _, spec in ins],
            out_specs=[spec for _, _, spec in outs],
            scratch_shapes=list(scratch),
        ),
        out_shape=[
            pltpu.HBM(shape, kind) if keep else jax.ShapeDtypeStruct(shape, kind)
            for keep, (shape, kind, _) in zip(kept, outs)
        ],
        compiler_params=params(blocks, held, spare),
        cost_estimate=cost(micros),
        name=name,
    )(place, *[in_hbm(item) for item, _ in ins])


def project_kernel(place, left_ref, *refs):
    refs[-1][...] = times(left_ref, place, refs[:-1]).astype(BF16)


def project(place, left, weight, first, count, name):
    rows, depth = left[1].block_shape
    chunk = 512
    steps = count * 1024 // chunk
    base = first * 1024 // chunk
    return run(
        project_kernel,
        name,
        place,
        (steps,),
        [left]
        + list(zip(weight, part_specs(weight, chunk, lambda j, s: base + j))),
        [((rows, count * 1024), BF16, pl.BlockSpec((rows, chunk), lambda j, s: (0, j)))],
        2.5 * count,
    )[0]


def mix_kernel(parts, both, place, mixed_ref, resid_ref, norm_ref, *refs):
    out_parts = refs[:parts]
    query_parts = refs[parts : 2 * parts] if both else ()
    outs = refs[2 * parts :] if both else refs[parts:]
    summed_ref, normed_ref, low_ref = outs[:3]
    step = pl.program_id(0)
    rows, width = summed_ref.shape
    half = width // 2

    @pl.when(step < 2)
    def _():
        columns = pl.ds(offset(step, half), half)
        summed_ref[:, columns] = resid_ref[:, columns].astype(F32) + times(
            mixed_ref, place, out_parts
        )

    @pl.when(step == 1)
    def _():
        for strip in strips(rows):
            normed, _ = norm_parts(summed_ref[strip, :])
            value = normed * norm_ref[0:1, :] + norm_ref[1:2, :]
            normed_ref[strip, :] = value
            low_ref[strip, :] = value.astype(BF16)

    if both:

        @pl.when(step >= 2)
        def _():
            outs[3][...] = times(low_ref, place, query_parts).astype(BF16)


def mix(place, mixed, resid, norm, w_out, at_out, w_query, at_query, name):
    rows, width = mixed.shape
    half = width // 2
    both = w_query is not None
    ins = [(mixed, fixed(mixed.shape)), resid, (norm, fixed(norm.shape))]
    ins += zip(
        w_out, part_specs(w_out, half, lambda j, s: at_out * 2 + jnp.minimum(j, 1))
    )
    outs = [
        ((rows, width), F32, fixed((rows, width)), True),
        ((rows, width), F32, fixed((rows, width)), True),
        ((rows, width), BF16, fixed((rows, width)), True),
    ]
    if both:
        ins += zip(
            w_query,
            part_specs(w_query, half, lambda j, s: at_query * 2 + jnp.maximum(j - 2, 0)),
        )
        outs += [
            (
                (rows, width),
                BF16,
                pl.BlockSpec((rows, half), lambda j, s: (0, jnp.maximum(j - 2, 0))),
            )
        ]
    return run(
        functools.partial(mix_kernel, len(w_out), both),
        name,
        place,
        (4 if both else 2,),
        ins,
        outs,
        6.3 if both else 4,
    )


def up_parts(place, refs, packed):
    if not packed:
        return [(0, refs[0][...])]
    unpacked = []
    for slot, part in row_parts(place, refs):
        rows = part.shape[0] // 2
        unpacked.append((slot, jnp.concatenate([part[:rows], part[rows:]], axis=1)))
    return unpacked


def chunk_of(refs, step, counts, use):
    low = 0
    for ref, count in zip(refs, counts):

        @pl.when((step >= low) & (step < low + count))
        def _(ref=ref):
            use(ref)

        low += count


def feed_specs(w_in, w_out, counts, first, chunk, width):
    in_specs = part_specs(w_in, chunk, lambda j, s: s[8 + first + j])
    shift = first if len(w_in) == 1 else 0
    out_specs, start = [], 0
    for count in counts:
        out_specs.append(
            pl.BlockSpec(
                (chunk, width),
                lambda j, s, start=start, count=count: (
                    shift + jnp.clip(j - start, 0, count - 1),
                    0,
                ),
            )
        )
        start += count
    return in_specs, out_specs


def feed_first_kernel(
    sizes, counts, packed, place, low_ref, second_ref, *refs
):
    n_in, n_out, n_down, n_up = sizes
    in_refs, refs = refs[:n_in], refs[n_in:]
    out_refs, refs = refs[:n_out], refs[n_out:]
    down_refs, refs = refs[:n_down], refs[n_down:]
    up_refs, refs = refs[:n_up], refs[n_up:]
    total_ref, slope_ref, hidden_ref, aslope_ref = refs
    step = pl.program_id(0)

    @pl.when(step == 0)
    def _():
        hidden, slope = gelu_pair(times(low_ref, place, down_refs))
        hidden_ref[...] = hidden.astype(BF16)
        aslope_ref[...] = slope.astype(BF16)
        total = None
        for slot, part in up_parts(place, up_refs, packed):
            count = part.shape[0]
            term = dot(hidden_ref[:, pl.ds(offset(slot, count), count)], part)
            total = term if total is None else total + term
        total_ref[...] = second_ref[...] + 4.0 * total

    feed_chunk(place, low_ref, in_refs, out_refs, counts, total_ref, slope_ref)


def feed_chunk(place, low_ref, in_refs, out_refs, counts, total_ref, slope_ref):
    hidden, slope = gelu_pair(times(low_ref, place, in_refs))
    slope_ref[...] = slope.astype(BF16)
    hidden = hidden.astype(BF16)

    def use(ref):
        total_ref[...] += dot(hidden, ref[...])

    chunk_of(out_refs, pl.program_id(0), counts, use)


def feed_second_kernel(
    sizes, counts, steps, place, low_ref, first_ref, grad_ref, norm_ref, *refs
):
    n_in, n_out = sizes
    in_refs, refs = refs[:n_in], refs[n_in:]
    out_refs, refs = refs[:n_out], refs[n_out:]
    final_ref, d_ref, dlow_ref, dnorm_ref, slope_ref, total_ref = refs
    step = pl.program_id(0)
    rows, width = total_ref.shape

    @pl.when(step == 0)
    def _():
        total_ref[...] = first_ref[...]

    feed_chunk(place, low_ref, in_refs, out_refs, counts, total_ref, slope_ref)

    @pl.when(step == steps - 1)
    def _():
        gain, shift = norm_ref[0:1, :], norm_ref[1:2, :]
        dgain = jnp.zeros((1, width), F32)
        dshift = jnp.zeros((1, width), F32)
        for strip in strips(rows):
            normed, rstd = norm_parts(total_ref[strip, :])
            final_ref[strip, :] = (normed * gain + shift).astype(BF16)
            grad = grad_ref[strip, :].astype(F32)
            dgain += jnp.sum(grad * normed, axis=0, keepdims=True)
            dshift += jnp.sum(grad, axis=0, keepdims=True)
            back = norm_backward(normed, rstd, gain, grad)
            d_ref[strip, :] = back
            dlow_ref[strip, :] = back.astype(BF16)
        dnorm_ref[0:1, :] = dgain
        dnorm_ref[1:2, :] = dshift


CHUNK = 512


def feed_first(place, low, second, w_in, w_out, counts, w_down, at_down, w_up, at_up):
    rows, width = low.shape
    adapter = 512
    packed = len(w_up) > 1
    steps = sum(counts)
    in_specs, out_specs = feed_specs(w_in, w_out, counts, 0, CHUNK, width)
    up_columns = 512 if packed else width
    full = fixed((rows, width))
    ins = [(low, full), (second, full)]
    ins += zip(w_in, in_specs)
    ins += zip(w_out, out_specs)
    ins += zip(w_down, part_specs(w_down, adapter, lambda j, s: at_down))
    ins += zip(w_up, part_specs(w_up, up_columns, lambda j, s: at_up))
    return run(
        functools.partial(
            feed_first_kernel, (len(w_in), len(w_out), len(w_down), len(w_up)), counts, packed
        ),
        "feed_first",
        place,
        (steps,),
        ins,
        [
            ((rows, width), F32, full),
            ((rows, steps * CHUNK), BF16, pl.BlockSpec((rows, CHUNK), lambda j, s: (0, j)), True),
            ((rows, adapter), BF16, fixed((rows, adapter)), True),
            ((rows, adapter), BF16, fixed((rows, adapter)), True),
        ],
        13,
    )


def feed_second(place, low, first, grad, norm, w_in, w_out, counts, start):
    rows, width = low.shape
    steps = sum(counts)
    in_specs, out_specs = feed_specs(w_in, w_out, counts, start, CHUNK, width)
    full = fixed((rows, width))
    ins = [(low, full), (first, full), (grad, full), (norm, fixed(norm.shape))]
    ins += zip(w_in, in_specs)
    ins += zip(w_out, out_specs)
    return run(
        functools.partial(feed_second_kernel, (len(w_in), len(w_out)), counts, steps),
        "feed_second",
        place,
        (steps,),
        ins,
        [
            ((rows, width), BF16, full, True),
            ((rows, width), F32, full),
            ((rows, width), BF16, full),
            ((2, width), F32, fixed((2, width)), True),
            ((rows, steps * CHUNK), BF16, pl.BlockSpec((rows, CHUNK), lambda j, s: (0, j)), True),
        ],
        13.5,
        scratch=[pltpu.VMEM((rows, width), F32)],
    )


def feed_backward_kernel(
    sizes,
    counts,
    packed,
    steps,
    place,
    dlow_ref,
    d_ref,
    resid_ref,
    norm_ref,
    slope_ref,
    later_ref,
    aslope_ref,
    *refs,
):
    n_in, n_out, n_down, n_up, n_mix = sizes
    in_refs, refs = refs[:n_in], refs[n_in:]
    out_refs, refs = refs[:n_out], refs[n_out:]
    down_refs, refs = refs[:n_down], refs[n_down:]
    up_refs, refs = refs[:n_up], refs[n_up:]
    mix_refs, refs = refs[:n_mix], refs[n_mix:]
    dtwo_ref, dtwo_low_ref, dnorm_ref, dadapter_ref, dmixed_ref, total_ref, dhidden_ref = refs
    step = pl.program_id(0)
    rows, width = total_ref.shape

    def add(columns, value):
        total_ref[:, columns] += value

    @pl.when(step == 0)
    def _():
        total_ref[...] = d_ref[...]
        for slot, part in up_parts(place, up_refs, packed):
            count = part.shape[0]
            columns = pl.ds(offset(slot, count), count)
            back = 4.0 * dot_nt(dlow_ref[...], part)
            dadapter_ref[:, columns] = (aslope_ref[:, columns].astype(F32) * back).astype(BF16)
        times_up(dadapter_ref[...], place, down_refs, add)

    def use(ref):
        back = dot_nt(dlow_ref[...], ref[...])
        chosen = jnp.where(step < steps // 2, slope_ref[...], later_ref[...])
        dhidden_ref[...] = (chosen.astype(F32) * back).astype(BF16)

    chunk_of(out_refs, step, counts, use)
    times_up(dhidden_ref[...], place, in_refs, add)

    @pl.when(step == steps - 1)
    def _():
        finish_norm(total_ref, resid_ref, norm_ref, dtwo_ref, dtwo_low_ref, dnorm_ref)

        def keep(columns, value):
            dmixed_ref[:, columns] = value.astype(BF16)

        times_up(dtwo_low_ref[...], place, mix_refs, keep)


def finish_norm(grad_ref, resid_ref, norm_ref, d_ref, dlow_ref, dnorm_ref):
    rows, width = grad_ref.shape
    gain = norm_ref[0:1, :]
    dgain = jnp.zeros((1, width), F32)
    dshift = jnp.zeros((1, width), F32)
    for strip in strips(rows):
        grad = grad_ref[strip, :]
        normed, rstd = norm_parts(resid_ref[strip, :])
        dgain += jnp.sum(grad * normed, axis=0, keepdims=True)
        dshift += jnp.sum(grad, axis=0, keepdims=True)
        back = norm_backward(normed, rstd, gain, grad)
        d_ref[strip, :] = back
        dlow_ref[strip, :] = back.astype(BF16)
    dnorm_ref[0:1, :] = dgain
    dnorm_ref[1:2, :] = dshift


def feed_backward(
    place,
    dlow,
    d_three,
    resid,
    norm,
    slope,
    later,
    aslope,
    w_in,
    w_out,
    counts,
    w_down,
    at_down,
    w_up,
    at_up,
    w_mix,
    at_mix,
):
    rows, width = dlow.shape
    hidden = w_in[0].shape[1]
    adapter = 512
    packed = len(w_up) > 1
    chunk = CHUNK
    steps = hidden // chunk
    in_specs, out_specs = feed_specs(w_in, w_out, counts, 0, chunk, width)
    middle = steps // 2
    up_columns = 512 if packed else width
    full = fixed((rows, width))
    ins = [
        (dlow, full),
        (d_three, full),
        (resid, full),
        (norm, fixed(norm.shape)),
        (slope, pl.BlockSpec((rows, chunk), lambda j, s: (0, jnp.minimum(j, middle - 1)))),
        (later, pl.BlockSpec((rows, chunk), lambda j, s: (0, jnp.maximum(j - middle, 0)))),
        (aslope, fixed((rows, adapter))),
    ]
    ins += zip(w_in, in_specs)
    ins += zip(w_out, out_specs)
    ins += zip(w_down, part_specs(w_down, adapter, lambda j, s: at_down))
    ins += zip(w_up, part_specs(w_up, up_columns, lambda j, s: at_up))
    ins += zip(w_mix, part_specs(w_mix, width, lambda j, s: at_mix))
    return run(
        functools.partial(
            feed_backward_kernel,
            (len(w_in), len(w_out), len(w_down), len(w_up), len(w_mix)),
            counts,
            packed,
            steps,
        ),
        "feed_backward",
        place,
        (steps,),
        ins,
        [
            ((rows, width), F32, full, True),
            ((rows, width), BF16, full),
            ((2, width), F32, fixed((2, width)), True),
            ((rows, adapter), BF16, fixed((rows, adapter))),
            ((rows, width), BF16, full),
        ],
        29,
        scratch=[pltpu.VMEM((rows, width), F32), pltpu.VMEM((rows, chunk), BF16)],
    )


def norm_step_kernel(parts, place, dquery_ref, d_ref, resid_ref, norm_ref, *refs):
    query_refs, refs = refs[:parts], refs[parts:]
    out_refs, refs = refs[:parts], refs[parts:]
    done_ref, done_low_ref, dnorm_ref, dmixed_ref, total_ref = refs
    step = pl.program_id(0)

    @pl.when(step == 0)
    def _():
        def add(columns, value):
            total_ref[:, columns] = d_ref[:, columns] + value

        times_up(dquery_ref[...], place, query_refs, add)
        finish_norm(total_ref, resid_ref, norm_ref, done_ref, done_low_ref, dnorm_ref)

    @pl.when(step == 1)
    def _():
        def keep(columns, value):
            dmixed_ref[:, columns] = value.astype(BF16)

        times_up(done_low_ref[...], place, out_refs, keep)


def norm_step(place, dquery, d_two, resid, norm, w_query, at_query, w_out, at_out):
    rows, width = dquery.shape
    full = fixed((rows, width))
    ins = [(dquery, full), (d_two, full), (resid, full), (norm, fixed(norm.shape))]
    ins += zip(w_query, part_specs(w_query, width, lambda j, s: at_query))
    ins += zip(w_out, part_specs(w_out, width, lambda j, s: at_out))
    return run(
        functools.partial(norm_step_kernel, len(w_query)),
        "norm_step",
        place,
        (2,),
        ins,
        [
            ((rows, width), F32, full, True),
            ((rows, width), BF16, full),
            ((2, width), F32, fixed((2, width)), True),
            ((rows, width), BF16, full),
        ],
        6.6,
        scratch=[pltpu.VMEM((rows, width), F32)],
    )


def inputs_back_kernel(lefts, parts, extra, place, *refs):
    left_refs, refs = refs[:lefts], refs[lefts:]
    part_refs, refs = refs[:parts], refs[parts:]
    if extra:
        extra_ref, refs = refs[0], refs[1:]
    out_ref, total_ref = refs
    step = pl.program_id(0)
    width = total_ref.shape[1]

    @pl.when(step == 0)
    def _():
        if extra == "base":
            total_ref[...] = extra_ref[...]
        else:
            total_ref[...] = jnp.zeros_like(total_ref)
        if extra == "beside":
            out_ref[:, :width] = extra_ref[...]

    def add(columns, value):
        total_ref[:, columns] += value

    for which in range(lefts):

        @pl.when(step == which)
        def _(which=which):
            left = left_refs[which][...]
            times_up(left.reshape(left.shape[-2:]), place, part_refs, add)

    @pl.when(step == lefts - 1)
    def _():
        out_ref[:, out_ref.shape[1] - width :] = total_ref[...].astype(BF16)


def inputs_back(place, lefts, weight, blocks, extra, item, name):
    depth = lefts[0][1].block_shape[-1]
    rows = lefts[0][1].block_shape[-2]
    width = 1024
    first = blocks[0]
    strides = {blocks[k + 1] - blocks[k] for k in range(len(blocks) - 1)}

    def at(j, s):
        index = first
        for k in range(1, len(blocks)):
            index = jnp.where(j == k, blocks[k], index)
        return first + j if strides == {1} else index

    ins = list(lefts)
    ins += zip(weight, part_specs(weight, depth, at))
    if extra:
        ins += [(item, fixed((rows, width)))]
    size = 2 * width if extra == "beside" else width
    return run(
        functools.partial(inputs_back_kernel, len(lefts), len(weight), extra),
        name,
        place,
        (len(lefts),),
        ins,
        [((rows, size), BF16, fixed((rows, size)))],
        3 * len(lefts) * depth / width,
        scratch=[pltpu.VMEM((rows, width), F32)],
    )[0]


def laid_out_kernel(slots, item_ref, *refs):
    out_ref = refs[-1]
    out_ref[slots[0]] = item_ref[0]
    for index, ref in enumerate(refs[:-1], 1):
        out_ref[slots[index]] = ref[...]


def laid_out(slots, item, parts):
    part = parts[0].shape
    return run(
        laid_out_kernel,
        "laid_out",
        slots,
        (1,),
        [(item, pl.BlockSpec((1,) + part, lambda j, s: (s[0], 0, 0)))]
        + [(piece, fixed(part)) for piece in parts],
        [(item.shape, item.dtype, fixed(item.shape))],
        1.5,
    )[0]


def swap_pairs(size, bit):
    return [(index, index ^ bit) for index in range(size)]


def by_core(even, odd):
    return [
        (d * 8 + s, (d ^ (odd if s % 2 else even)) * 8 + s) for d in range(4) for s in range(8)
    ]


def after(item, *others):
    return lax.optimization_barrier((item,) + others)[0]


def gather_first(own):
    return (own, lax.ppermute(own, ("dp", "seq"), by_core(1, 2)))


def gather_swap(parts, *others):
    return parts + (lax.ppermute(after(parts[1], *others), "seq", swap_pairs(8, 1)),)


def gather_near(parts, core, *others):
    one = parts[1]
    half = one.shape[0] // 2
    half_one = lax.dynamic_slice_in_dim(after(one, *others), core * half, half, 0)
    return parts + (lax.ppermute(half_one, ("dp", "seq"), by_core(2, 1)),)


def gather_far(parts, *others):
    return parts + (lax.ppermute(after(parts[3], *others), "seq", swap_pairs(8, 1)),)


def gather_dp(item):
    return (lax.all_gather(item, "dp", axis=0, tiled=True),)


def row_blocks(value, size):
    return [value[start : start + size] for start in range(0, value.shape[0], size)]


def wgrad_kernel(fresh, split, scales, extra, place, *refs):
    count = len(fresh)
    left_refs, right_refs = refs[:count], refs[count : 2 * count]
    outs, up_ref = refs[2 * count + extra : -1], refs[-1]
    step = pl.program_id(0)
    wide = outs[0].shape[1]
    if extra:

        @pl.when(step == count)
        def _():
            rows = jnp.concatenate([ref[...] for ref in refs[2 * count : 2 * count + extra]])
            filler = jnp.zeros((128 - rows.shape[0], rows.shape[1]), F32)
            columns = jnp.concatenate([rows, filler], axis=0).T.astype(BF16)
            blocks = row_blocks(columns, 32)
            even = jnp.concatenate(blocks[0::2], axis=0)
            odd = jnp.concatenate(blocks[1::2], axis=0)
            outs[0][:, :128] = jnp.where(place[4] == 0, odd, even)
            outs[1][:, :128] = jnp.where(place[4] == 0, even, odd)
            for out in outs:
                out[:, 128:256] = jnp.zeros(even.shape, BF16)

    for which in range(count):

        @pl.when(step == which)
        def _(which=which):
            right = right_refs[which][...]
            right = right.reshape(right.shape[-2:])
            tall = left_refs[which].shape[-1]
            if fresh[which]:
                left = left_refs[which][...]
                up_ref[:tall, :] = left.reshape(left.shape[-2:]).T
            value = dot(up_ref[:tall, :], right)
            value = (value * scales[which] if scales[which] != 1.0 else value).astype(BF16)
            own = tall // 32
            blocks = row_blocks(value, own)
            if split:
                even = jnp.concatenate(blocks[0::2], axis=0)
                odd = jnp.concatenate(blocks[1::2], axis=0)
                outs[0][...] = jnp.where(place[4] == 0, odd, even)
                outs[1][...] = jnp.where(place[4] == 0, even, odd)
                return
            folds = right.shape[1] // wide
            for index, item in enumerate(blocks):
                at = (index % 8 * 4 + index // 8) * own * folds
                for fold in range(folds):
                    low = at + fold * own
                    outs[0][low : low + own, :] = item[:, fold * wide : (fold + 1) * wide]


def wgrad(place, lefts, rights, wide, split, scales, name, extra=()):
    fresh = []
    for index, (item, spec) in enumerate(lefts):
        before = lefts[index - 1] if index else (None, None)
        fresh.append(item is not before[0] or spec is not before[1])
    rows, tall = lefts[0][1].block_shape[-2:]
    high = tall // 2 if split else tall
    spec = pl.BlockSpec((high, wide), lambda j, s: (0, j))
    more = 1 if extra else 0
    return run(
        functools.partial(wgrad_kernel, tuple(fresh), split, scales, len(extra)),
        name,
        place,
        (len(lefts) + more,),
        list(lefts) + list(rights) + [(item, fixed(item.shape)) for item in extra],
        [((high, wide * len(lefts) + 256 * more), BF16, spec, True)] * (2 if split else 1),
        1.6 * len(lefts) * wide / 1024,
        scratch=[pltpu.VMEM((tall, rows), BF16)],
    )


def take(item, index, axis):
    return lax.dynamic_index_in_dim(item, index, axis, keepdims=False)


def add(kept, received, kind=BF16):
    return (kept.astype(F32) + received.astype(F32)).astype(kind)


def sum_over(partial, name):
    return lax.psum_scatter(partial, name, scatter_dimension=0, tiled=True)


class Scatter:
    def __init__(self, send, keep):
        here, there = lax.axis_index("dp"), lax.axis_index("seq")
        self.x, self.y = here % 2, here // 2
        self.low, self.high = (there // 2) % 2, there // 4
        self.send, self.keep = send, keep
        self.width = keep.shape[1]

    def core(self):
        received = lax.ppermute(self.send, "seq", swap_pairs(8, 1))
        item = add(self.keep, received).reshape(2, 2, 128, self.width)
        self.one, self.two = item[..., : self.width // 2], item[..., self.width // 2 :]
        return self.one

    def plane_one(self):
        x, y = self.x, self.y
        from_x = lax.ppermute(take(self.one, 1 - x, 1), "dp", swap_pairs(4, 1))
        from_y = lax.ppermute(take(self.two, 1 - y, 0), "dp", swap_pairs(4, 2))
        self.one = add(take(self.one, x, 1), from_x)
        self.two = add(take(self.two, y, 0), from_y)
        return self.one, self.two

    def plane_two(self):
        x, y = self.x, self.y
        from_y = lax.ppermute(take(self.one, 1 - y, 0), "dp", swap_pairs(4, 2))
        from_x = lax.ppermute(take(self.two, 1 - x, 0), "dp", swap_pairs(4, 1))
        one = add(take(self.one, y, 0), from_y)
        two = add(take(self.two, x, 0), from_x)
        self.item = jnp.concatenate([one, two], axis=1)
        return self.item

    def z_one(self):
        self.item = self.item.reshape(2, 2, 32, self.width)
        received = lax.ppermute(take(self.item, 1 - self.low, 1), "seq", swap_pairs(8, 2))
        self.item = add(take(self.item, self.low, 1), received)
        return self.item

    def z_two(self):
        received = lax.ppermute(take(self.item, 1 - self.high, 0), "seq", swap_pairs(8, 4))
        self.item = add(take(self.item, self.high, 0), received, F32)
        return self.item


def sum_all(partial):
    return lax.psum_scatter(
        partial.astype(BF16), ("dp", "seq"), scatter_dimension=0, tiled=True
    ).astype(F32)


def body(
    target,
    source,
    target_len,
    source_len,
    self_query,
    self_key,
    self_value,
    self_output,
    cross_query,
    cross_key,
    cross_value,
    cross_output,
    feed_in,
    feed_out,
    adapter_down,
    adapter_up,
    self_gain,
    self_shift,
    cross_gain,
    cross_shift,
    final_gain,
    final_shift,
    cotangent,
):
    block, seqs, width = target.shape
    dp, seq = lax.axis_size("dp"), lax.axis_size("seq")
    group = seq // seqs
    rows = seqs * block
    here, there = lax.axis_index("dp"), lax.axis_index("seq")
    inner, which = there % group, there // group
    core = there % 2
    halving = dp == 4 and seq == 8
    apart = [[start + group * step for step in range(seqs)] for start in range(group)]

    def to_sequence(item):
        return lax.all_to_all(
            item.swapaxes(0, 1), "seq", 0, 0, axis_index_groups=apart, tiled=True
        ).reshape(rows, item.shape[-1])

    slots = jnp.stack([which ^ bit for bit in range(seqs)]).astype(jnp.int32)

    def send_back(item):
        item = item.reshape(seqs, block, item.shape[-1])
        parts = [item]
        for bit in range(1, seqs):
            pairs = [(index, (index // group ^ bit) * group + index % group) for index in range(seq)]
            parts.append(lax.ppermute(take(item, which ^ bit, 0), "seq", pairs))
        return parts

    def set_down(parts, *others):
        item, *parts = lax.optimization_barrier((*parts, *others))[: len(parts)]
        return laid_out(slots, item, parts).swapaxes(0, 1)

    def near(shift):
        return [
            (k * group + c, k * group + (c + shift) % group)
            for k in range(seqs)
            for c in range(group)
        ]

    def spread(item):
        return [item] + [lax.ppermute(item, "seq", near(-s)) for s in range(1, group)]

    def collect(own, others):
        for shift, other in enumerate(others, 1):
            own = own + lax.ppermute(other, "seq", near(shift)).astype(F32)
        return own.astype(BF16)

    own_inputs, own_memory = to_sequence(target), to_sequence(source)
    inputs, memory = view(own_inputs, width, 0), view(own_memory, width, 0)
    grad_out = to_sequence(cotangent)
    vectors = jnp.stack([self_gain, self_shift, cross_gain, cross_shift, final_gain, final_shift])
    if halving:
        one = jnp.where(core == 0, here ^ 1, here ^ 2)
        two = jnp.where(core == 0, here ^ 2, here ^ 1)
        diagonal = here ^ 3
        chunks = [item * 2 + part for item in (here, one, two) for part in (0, 1)]
        chunks += [diagonal * 2 + core, diagonal * 2 + 1 - core]
        place = jnp.stack([here, one, two, diagonal, core, core, core, core] + chunks)
        first_group = jnp.concatenate(
            [self_query, self_key, self_value, cross_key, cross_value], axis=1
        )
        half = width // 2
        up_packed = jnp.concatenate([adapter_up[:, :half], adapter_up[:, half:]], axis=0)
        second_group = jnp.concatenate(
            [self_output, cross_query, cross_output, adapter_down, up_packed], axis=1
        )
        vector_parts = [vectors] + [
            lax.ppermute(vectors, "dp", swap_pairs(4, bit)) for bit in (1, 2, 3)
        ]
        w_self = gather_swap(gather_first(first_group))
        w_self = gather_far(
            gather_near(w_self, core, own_inputs, second_group, *vector_parts)
        )
        w_mid = gather_swap(gather_first(after(second_group, w_self[3])))
        w_in = gather_first(after(feed_in, w_mid[1]))
        at_q, at_kv, at_ckv = (w_self, 0), (w_self, 1), (w_self, 3)
        parts = jnp.stack(vector_parts)
        vectors = jnp.concatenate([take(parts, here ^ slot, 0) for slot in range(4)], axis=1)
        counts_first, counts_second = (2, 2), (2, 1, 1)
    else:
        steps = feed_in.shape[1] // CHUNK
        place = jnp.stack([jnp.int32(0)] * 8 + [jnp.int32(j) for j in range(steps)])
        at_q = (gather_dp(self_query), 0)
        at_kv = (gather_dp(jnp.concatenate([self_key, self_value], axis=1)), 0)
        at_o, at_cq = (gather_dp(self_output), 0), (gather_dp(cross_query), 0)
        at_ckv = (gather_dp(jnp.concatenate([cross_key, cross_value], axis=1)), 0)
        at_co = (gather_dp(cross_output), 0)
        w_in, w_out = gather_dp(feed_in), gather_dp(feed_out)
        at_down, at_up = (gather_dp(adapter_down), 0), (gather_dp(adapter_up), 0)
        vectors = lax.all_gather(vectors, "dp", axis=1, tiled=True)
        out_first = out_second = w_out
        counts_first, counts_second = (steps // 2,), (steps - steps // 2,)
    place = place.astype(jnp.int32)
    vectors = vectors.astype(F32)
    norm_one, norm_two, norm_three = vectors[0:2], vectors[2:4], vectors[4:6]

    local = jnp.arange(rows, dtype=jnp.int32)

    def positions(place_in_group):
        return (local // block * group + place_in_group) * block + local % block

    target_limit = take(target_len, which, 0)
    source_limit = take(source_len, which, 0)
    key_pos = jnp.stack([positions((inner + shift) % group) for shift in range(group)])
    self_keys = jnp.where(key_pos < target_limit, key_pos, NEVER)[..., None]
    cross_keys = jnp.where(key_pos < source_limit, key_pos, NEVER)[..., None]
    self_rows = positions(inner)[None]
    cross_rows = jnp.full((1, rows), ALWAYS, jnp.int32)

    kv_own = project(place, inputs, *at_kv, 2, "self_kv")
    kv_all = spread(kv_own)
    queries = project(place, inputs, *at_q, 1, "self_q")
    if halving:
        w_mid = gather_near(w_mid, core, queries)
        queries = after(queries, w_mid[1])
    mixed, totals = attend_forward(queries, kv_all, self_keys, self_rows, block, True)
    ckv_own = project(
        place, (after(own_memory, mixed), memory[1]), *at_ckv, 2, "cross_kv"
    )
    ckv_all = spread(ckv_own)
    mixed = after(mixed, ckv_own)
    if halving:
        w_mid = gather_far(w_mid, mixed)
        w_out = gather_first(after(feed_out, mixed))
        at_o, at_cq, at_co = (w_mid, 0), (w_mid, 1), (w_mid, 2)
        at_down, at_up = (w_mid, 6), (w_mid, 7)
    resid_one, first, first_low, cross_q = mix(
        place, mixed, inputs, norm_one, *at_o, *at_cq, "mix_self"
    )
    if halving:
        w_in = gather_near(gather_swap(w_in, cross_q), core, cross_q)
        cross_q = after(cross_q, w_in[1])
    cross_mixed, cross_totals = attend_forward(
        cross_q, ckv_all, cross_keys, cross_rows, block, False
    )
    if halving:
        w_in = gather_far(w_in, cross_mixed)
        w_out = gather_far(gather_near(gather_swap(w_out, cross_mixed), core, cross_mixed))
        out_first, out_second = w_out[:2], w_out[2:]
    cross_mixed = after(cross_mixed, grad_out)
    resid_two, second, second_low = mix(
        place, cross_mixed, view(first, width, 0), norm_two, *at_co, None, None, "mix_cross"
    )
    partial, slope, hidden, adapter_slope = feed_first(
        place, second_low, second, w_in, out_first, counts_first, *at_down, *at_up
    )
    final, d_three, d_branch, d_norm_three, later = feed_second(
        place,
        second_low,
        partial,
        grad_out,
        norm_three,
        w_in,
        out_second,
        counts_second,
        sum(counts_first),
    )
    output = send_back(final)

    d_two, d_two_low, d_norm_two, d_adapter, d_cross = feed_backward(
        place,
        d_branch,
        d_three,
        resid_two,
        norm_two,
        slope,
        later,
        adapter_slope,
        w_in,
        w_out,
        counts_first + counts_second if halving else (steps,),
        *at_down,
        *at_up,
        *at_co,
    )

    d_two_low = after(d_two_low, *output[1:])

    def whole(item, layer=0):
        return view(item, item.shape[-1], layer)

    pairs = width // PAIR
    if halving:
        half = width // 2
        left = whole(cross_mixed)
        early = wgrad(
            place,
            [left, left, whole(second_low), whole(hidden)],
            [view(d_two_low, half, 0), view(d_two_low, half, 1), whole(d_adapter), whole(d_branch)],
            half,
            False,
            (1.0, 1.0, 1.0, 4.0),
            "wgrad_early",
        )[0]
        d_cross = after(d_cross, early)
        early = sum_over(early, "seq")
    d_cq, *d_ckv = attend_backward(
        cross_q,
        ckv_all,
        cross_mixed,
        d_cross,
        cross_totals,
        cross_keys,
        cross_rows,
        block,
        False,
        (0, pairs),
    )
    output = set_down(output, d_cq)
    d_one, d_one_low, d_norm_one, d_mixed = norm_step(
        place, d_cq, d_two, resid_one, norm_one, *at_cq, *at_o
    )
    d_ckv = collect(after(d_ckv[0], d_one_low), d_ckv[1:])
    grad_source = inputs_back(
        place,
        [whole(d_ckv, 0), whole(d_ckv, 1)],
        at_ckv[0],
        [at_ckv[1], at_ckv[1] + 1],
        None,
        None,
        "source_back",
    )
    d_ckv = after(d_ckv, grad_source)
    grad_source = send_back(grad_source)
    if halving:
        d_one_low = after(d_one_low, early)
        early = sum_over(early, "dp").astype(F32)
        inner_sums = Scatter(
            *wgrad(
                place,
                [memory, memory, whole(mixed), whole(first_low)],
                [whole(d_ckv, 0), whole(d_ckv, 1), whole(d_one_low), whole(d_cq)],
                width,
                True,
                (1.0,) * 4,
                "wgrad_inner",
                [d_norm_one, d_norm_two, d_norm_three],
            )
        )
    if halving:
        d_mixed = after(d_mixed, inner_sums.core())
    else:
        d_mixed = after(d_mixed, grad_source[0])

    begun = ()
    split = pairs * 7 // 8
    for span in ((0, split), (split, pairs - split)):
        begun = attend_backward(
            queries,
            kv_all,
            mixed,
            d_mixed,
            totals,
            self_keys,
            self_rows,
            block,
            True,
            span,
            begun,
        )
        if halving and span[0] == 0:
            d_mixed = after(d_mixed, begun[0], inner_sums.plane_one(), *grad_source[1:3])
    d_q, *d_kv = begun
    d_kv = collect(d_kv[0], d_kv[1:])
    at_self = at_q if halving else ((jnp.concatenate([at_q[0][0], at_kv[0][0]], axis=1),), 0)
    grad_target = inputs_back(
        place,
        [whole(d_q), whole(d_kv, 0), whole(d_kv, 1)],
        at_self[0],
        [at_self[1] + index for index in range(3)],
        "base",
        d_one,
        "target_back",
    )
    d_q = after(d_q, grad_target)
    grad_target = send_back(grad_target)
    if not halving:
        grad_source = set_down(grad_source)
        grad_target = set_down(grad_target)
    if halving:
        inner_sums.one, inner_sums.two, _ = lax.optimization_barrier(
            (inner_sums.one, inner_sums.two, grad_target[0])
        )
        late = Scatter(
            *wgrad(
                place,
                [inputs] * 3,
                [whole(d_q), whole(d_kv, 0), whole(d_kv, 1)],
                width,
                True,
                (1.0,) * 3,
                "wgrad_self",
            )
        )
        grad_source = set_down(grad_source, late.send)
        late.keep = after(late.keep, inner_sums.plane_two(), grad_source, grad_target[1])
        late.core()
        late.plane_one()
        late.one, late.two, *_ = lax.optimization_barrier(
            (late.one, late.two, inner_sums.z_one(), *grad_target)
        )
        grad_target = set_down(grad_target, late.one)
        late.plane_two()
        late.item = after(late.item, grad_target, inner_sums.z_two())
        late.z_one()
        late.z_two()
        grad_co, grad_down = early[:, :width], early[:, width : width + half]
        lifted = early[:, width + half :]
        folded = lifted.shape[0] // 2
        grad_up = jnp.concatenate([lifted[:folded], lifted[folded:]], axis=1)
        norm_sums = inner_sums.item[:, 4 * width : 4 * width + 6].T
        grad_ck, grad_cv, grad_o, grad_cq = [
            inner_sums.item[:, index * width : (index + 1) * width] for index in range(4)
        ]
        grad_q, grad_k, grad_v = [
            late.item[:, index * width : (index + 1) * width] for index in range(3)
        ]
    else:
        norm_sums = jnp.concatenate([d_norm_one, d_norm_two, d_norm_three], axis=0)
        norm_sums = lax.psum_scatter(norm_sums, ("dp", "seq"), scatter_dimension=1, tiled=True)
        grad_down = sum_all(dot_tn(second_low, d_adapter))
        grad_up = sum_all(4.0 * dot_tn(hidden, d_branch))
        grad_co = sum_all(dot_tn(cross_mixed, d_two_low))
        grad_o = sum_all(dot_tn(mixed, d_one_low))
        grad_cq = sum_all(dot_tn(first_low, d_cq))
        grad_ck = sum_all(dot_tn(own_memory, d_ckv[0]))
        grad_cv = sum_all(dot_tn(own_memory, d_ckv[1]))
        grad_q = sum_all(dot_tn(own_inputs, d_q))
        grad_k = sum_all(dot_tn(own_inputs, d_kv[0]))
        grad_v = sum_all(dot_tn(own_inputs, d_kv[1]))
    return (
        output,
        grad_target,
        grad_source,
        grad_q,
        grad_k,
        grad_v,
        grad_o,
        grad_cq,
        grad_ck,
        grad_cv,
        grad_co,
        grad_down,
        grad_up,
        *[norm_sums[index] for index in range(6)],
    )


def solution(mesh):
    tokens = P("seq", "dp", None)
    rows = P("dp", None)
    vector = P("dp")
    both = P(("dp", "seq"), None)
    return jax.shard_map(
        body,
        mesh=mesh,
        in_specs=(tokens, tokens, vector, vector) + (rows,) * 12 + (vector,) * 6 + (tokens,),
        out_specs=(tokens,) * 3 + (both,) * 10 + (P(("dp", "seq")),) * 6,
        check_vma=False,
    )
```
